32 devices in a mesh: section: 2 (over core), row: 4 (over z), col: 4 (over y, x).
Axes of the slice: x: 2, y: 2, z: 4, core: 2. Of those that a mesh axis runs over, the one named last changes fastest.
Arguments:
- tokens: bfloat16 [4, 1024, 1536], P(None, 'row'), may hold values from -6 to 6
- cotangent: bfloat16 [4, 1024, 1536], P(None, 'row'), may hold values from -6 to 6
- lengths: int32 [4, 3], replicated, may hold values from 1 to 1022, as said below
- norm_attn: bfloat16 [2, 1536], P('section'), may hold values from 0.5 to 1.5
- w_query: bfloat16 [2, 1536, 1536], P('section', 'row', 'col'), may hold values from -0.15625 to 0.15625
- b_query: bfloat16 [2, 1536], P('section', 'col'), may hold values from -3 to 3
- w_keyval: bfloat16 [2, 1536, 512], P('section', ('row', 'col')), may hold values from -0.15625 to 0.15625
- b_keyval: bfloat16 [2, 512], P('section'), may hold values from -3 to 3
- w_out: bfloat16 [2, 1536, 1536], P('section', 'col', 'row'), may hold values from -0.5 to 0.5
- norm_ffn: bfloat16 [2, 1536], P('section'), may hold values from 0.5 to 1.5
- w_gate: bfloat16 [2, 1536, 8960], P('section', 'row', 'col'), may hold values from -0.15625 to 0.15625
- w_up: bfloat16 [2, 1536, 8960], P('section', 'row', 'col'), may hold values from -0.15625 to 0.15625
- w_down: bfloat16 [2, 8960, 1536], P('section', 'col', 'row'), may hold values from -0.0625 to 0.0625
Outputs:
- activations: bfloat16 [2, 4, 1024, 1536], P('section', None, 'row')
- input_grads: bfloat16 [2, 4, 1024, 1536], P('section', None, 'row')
- grad_norm_attn: float32 [2, 1536], P('section')
- grad_w_query: float32 [2, 1536, 1536], P('section', 'row', 'col')
- grad_b_query: float32 [2, 1536], P('section', 'col')
- grad_w_keyval: float32 [2, 1536, 512], P('section', ('row', 'col'))
- grad_b_keyval: float32 [2, 512], P('section')
- grad_w_out: float32 [2, 1536, 1536], P('section', 'col', 'row')
- grad_norm_ffn: float32 [2, 1536], P('section')
- grad_w_gate: float32 [2, 1536, 8960], P('section', 'row', 'col')
- grad_w_up: float32 [2, 1536, 8960], P('section', 'row', 'col')
- grad_w_down: float32 [2, 8960, 1536], P('section', 'col', 'row')
The draws below stay inside these ranges and needn't reach their ends.
Inputs may be any that keep to these rules, and one draw needn't show every extreme that they name: `lengths`: each micro-batch holds three sequences: the first and the last have fewer than 256 tokens each, the middle one the rest of the 1024; in one micro-batch the first and the last have one token each.
All inputs are finite; a program needn't handle non-finite values.
Results may differ from the reference program's by a relative error of at most 0.025.
Values may be sent and summed in bfloat16 or wider, within the bound.
A program may use at most 320 MiB of HBM per device.

```python
import math
import jax
import jax.numpy as jnp
from jax import lax

D = 1536
FF = 8960
HEADS = 12
KV = 2
HEAD = 128
MICRO = 4
PIECES = 3
MB_TOK = 256
TOKENS_MB = 1024
LAYERS = 2


def draw_lengths(key, part):
    key = jax.random.fold_in(key, 7)
    keys_all = jax.random.split(key, 3)
    head_len = jax.random.randint(keys_all[0], (MICRO,), 1, MB_TOK)
    tail_len = jax.random.randint(keys_all[1], (MICRO,), 1, MB_TOK)
    chosen = jax.random.randint(keys_all[2], (), 0, MICRO)
    picked = jnp.arange(MICRO) == chosen
    head_len = jnp.where(picked, 1, head_len)
    tail_len = jnp.where(picked, 1, tail_len)
    middle_len = TOKENS_MB - head_len - tail_len
    return jnp.stack([head_len, middle_len, tail_len], axis=1).astype(jnp.int32)


def level_of(stream_key, dims, shards, smallest, high):
    def one(axis_at, parts):
        heights = jax.random.uniform(jax.random.fold_in(jax.random.fold_in(stream_key, 6), axis_at), (parts,), jnp.float32, smallest / len(shards), high / len(shards))
        return jnp.repeat(jnp.exp(heights), dims[axis_at] // parts).reshape((-1,) + (1,) * (len(dims) - axis_at - 1))

    loudness = one(*shards[0])
    for cut in shards[1:]:
        loudness = loudness * one(*cut)
    return loudness


def scatter_about(own_key, shape, width, bound, cuts=(), kind=jnp.bfloat16):
    level = level_of(own_key, shape, cuts, -0.22, 0.18) if cuts else 1.0
    values = jax.random.normal(own_key, shape, jnp.float32) * width * level
    return jnp.minimum(jnp.maximum(values, -bound), bound).astype(kind)


def setup_inputs(seed: int = 0) -> dict:
    key_of = jax.random.split(jax.random.key(seed), 14)
    return {
        "tokens": scatter_about(key_of[0], (MICRO, TOKENS_MB, D), 1.0, 6.0, ((1, 4),)),
        "cotangent": scatter_about(key_of[1], (MICRO, TOKENS_MB, D), 1.0, 6.0, ((1, 4),)),
        "lengths": draw_lengths(jax.random.fold_in(key_of[13], 71), 0),
        "norm_attn": jnp.clip(1.0 + 0.1 * jax.random.normal(key_of[3], (LAYERS, D), jnp.float32), 0.5, 1.5).astype(jnp.bfloat16),
        "w_query": scatter_about(key_of[4], (LAYERS, D, HEADS * HEAD), D ** -0.5, 0.15625, ((0, 2), (1, 4), (2, 4))),
        "b_query": scatter_about(key_of[5], (LAYERS, HEADS * HEAD), 0.5, 3.0, ((0, 2), (1, 4))),
        "w_keyval": scatter_about(key_of[6], (LAYERS, D, 2 * KV * HEAD), D ** -0.5, 0.15625, ((0, 2), (1, 16))),
        "b_keyval": scatter_about(key_of[7], (LAYERS, 2 * KV * HEAD), 0.5, 3.0, ((0, 2),)),
        "w_out": scatter_about(key_of[8], (LAYERS, HEADS * HEAD, D), HEAD ** -0.5, 0.5, ((0, 2), (1, 4), (2, 4))),
        "norm_ffn": jnp.clip(1.0 + 0.1 * jax.random.normal(key_of[9], (LAYERS, D), jnp.float32), 0.5, 1.5).astype(jnp.bfloat16),
        "w_gate": scatter_about(key_of[10], (LAYERS, D, FF), D ** -0.5, 0.15625, ((0, 2), (1, 4), (2, 4))),
        "w_up": scatter_about(key_of[11], (LAYERS, D, FF), D ** -0.5, 0.15625, ((0, 2), (1, 4), (2, 4))),
        "w_down": scatter_about(key_of[12], (LAYERS, FF, D), FF ** -0.5, 0.0625, ((0, 2), (1, 4), (2, 4))),
    }


EPS = 1e-06
THETA = 1000000.0
HIGHEST = lax.Precision.HIGHEST

@jax.custom_vjp
def low(v):
    return lax.optimization_barrier(v.astype(jnp.bfloat16)).astype(jnp.float32)

@jax.custom_vjp
def low_back(v):
    return v

def low_keep(v):
    return (low(v), None)

def low_pass(kept, grad):
    return (grad,)

def back_keep(v):
    return (v, None)

def back_low(kept, grad):
    return (low(grad),)
low.defvjp(low_keep, low_pass)
low_back.defvjp(back_keep, back_low)

def product(left_side, right_side):
    return jnp.dot(left_side, right_side, precision=HIGHEST)

def rms_norm(stream, gain):
    inverse = lax.rsqrt(lax.optimization_barrier(jnp.mean(stream * stream, axis=-1, keepdims=True)) + EPS)
    return stream * inverse * gain

def rope_tables(positions):
    inverse = THETA ** (-(jnp.arange(HEAD // 2, dtype=jnp.float32) * 2.0 / HEAD))
    angle = positions.astype(jnp.float32)[:, None] * inverse[None, :]
    return (jnp.cos(angle)[:, None, :], jnp.sin(angle)[:, None, :])

def rotate(vectors, cosine, sine):
    half_size = vectors.shape[-1] // 2
    first_half = vectors[..., :half_size]
    second_half = vectors[..., half_size:]
    return jnp.concatenate([first_half * cosine - second_half * sine, second_half * cosine + first_half * sine], axis=-1)

def layout(lengths_row):
    token_index = jnp.arange(TOKENS_MB, dtype=jnp.int32)
    seq_ends = jnp.cumsum(lengths_row).astype(jnp.int32)
    segment = lax.optimization_barrier(jnp.sum((token_index[:, None] >= seq_ends[None, :]).astype(jnp.int32), axis=1)).astype(jnp.int32)
    seq_starts = seq_ends - lengths_row.astype(jnp.int32)
    piece_ids = jnp.arange(PIECES, dtype=jnp.int32)
    first_index = lax.optimization_barrier(jnp.sum(jnp.where(segment[:, None] == piece_ids[None, :], seq_starts[None, :], 0), axis=1)).astype(jnp.int32)
    return (segment, token_index - first_index)

def layer(params, stream, segment, positions):
    gain_attn, w_query, b_query, w_keyval, b_keyval, w_out, gain_ffn, w_gate, w_up, w_down = params
    count = stream.shape[0]
    normed = low(rms_norm(stream, gain_attn))
    query = low_back(product(normed, w_query) + b_query).reshape(count, HEADS, HEAD)
    keyval = low_back(product(normed, w_keyval) + b_keyval)
    key_heads = keyval[:, :KV * HEAD].reshape(count, KV, HEAD)
    value_heads = low(keyval[:, KV * HEAD:].reshape(count, KV, HEAD))
    cosine, sine = rope_tables(positions)
    query = low(rotate(query, cosine, sine)).reshape(count, KV, HEADS // KV, HEAD)
    key_heads = low(rotate(key_heads, cosine, sine))
    scores = jnp.einsum('tkgd,skd->kgts', query, key_heads, precision=HIGHEST) * (1.0 / math.sqrt(HEAD))
    scores = low_back(scores)
    token_index = jnp.arange(count, dtype=jnp.int32)
    allowed = (segment[:, None] == segment[None, :]) & (token_index[None, :] <= token_index[:, None])
    masked = jnp.where(allowed, scores, -1e+30)
    row_max = lax.optimization_barrier(jnp.max(masked, axis=-1, keepdims=True))
    weights = jnp.exp(masked - row_max)
    probs = weights / lax.optimization_barrier(jnp.sum(weights, axis=-1, keepdims=True))
    mixed = jnp.einsum('kgts,skd->tkgd', low(probs), value_heads, precision=HIGHEST).reshape(count, HEADS * HEAD)
    mixed = low_back(low(mixed))
    second = stream + low_back(product(mixed, w_out))
    normed_two = low(rms_norm(second, gain_ffn))
    gate = low_back(product(normed_two, w_gate))
    up_proj = low_back(product(normed_two, w_up))
    hidden = low(jax.nn.silu(gate) * up_proj)
    return second + low_back(product(hidden, w_down))

def reference(tokens, cotangent, lengths, norm_attn, w_query, b_query, w_keyval, b_keyval, w_out, norm_ffn, w_gate, w_up, w_down):
    params = tuple((weight.astype(jnp.float32) for weight in (norm_attn, w_query, b_query, w_keyval, b_keyval, w_out, norm_ffn, w_gate, w_up, w_down)))

    def forward(layer_params, stream_in, probe):
        layer_one = tuple((weight[0] for weight in layer_params))
        layer_two = tuple((weight[1] for weight in layer_params))

        def one_batch(items):
            batch_in, batch_probe, batch_lengths = items
            segment, positions = layout(batch_lengths)
            middle = low_back(low(layer(layer_one, batch_in, segment, positions))) + batch_probe
            return (middle, layer(layer_two, middle, segment, positions))
        return lax.map(jax.checkpoint(one_batch), (stream_in, probe, lengths))
    stream_in = tokens.astype(jnp.float32)
    probe = jnp.zeros_like(stream_in)
    (middle, final), pullback = jax.vjp(forward, params, stream_in, probe)
    grad_params, grad_in, grad_middle = pullback((jnp.zeros_like(middle), cotangent.astype(jnp.float32)))
    activations = jnp.stack([middle, final]).astype(jnp.bfloat16)
    input_grads = jnp.stack([grad_in, grad_middle]).astype(jnp.bfloat16)
    return (activations, input_grads, grad_params[0], grad_params[1], grad_params[2], grad_params[3], grad_params[4], grad_params[5], grad_params[6], grad_params[7], grad_params[8], grad_params[9])
```

```python
import functools
import math

import jax
import jax.numpy as jnp
from jax import lax
from jax.experimental import pallas as pl
from jax.experimental.pallas import tpu as pltpu
from jax.sharding import PartitionSpec as P

HEADS = 12
KV = 2
HEAD = 128

EPS = 1e-06
THETA = 1000000.0

F32 = jnp.float32
BF16 = jnp.bfloat16

COL_LOW = ("col", 1)
COL_HIGH = ("col", 2)
ROW_LOW = ("row", 1)
SECTION = ("section", 1)


def swap(value, axis, flip):
    pairs = [(i, i ^ flip) for i in range(lax.axis_size(axis))]
    return lax.ppermute(value, axis, pairs)


def bit_of(index, bit):
    return (index >> bit) & 1


def pick(array, index, axis=0):
    return lax.dynamic_index_in_dim(array, index, axis, keepdims=False)


def ordered(mine, other, bit, axis):
    first = jnp.where(bit == 0, mine, other)
    second = jnp.where(bit == 0, other, mine)
    return jnp.concatenate([first, second], axis=axis)


def row_bits():
    return lax.axis_size("row").bit_length() - 1


def norm_backward(stream, inverse, gain, gradient):
    inner = jnp.mean(gradient * gain * stream, axis=-1, keepdims=True)
    d_stream = gain * gradient * inverse - stream * (inverse * inverse * inverse) * inner
    return (d_stream, jnp.sum(gradient * stream * inverse, axis=0, keepdims=True))


def dot(left, right, left_dim, right_dim):
    return lax.dot_general(
        left, right, (((left_dim,), (right_dim,)), ((), ())), preferred_element_type=F32
    )


def layout(lengths, place, row_count):
    section, row, low, high = place
    rows = lax.axis_size("row")
    half = row_count // 2
    inside = jnp.arange(row_count, dtype=jnp.int32)
    inside = (((inside // half) ^ low) * half) + inside % half
    own_index = row * row_count + inside
    key_index = ((jnp.arange(rows, dtype=jnp.int32) ^ row) * row_count)[:, None] + inside[None, :]
    slots = 2 * section + (jnp.arange(2, dtype=jnp.int32) ^ high)
    picked = jnp.stack([pick(lengths, slots[0]), pick(lengths, slots[1])])
    ends = jnp.cumsum(picked, axis=1)
    starts = ends - picked
    inside_piece = (own_index[None, None, :] >= starts[:, :, None]) & (
        own_index[None, None, :] < ends[:, :, None]
    )
    first = jnp.sum(jnp.where(inside_piece, starts[:, :, None], 0), axis=1)
    inverse = THETA ** (-(jnp.arange(HEAD // 2, dtype=F32) * 2.0 / HEAD))
    angle = (own_index[None, :] - first).astype(F32).reshape(-1, 1) * inverse
    cosine, sine = jnp.cos(angle), jnp.sin(angle)
    return (
        jnp.concatenate([cosine, cosine], axis=1),
        jnp.concatenate([-sine, sine], axis=1),
        first,
        own_index[None, :],
        key_index.reshape(-1, 1),
    )


MESH = pl.DeviceIdType.MESH
VMEM_LIMIT = 60 * 1024 * 1024


def partner_of(way):
    axis, flip = way
    return {axis: lax.axis_index(axis) ^ flip}


def enter(ways):
    barrier = pltpu.get_barrier_semaphore()
    for way in ways:
        pl.semaphore_signal(barrier, inc=1, device_id=partner_of(way), device_id_type=MESH)
    pl.semaphore_wait(barrier, len(ways))


class Links:
    def __init__(self, send, recv):
        self.send, self.recv, self.used = send, recv, 0

    def copy(self, source, target, way):
        slot = self.used
        self.used += 1
        return pltpu.make_async_remote_copy(
            src_ref=source,
            dst_ref=target,
            send_sem=self.send.at[slot],
            recv_sem=self.recv.at[slot],
            device_id=partner_of(way),
            device_id_type=MESH,
        )


def gather_copies(links, blocks, a, b, sides=True, own=None):
    h = blocks.shape[2] // 2
    own = blocks.at[0, 0] if own is None else own
    copies = {
        "a": links.copy(own, blocks.at[1, 0], a),
        "b": links.copy(own, blocks.at[2, 0], b),
        "ab": links.copy(blocks.at[1, 0, pl.ds(0, h)], blocks.at[3, 0, pl.ds(0, h)], b),
        "ba": links.copy(blocks.at[2, 0, pl.ds(h, h)], blocks.at[3, 0, pl.ds(h, h)], a),
    }
    if sides:
        copies["s0"] = links.copy(own, blocks.at[0, 1], SECTION)
        for k in (1, 2, 3):
            copies[f"s{k}"] = links.copy(blocks.at[k, 0], blocks.at[k, 1], SECTION)
    return copies


def ffn_exchange(links, a, b, blocks, gathers, buffers, step, moves):
    mine, side_out, side_in, corner_out, corner_in, edge_out, edge_in = buffers
    n = blocks.shape[2]
    h = n // 2
    gather = gather_copies(links, blocks, a, b) if gathers else {}
    sides = [links.copy(side_out.at[k], side_in.at[k], SECTION) for k in range(4)]
    corner_b, corner_a, edge_a, edge_b = scatter_copies(
        links, corner_out, corner_in, edge_out, edge_in, a, b
    )
    lead, rest = moves[:1], moves[1:]

    def start(*names):
        for name in names:
            if gathers:
                gather[name].start()

    def wait(*names):
        for name in names:
            if gathers:
                gather[name].wait_recv()

    start("a", "b", "s0")
    for move in lead:
        move.advance()
    wait("s0")
    step(0)
    sides[0].start()
    wait("a")
    start("ab", "s1")
    wait("b")
    start("ba", "s2")
    wait("s1")
    step(1)
    sides[1].start()
    wait("ab", "ba")
    start("s3")
    wait("s3")
    step(3)
    sides[3].start()
    sides[3].wait_recv()
    total = mine[3] + side_in[3].astype(F32)
    corner_out[...] = total.astype(BF16).reshape(corner_out.shape)
    corner_b.start()
    corner_a.start()
    for move in moves:
        move.advance()
    wait("s2")
    step(2)
    sides[2].start()
    sides[1].wait_recv()
    corner_b.wait_recv()
    edge_out[0, :h] = (mine[1, :h] + side_in[1, :h].astype(F32) + corner_in[0].astype(F32)).astype(BF16)
    edge_out[0, h:] = (mine[1, h:] + side_in[1, h:].astype(F32)).astype(BF16)
    edge_a.start()
    sides[2].wait_recv()
    corner_a.wait_recv()
    edge_out[1, :h] = (mine[2, :h] + side_in[2, :h].astype(F32)).astype(BF16)
    edge_out[1, h:] = (mine[2, h:] + side_in[2, h:].astype(F32) + corner_in[1].astype(F32)).astype(BF16)
    edge_b.start()
    for move in rest:
        move.advance()
    sides[0].wait_recv()
    total = mine[0] + side_in[0].astype(F32)
    edge_a.wait_recv()
    edge_b.wait_recv()
    total = total + edge_in[0].astype(F32) + edge_in[1].astype(F32)
    for move in rest:
        move.advance()
    for move in moves:
        move.end()
    wait_all([], [*gather.values(), *sides, corner_a, corner_b, edge_a, edge_b])
    return total


def hidden_tiles(hidden):
    return [(at, min(384, hidden - at)) for at in range(0, hidden, 384)]


def padded(hidden):
    return -(-hidden // 128) * 128


def width_tiles(width):
    return [(at, 512) for at in range(0, width, 512)]


def load_copies(sources, targets, sems):
    each = len(sources) // len(targets)
    copies = []
    for i, source in enumerate(sources):
        rows, columns = source.shape[1:]
        for block in range(source.shape[0]):
            place = (pl.ds((i % each) * rows, rows), pl.ds(block * columns, columns))
            copies.append(
                pltpu.make_async_copy(
                    source.at[block], targets[i // each].at[place], sems.at[len(copies)]
                )
            )
    return copies


def load_count(sources):
    return sum(source.shape[0] for source in sources)


def pad_weights(sources, targets):
    filled = sources[0].shape[1] * (len(sources) // len(targets))
    for target in targets:
        if filled < target.shape[0]:
            target[filled:] = jnp.zeros((target.shape[0] - filled, target.shape[1]), target.dtype)


def save(started, sems, sources, targets):
    for source, target in zip(sources, targets, strict=True):
        started.append(pltpu.make_async_copy(source, target, sems.at[len(started)]))
        started[-1].start()


def put_partial(k, at, size, value, mine, side_out):
    n = mine.shape[1]
    mine[k, :, pl.ds(at, size)] = value[:n]
    side_out[k, :, pl.ds(at, size)] = value[n:].astype(BF16)


def ffn_forward_kernel(
    a, b, run,
    second_ref, gain_ref, *refs,
):
    weights_hbm, refs = refs[:-23], refs[-23:]
    (
        result_ref, blocks_hbm, gate_hbm, up_hbm, act_hbm,
        w_gate, w_up, w_down, blocks, gate_out, up_out, act_out, *buffers,
        load_sem, save_sem, send, recv,
    ) = refs
    loads = load_copies(weights_hbm, (w_gate, w_up, w_down), load_sem)
    for copy in loads:
        copy.start()
    pad_weights(weights_hbm, (w_gate, w_up, w_down))
    second = second_ref[...]
    inverse = lax.rsqrt(jnp.mean(second * second, axis=-1, keepdims=True) + EPS)
    blocks[0, 0] = (second * inverse * gain_ref[...]).astype(BF16)
    run.enter()
    n = blocks.shape[2]
    width = blocks.shape[3]
    hidden = w_gate.shape[0]
    saves = []

    def step(k):
        if k == 0:
            for copy in loads:
                copy.wait()
        x = blocks[k].reshape(2 * n, width)
        rows = pl.ds(k * 2 * n, 2 * n)
        for at, size in hidden_tiles(hidden):
            gate = dot(x, w_gate[pl.ds(at, size)], 1, 1)
            up = dot(x, w_up[pl.ds(at, size)], 1, 1)
            act = gate / (1.0 + jnp.exp(-gate)) * up
            gate_out[rows, pl.ds(at, size)] = gate.astype(BF16)
            up_out[rows, pl.ds(at, size)] = up.astype(BF16)
            act_out[rows, pl.ds(at, size)] = act.astype(BF16)
        save(saves, save_sem, (blocks.at[k], gate_out.at[rows], up_out.at[rows], act_out.at[rows]),
             (blocks_hbm.at[k], gate_hbm.at[rows], up_hbm.at[rows], act_hbm.at[rows]))
        act = act_out[rows]
        for at, size in width_tiles(width):
            put_partial(k, at, size, dot(act, w_down[:, pl.ds(at, size)], 1, 0), *buffers[:2])

    total = ffn_exchange(Links(send, recv), a, b, blocks, True, buffers, step, run.moves)
    result_ref[...] = second_ref[...] + total
    for copy in saves:
        copy.wait()


def ffn_backward_kernel(
    gathers, a, b, run,
    grad_ref, second_ref, gain_ref, gate_hbm, up_hbm, *refs,
):
    weights_hbm, refs = refs[:-24], refs[-24:]
    (
        result_ref, d_gain_ref, blocks_hbm, d_gate_hbm, d_up_hbm,
        w_gate, w_up, w_down, blocks, gate_in, up_in, d_gate_out, d_up_out, *buffers,
        load_sem, save_sem, send, recv,
    ) = refs
    more = [(gate_hbm, gate_in), (up_hbm, up_in)]
    if not gathers:
        gathered, *weights_hbm = weights_hbm
        more.append((gathered, blocks))
    loads = load_copies(weights_hbm, (w_gate, w_up, w_down), load_sem)
    pad_weights(weights_hbm, (w_gate, w_up, w_down))
    for source, target in more:
        loads.append(pltpu.make_async_copy(source, target, load_sem.at[len(loads)]))
    for copy in loads:
        copy.start()
    if gathers:
        blocks[0, 0] = grad_ref[...]
    run.enter()
    n = blocks.shape[2]
    width = blocks.shape[3]
    hidden = w_gate.shape[0]
    saves = []

    def step(k):
        if k == 0:
            for copy in loads:
                copy.wait()
        g = blocks[k].reshape(2 * n, width)
        rows = pl.ds(k * 2 * n, 2 * n)
        for at, size in hidden_tiles(hidden):
            d_act = dot(g, w_down[pl.ds(at, size)], 1, 1)
            gate = gate_in[rows, pl.ds(at, size)].astype(F32)
            up = up_in[rows, pl.ds(at, size)].astype(F32)
            sigma = 1.0 / (1.0 + jnp.exp(-gate))
            d_gate_out[rows, pl.ds(at, size)] = (
                d_act * up * sigma * (1.0 + gate * (1.0 - sigma))
            ).astype(BF16)
            d_up_out[rows, pl.ds(at, size)] = (d_act * gate * sigma).astype(BF16)
        save(saves, save_sem, (blocks.at[k], d_gate_out.at[rows], d_up_out.at[rows]),
             (blocks_hbm.at[k], d_gate_hbm.at[rows], d_up_hbm.at[rows]))
        d_gate = d_gate_out[rows]
        d_up = d_up_out[rows]
        for at, size in width_tiles(width):
            value = dot(d_gate, w_gate[:, pl.ds(at, size)], 1, 0)
            value = value + dot(d_up, w_up[:, pl.ds(at, size)], 1, 0)
            put_partial(k, at, size, value, *buffers[:2])

    d_normed = ffn_exchange(Links(send, recv), a, b, blocks, gathers, buffers, step, run.moves)
    second = second_ref[...]
    inverse = lax.rsqrt(jnp.mean(second * second, axis=-1, keepdims=True) + EPS)
    d_second, d_gain = norm_backward(second, inverse, gain_ref[...], d_normed)
    d_gain_ref[...] = d_gain
    result_ref[...] = grad_ref[...].astype(F32) + d_second
    for copy in saves:
        copy.wait()


class Run:
    def __init__(self, ways, moves):
        self.ways, self.moves = ways, moves

    def enter(self):
        enter(self.ways)


def kernel_call(kernel, collective_id, ways, operands, after, outs, scratch, flops, moves=()):
    vmem = pl.BlockSpec(memory_space=pltpu.VMEM)
    hbm = pl.BlockSpec(memory_space=pl.ANY)
    moved_in = [array for move in moves for array in move.operands]
    moved_out = [out for move in moves for out in move.outs]
    every = list(ways)
    for move in moves:
        every += [way for way in move.ways if way not in every]

    def body(*refs):
        refs = list(refs)

        def take(count):
            taken, refs[:] = refs[:count], refs[count:]
            return taken

        own_in = take(len(operands))
        take(len(after))
        moves_in = [take(len(move.operands)) for move in moves]
        token = take(1)[0]
        own_out = take(len(outs))
        moves_out = [take(len(move.outs)) for move in moves]
        own_scratch = take(len(scratch))
        for move, sources, targets in zip(moves, moves_in, moves_out, strict=True):
            move.bind(sources, targets, take(len(move.scratch)))
        token[...] = jnp.zeros_like(token)
        kernel(Run(every, moves), *own_in, *own_out, *own_scratch)

    token, *results = pl.pallas_call(
        body,
        out_shape=[
            jax.ShapeDtypeStruct((8, 128), jnp.int32),
            *[jax.ShapeDtypeStruct(shape, dtype) for shape, dtype, _ in outs],
            *[jax.ShapeDtypeStruct(shape, BF16) for shape in moved_out],
        ],
        in_specs=[vmem if inside else hbm for _, inside in operands]
        + [hbm] * (len(after) + len(moved_in)),
        out_specs=[vmem]
        + [vmem if inside else hbm for _, _, inside in outs]
        + [hbm] * len(moved_out),
        scratch_shapes=[*scratch, *[ref for move in moves for ref in move.scratch]],
        compiler_params=pltpu.CompilerParams(
            collective_id=collective_id, has_side_effects=True, vmem_limit_bytes=VMEM_LIMIT
        ),
        cost_estimate=pl.CostEstimate(flops=flops, bytes_accessed=16 << 20, transcendentals=1 << 20),
    )(*[array for array, _ in operands], *after, *moved_in)
    results, moved = results[: len(outs)], results[len(outs) :]
    lists = []
    for move in moves:
        lists.append(moved[: len(move.outs)])
        moved = moved[len(move.outs) :]
    return token[0, 0], results, lists


def remote(source, target, send, recv, way):
    return pltpu.make_async_remote_copy(
        src_ref=source,
        dst_ref=target,
        send_sem=send,
        recv_sem=recv,
        device_id=partner_of(way),
        device_id_type=MESH,
    )


def row_hops(bits):
    hops, known = [], [0]
    for bit in reversed(range(bits)):
        step = 1 << bit
        hops += [(slot, slot | step, bit) for slot in known]
        known += [slot | step for slot in known]
    return hops


class Move:
    def __init__(self, operands, outs, scratch, ways):
        self.operands, self.outs, self.scratch, self.ways = operands, outs, scratch, ways
        self.steps, self.at = [], 0

    def advance(self):
        if self.at < len(self.steps):
            self.steps[self.at]()
            self.at += 1

    def end(self):
        while self.at < len(self.steps):
            self.advance()


def semaphores(*counts):
    return [pltpu.SemaphoreType.DMA((count,)) for count in counts]


def wait_all(arriving, leaving):
    for copy in arriving:
        copy.wait_recv()
    for copy in leaving:
        copy.wait_send()


class FfnGather(Move):
    def __init__(self, part, across):
        rows = lax.axis_size("row")
        self.flips, self.across = list(range(1, rows)), across
        outs = [(rows, *part.shape[1:])] * 2
        ways = [("row", flip) for flip in self.flips] + [across]
        super().__init__([part], outs, semaphores(rows, rows, rows, rows, 1), ways)

    def bind(self, sources, targets, scratch):
        (part,), (own, other) = sources, targets
        row_send, row_recv, far_send, far_recv, local_sem = scratch
        row = lax.axis_index("row")
        near = part.at[row & 1]
        local = pltpu.make_async_copy(near, own.at[row], local_sem.at[0])
        hops = {
            flip: remote(
                part.at[(row ^ flip) & 1], own.at[row], row_send.at[flip], row_recv.at[flip], ("row", flip)
            )
            for flip in self.flips
        }
        far = [
            remote(
                own.at[row ^ flip] if flip else near,
                other.at[row ^ flip],
                far_send.at[flip],
                far_recv.at[flip],
                self.across,
            )
            for flip in [0] + self.flips
        ]

        def start():
            local.start()
            for flip in self.flips:
                hops[flip].start()

        def forward():
            far[0].start()
            for flip in self.flips:
                hops[flip].wait_recv()
                far[flip].start()

        def finish():
            local.wait()
            wait_all(far, [*hops.values(), *far])

        self.steps = [start, forward, finish]


class AttnGather(Move):
    def __init__(self, part):
        rows = lax.axis_size("row")
        self.bits = rows.bit_length() - 1
        ways = [("row", 1 << bit) for bit in range(self.bits)] + [SECTION]
        super().__init__([part], [(2, rows, *part.shape)], semaphores(rows, rows, rows, rows, 1), ways)

    def bind(self, sources, targets, scratch):
        (part,), (blocks,) = sources, targets
        row_send, row_recv, side_send, side_recv, local_sem = scratch
        section, row = lax.axis_index("section"), lax.axis_index("row")

        def place(slot):
            return blocks.at[section, row ^ slot]

        def source(slot):
            return place(slot) if slot else part

        local = pltpu.make_async_copy(part, place(0), local_sem.at[0])
        hops = [
            (slot, filled, remote(source(slot), place(slot), row_send.at[filled], row_recv.at[filled], ("row", 1 << bit)))
            for slot, filled, bit in row_hops(self.bits)
        ]
        sides = [
            remote(source(slot), place(slot), side_send.at[slot], side_recv.at[slot], SECTION)
            for slot in range(1 << self.bits)
        ]
        arrived = {0}

        def arrive(slot):
            if slot not in arrived:
                arrived.add(slot)
                for _, filled, copy in hops:
                    if filled == slot:
                        copy.wait_recv()
                sides[slot].start()

        def start():
            local.start()
            for slot, _, copy in hops:
                if slot == 0:
                    copy.start()
            sides[0].start()

        def forward():
            for slot, _, copy in hops:
                if slot:
                    arrive(slot)
                    copy.start()

        def finish():
            for slot in range(len(sides)):
                arrive(slot)
            local.wait()
            wait_all(sides, [copy for _, _, copy in hops] + sides)

        self.steps = [start, forward, finish]


class TokenGather(Move):
    def __init__(self, own, a, b, sides):
        self.a, self.b, self.sides = a, b, sides
        ways = [a, b] + ([SECTION] if sides else [])
        super().__init__([own], [(4, 1 + sides, *own.shape)], semaphores(8, 8, 1), ways)

    def bind(self, sources, targets, scratch):
        (own,), (blocks,) = sources, targets
        send, recv, local_sem = scratch
        local = pltpu.make_async_copy(own, blocks.at[0, 0], local_sem.at[0])
        copies = gather_copies(Links(send, recv), blocks, self.a, self.b, self.sides, own)
        sides = [name for name in ("s0", "s1", "s2", "s3") if self.sides]

        def start():
            local.start()
            for name in ["a", "b"] + sides[:1]:
                copies[name].start()

        def forward():
            copies["a"].wait_recv()
            copies["ab"].start()
            copies["b"].wait_recv()
            copies["ba"].start()
            for name in sides[1:3]:
                copies[name].start()

        def last():
            copies["ab"].wait_recv()
            copies["ba"].wait_recv()
            for name in sides[3:]:
                copies[name].start()

        def finish():
            local.wait()
            wait_all([copies[name] for name in sides], copies.values())

        self.steps = [start, forward, last, finish]


class Across(Move):
    def __init__(self, grad, n, way):
        self.n, self.way = n, way
        super().__init__([grad], [(n, grad.shape[1])], semaphores(1, 1), [way])

    def bind(self, sources, targets, scratch):
        (grad,), (arrived,) = sources, targets
        send, recv = scratch
        copy = remote(grad.at[pl.ds(self.n, self.n)], arrived, send.at[0], recv.at[0], self.way)
        self.steps = [copy.start, lambda: wait_all([copy], [copy])]


class Rows(Move):
    def __init__(self, total):
        rows = total.shape[0]
        self.flips = list(range(1, rows))
        ways = [("row", flip) for flip in self.flips]
        super().__init__([total], [total.shape], semaphores(rows, rows), ways)

    def bind(self, sources, targets, scratch):
        (total,), (arrived,) = sources, targets
        send, recv = scratch
        copies = row_copies(total, arrived, send, recv, self.flips)

        def start():
            for copy in copies:
                copy.start()

        self.steps = [start, lambda: wait_all(copies, copies)]


def row_copies(total, arrived, send, recv, flips):
    row = lax.axis_index("row")
    return [
        remote(total.at[row ^ flip], arrived.at[flip], send.at[flip], recv.at[flip], ("row", flip))
        for flip in flips
    ]


class GradScatter(Move):
    def __init__(self, grad, n, way):
        rows, width = lax.axis_size("row"), grad.shape[1]
        self.n, self.way, self.flips = n, way, list(range(1, rows))
        shape = (rows, n, width // rows)
        scratch = [pltpu.VMEM((n, width), BF16), pltpu.VMEM((n, width), BF16), pltpu.VMEM(shape, BF16)]
        scratch += semaphores(1, 1, 1, 1, rows, rows)
        ways = [way] + [("row", flip) for flip in self.flips]
        super().__init__([grad], [shape[1:], shape], scratch, ways)

    def bind(self, sources, targets, scratch):
        (grad,), (own, arrived) = sources, targets
        mine, theirs, total, local_sem, own_sem, far_send, far_recv, row_send, row_recv = scratch
        n, row = self.n, lax.axis_index("row")
        depth = total.shape[2]
        local = pltpu.make_async_copy(grad.at[pl.ds(0, n)], mine, local_sem.at[0])
        far = remote(grad.at[pl.ds(n, n)], theirs, far_send.at[0], far_recv.at[0], self.way)
        keep = pltpu.make_async_copy(total.at[row], own, own_sem.at[0])
        copies = row_copies(total, arrived, row_send, row_recv, self.flips)

        def start():
            local.start()
            far.start()

        def forward():
            local.wait()
            far.wait_recv()
            for block in range(total.shape[0]):
                at = slice(block * depth, (block + 1) * depth)
                total[block] = (mine[:, at].astype(F32) + theirs[:, at].astype(F32)).astype(BF16)
            for copy in copies + [keep]:
                copy.start()

        def finish():
            keep.wait()
            wait_all(copies, copies + [far])

        self.steps = [start, forward, finish]


class AttnScatter(Move):
    def __init__(self, grad):
        rows, width, m = lax.axis_size("row"), grad.shape[1], grad.shape[0] // 2
        self.bits, self.m = rows.bit_length() - 1, m
        blocks = (rows, m, width // rows)
        scratch = [
            pltpu.VMEM((m, width), BF16),
            pltpu.VMEM((m, width), BF16),
            pltpu.VMEM(blocks, F32),
            pltpu.VMEM(blocks, BF16),
            pltpu.VMEM(blocks, BF16),
        ]
        scratch += semaphores(1, 1, 1, 1, rows, rows)
        ways = [SECTION] + [("row", 1 << bit) for bit in range(self.bits)]
        super().__init__([grad], [blocks[1:]], scratch, ways)

    def bind(self, sources, targets, scratch):
        (grad,), (out,) = sources, targets
        mine, theirs, total, going, coming, local_sem, out_sem, side_send, side_recv, send, recv = scratch
        m, row, section = self.m, lax.axis_index("row"), lax.axis_index("section")
        depth = total.shape[2]
        local = pltpu.make_async_copy(
            grad.at[pl.ds(pl.multiple_of(section * m, m), m)], mine, local_sem.at[0]
        )
        side = remote(
            grad.at[pl.ds(pl.multiple_of((1 - section) * m, m), m)],
            theirs,
            side_send.at[0],
            side_recv.at[0],
            SECTION,
        )
        keep = pltpu.make_async_copy(going.at[0], out, out_sem.at[0])
        hops = [
            (slot, filled, remote(going.at[filled], coming.at[filled], send.at[filled], recv.at[filled], ("row", 1 << bit)))
            for slot, filled, bit in reversed(row_hops(self.bits))
        ]

        def start():
            local.start()
            side.start()

        def sum_sides():
            local.wait()
            side.wait_recv()
            for block in range(total.shape[0]):
                at = slice(block * depth, (block + 1) * depth)
                total[row ^ block] = mine[:, at].astype(F32) + theirs[:, at].astype(F32)
            send_bit(0)

        def send_bit(bit):
            for slot, filled, copy in hops:
                if filled - slot == 1 << bit:
                    going[filled] = total[filled].astype(BF16)
                    copy.start()

        def add_bit(bit):
            for slot, filled, copy in hops:
                if filled - slot == 1 << bit:
                    copy.wait_recv()
                    total[slot] = total[slot] + coming[filled].astype(F32)

        def hop(bit):
            def step():
                add_bit(bit - 1)
                send_bit(bit)

            return step

        def finish():
            add_bit(self.bits - 1)
            going[0] = total[0].astype(BF16)
            keep.start()
            keep.wait()
            wait_all([], [copy for _, _, copy in hops] + [side])

        self.steps = [start, sum_sides, *[hop(bit) for bit in range(1, self.bits)], finish]


def move_kernel(run):
    run.enter()
    while any(move.at < len(move.steps) for move in run.moves):
        for move in run.moves:
            move.advance()


def loadable(blocks):
    if blocks.shape[-1] % 128 == 0:
        return blocks
    whole = jnp.swapaxes(blocks, -3, -2)
    return whole.reshape(*whole.shape[:-3], 1, whole.shape[-3], -1)


def ffn_call(kernel, a, b, collective_id, operands, big, weights, after, sizes, small_outs, hidden_outs, moves=()):
    n, width, _, hidden = sizes
    tokens = 8 * n
    hidden = padded(hidden)
    weights = [loadable(half) for halves in weights for half in halves]
    token, outs, moved = kernel_call(
        functools.partial(kernel, a, b),
        collective_id,
        (a, b, SECTION),
        [(array, True) for array in operands] + [(array, False) for array in (*big, *weights)],
        after,
        [(shape, F32, True) for shape in small_outs]
        + [((4, 2, n, width), BF16, False)]
        + [((tokens, hidden), BF16, False)] * hidden_outs,
        [
            *[pltpu.VMEM((hidden, width), BF16) for _ in range(3)],
            pltpu.VMEM((4, 2, n, width), BF16),
            *[pltpu.VMEM((tokens, hidden), BF16) for _ in range(min(len(big), 2) + hidden_outs)],
            pltpu.VMEM((4, n, width), F32),
            pltpu.VMEM((4, n, width), BF16),
            pltpu.VMEM((4, n, width), BF16),
            pltpu.VMEM((2, n // 2, width), BF16),
            pltpu.VMEM((2, n // 2, width), BF16),
            pltpu.VMEM((2, n, width), BF16),
            pltpu.VMEM((2, n, width), BF16),
            pltpu.SemaphoreType.DMA((load_count(weights) + len(big),)),
            pltpu.SemaphoreType.DMA((4 * (1 + hidden_outs),)),
            pltpu.SemaphoreType.DMA((16,)),
            pltpu.SemaphoreType.DMA((16,)),
        ],
        3 * 2 * tokens * width * hidden,
        moves,
    )
    at = len(small_outs)
    outs[at] = outs[at].reshape(tokens, width)
    return token, outs, moved


def turn(vectors, cosine, sine):
    return vectors * cosine + pltpu.roll(vectors, HEAD // 2, 1) * sine


def scatter_copies(links, corner_out, corner_in, edge_out, edge_in, a, b):
    return (
        links.copy(corner_out.at[0], corner_in.at[0], b),
        links.copy(corner_out.at[1], corner_in.at[1], a),
        links.copy(edge_out.at[0], edge_in.at[0], a),
        links.copy(edge_out.at[1], edge_in.at[1], b),
    )


def seen(start_ref, own_ref, key_ref, slot):
    key = key_ref[...]
    visible = (key >= start_ref[pl.ds(slot, 1)]) & (key <= own_ref[...])
    return jnp.where(visible, 0.0, -1e30)


def attention_weights(blocks, weights, sems):
    loads = load_copies([blocks.at[0], blocks.at[1]], [weights], sems)
    for copy in loads:
        copy.start()
    heads_width = (weights.shape[0] - 2 * HEAD) // 2
    return (
        loads,
        weights.at[pl.ds(0, heads_width)],
        weights.at[pl.ds(heads_width, heads_width)],
        weights.at[pl.ds(2 * heads_width, 2 * HEAD)],
    )


def attention_forward_kernel(
    gathers, run,
    entry_ref, gain_ref, b_query_ref, b_pair_ref, cos_ref, sin_ref, start_ref, own_ref, key_ref,
    weights_hbm,
    second_ref, normed, query, mixed, lse_ref, kv_hbm, entry_hbm,
    weights, entry, kv, bias, partial, corner_out, corner_in, edge_out, edge_in,
    load_sem, save_sem, send, recv,
):
    loads, w_query, w_out, w_pair = attention_weights(weights_hbm, weights, load_sem)
    links = Links(send, recv)
    n, width = entry.shape[1:]
    h = n // 2
    tokens = 2 * n
    rows, heads = kv.shape[1], w_query.shape[0] // HEAD
    bits = rows.bit_length() - 1
    scale = 1.0 / math.sqrt(HEAD)
    if gathers:
        entry[0] = entry_ref[...].astype(BF16)
    else:
        entry[...] = entry_ref[...]
    run.enter()
    moves = run.moves

    def normalise(k):
        x = entry[k].astype(F32)
        inverse = lax.rsqrt(jnp.mean(x * x, axis=-1, keepdims=True) + EPS)
        normed[pl.ds(k * n, n)] = (x * inverse * gain_ref[...]).astype(BF16)

    saves, copies = [], []
    if gathers:
        to_low = links.copy(entry.at[0], entry.at[1], COL_LOW)
        to_high = links.copy(entry.at[0], entry.at[2], COL_HIGH)
        corner_high = links.copy(entry.at[1, pl.ds(0, h)], entry.at[3, pl.ds(0, h)], COL_HIGH)
        corner_low = links.copy(entry.at[2, pl.ds(h, h)], entry.at[3, pl.ds(h, h)], COL_LOW)
        to_low.start()
        to_high.start()
        normalise(0)
        to_low.wait_recv()
        corner_high.start()
        to_high.wait_recv()
        corner_low.start()
        normalise(1)
        normalise(2)
        copies += [to_low, to_high, corner_high, corner_low]

    hops = [
        [(slot, filled, links.copy(kv.at[b, slot], kv.at[b, filled], ("row", 1 << bit)))
         for slot, filled, bit in row_hops(bits)]
        for b in range(2)
    ]

    def project_pair(b):
        at = pl.ds(b * tokens, tokens)
        pair = dot(normed[at], w_pair[...], 1, 1) + b_pair_ref[...]
        kv[b, 0, :, :HEAD] = turn(pair[:, :HEAD], cos_ref[at], sin_ref[at]).astype(BF16)
        kv[b, 0, :, HEAD:] = pair[:, HEAD:].astype(BF16)
        for slot, _, copy in hops[b]:
            if slot == 0:
                copy.start()

    def project_query(b):
        at = pl.ds(b * tokens, tokens)
        projected = dot(normed[at], w_query[...], 1, 1) + b_query_ref[...]
        for head in range(heads):
            lanes = slice(head * HEAD, (head + 1) * HEAD)
            query[at, lanes] = turn(projected[:, lanes], cos_ref[at], sin_ref[at]).astype(BF16)

    arrived = [set(), set()]

    def arrive(b, slot):
        for _, filled, copy in hops[b]:
            if filled == slot and slot not in arrived[b]:
                copy.wait_recv()
                arrived[b].add(slot)

    for move in moves[:1]:
        move.advance()
    for copy in loads:
        copy.wait()
    if gathers:
        project_pair(0)
        corner_high.wait_recv()
        corner_low.wait_recv()
        normalise(3)
        project_pair(1)
    else:
        normalise(2)
        normalise(3)
        project_pair(1)
        normalise(0)
        normalise(1)
        project_pair(0)
    project_query(1)
    project_query(0)
    for move in moves[:1]:
        move.advance()
    for b in (1, 0):
        for slot, _, copy in hops[b]:
            if slot:
                arrive(b, slot)
                copy.start()
    for move in moves[1:]:
        move.advance()

    corner_b, corner_a, edge_a, edge_b = scatter_copies(
        links, corner_out, corner_in, edge_out, edge_in, COL_LOW, COL_HIGH
    )
    for b in (1, 0):
        for slot in range(1, rows):
            arrive(b, slot)
        save(saves, save_sem, (kv.at[b],), (kv_hbm.at[b],))
        keys = kv[b, :, :, :HEAD].reshape(rows * tokens, HEAD)
        values = kv[b, :, :, HEAD:].reshape(rows * tokens, HEAD)
        at = pl.ds(b * tokens, tokens)
        bias[...] = seen(start_ref, own_ref, key_ref, b)
        for head in range(heads):
            lanes = slice(head * HEAD, (head + 1) * HEAD)
            scores = dot(keys, query[at, lanes], 1, 1) * scale + bias[...]
            top = jnp.max(scores, axis=0, keepdims=True)
            raised = jnp.exp(scores - top)
            total = jnp.sum(raised, axis=0, keepdims=True)
            lse_ref[b, pl.ds(head, 1)] = top + jnp.log(total)
            probs = (raised * (1.0 / total)).astype(BF16)
            mixed[at, lanes] = dot(probs, values, 0, 0).astype(BF16)
        for k in (2 * b + 1, 2 * b):
            for lane, size in width_tiles(width):
                partial[k, :, pl.ds(lane, size)] = dot(
                    mixed[pl.ds(k * n, n)], w_out[:, pl.ds(lane, size)], 1, 0
                )
        if b == 1:
            corner_out[...] = partial[3].astype(BF16).reshape(corner_out.shape)
            corner_b.start()
            corner_a.start()
    corner_a.wait_recv()
    edge_out[1, :h] = partial[2, :h].astype(BF16)
    edge_out[1, h:] = (partial[2, h:] + corner_in[1].astype(F32)).astype(BF16)
    edge_b.start()
    corner_b.wait_recv()
    edge_out[0, :h] = (partial[1, :h] + corner_in[0].astype(F32)).astype(BF16)
    edge_out[0, h:] = partial[1, h:].astype(BF16)
    edge_a.start()
    if gathers:
        save(saves, save_sem, (entry,), (entry_hbm,))
    for move in moves[1:2]:
        move.advance()
    own = entry[0].astype(F32) + partial[0]
    edge_b.wait_recv()
    edge_a.wait_recv()
    second_ref[...] = own + edge_in[0].astype(F32) + edge_in[1].astype(F32)
    for move in moves[2:]:
        move.advance()
    for move in moves:
        move.end()
    copies += [copy for group in hops for _, _, copy in group] + [corner_a, corner_b, edge_a, edge_b]
    wait_all([], copies)
    for copy in saves:
        copy.wait()


def attention_backward_kernel(
    run,
    d_second_ref, entry_ref, gain_ref, cos_ref, sin_ref, start_ref, own_ref, key_ref,
    query, kv, lse_ref, weights_hbm,
    d_entry_ref, d_gain_ref, d_query, d_pair, d_bias_query_ref, d_bias_pair_ref, blocks_hbm,
    weights, blocks, d_mixed, bias, d_kv, d_kv_out, d_kv_in, share_out, share_in,
    partial, corner_out, corner_in, edge_out, edge_in,
    load_sem, save_sem, send, recv,
):
    loads, w_query, w_out, w_pair = attention_weights(weights_hbm, weights, load_sem)
    links = Links(send, recv)
    n, width = blocks.shape[1:]
    h = n // 2
    tokens = 2 * n
    rows, heads = kv.shape[1], w_query.shape[0] // HEAD
    bits = rows.bit_length() - 1
    scale = 1.0 / math.sqrt(HEAD)
    blocks[0] = d_second_ref[...].astype(BF16)
    run.enter()
    to_low = links.copy(blocks.at[0], blocks.at[1], COL_LOW)
    to_high = links.copy(blocks.at[0], blocks.at[2], COL_HIGH)
    corner_high = links.copy(blocks.at[1, pl.ds(0, h)], blocks.at[3, pl.ds(0, h)], COL_HIGH)
    corner_low = links.copy(blocks.at[2, pl.ds(h, h)], blocks.at[3, pl.ds(h, h)], COL_LOW)
    hops = [
        [(slot, filled, links.copy(d_kv_out.at[b, filled], d_kv_in.at[b, filled], ("row", 1 << bit)))
         for slot, filled, bit in reversed(row_hops(bits))]
        for b in range(2)
    ]
    share = [links.copy(share_out.at[b], share_in.at[b], COL_LOW) for b in range(2)]
    corner_b, corner_a, edge_a, edge_b = scatter_copies(
        links, corner_out, corner_in, edge_out, edge_in, COL_LOW, COL_HIGH
    )

    def unmix(k):
        d_mixed[pl.ds(k * n, n)] = dot(blocks[k], w_out[...], 1, 1).astype(BF16)

    def attend(b):
        keys = kv[b, :, :, :HEAD].reshape(rows * tokens, HEAD)
        values = kv[b, :, :, HEAD:].reshape(rows * tokens, HEAD)
        at = pl.ds(b * tokens, tokens)
        bias[...] = seen(start_ref, own_ref, key_ref, b)
        for head in range(heads):
            lanes = slice(head * HEAD, (head + 1) * HEAD)
            q = query[at, lanes]
            d_o = d_mixed[at, lanes]
            scores = dot(keys, q, 1, 1) * scale + bias[...]
            probs = jnp.exp(scores - lse_ref[b, pl.ds(head, 1)])
            d_probs = dot(values, d_o, 1, 1)
            delta = jnp.sum(d_probs * probs, axis=0, keepdims=True)
            d_scores = (probs * (d_probs - delta)).astype(BF16)
            d_keys = dot(d_scores, q, 1, 0) * scale
            d_values = dot(probs.astype(BF16), d_o, 1, 0)
            d_keys = d_keys.reshape(rows, tokens, HEAD)
            d_values = d_values.reshape(rows, tokens, HEAD)
            if head:
                d_keys = d_keys + d_kv[b, :, :, :HEAD]
                d_values = d_values + d_kv[b, :, :, HEAD:]
            d_kv[b, :, :, :HEAD] = d_keys
            d_kv[b, :, :, HEAD:] = d_values
            turned = dot(d_scores, keys, 0, 0) * scale
            d_query[at, lanes] = turn(turned, cos_ref[at], -sin_ref[at]).astype(BF16)

    def send_bit(b, step):
        for slot, filled, copy in hops[b]:
            if filled - slot == step:
                d_kv_out[b, filled] = d_kv[b, filled].astype(BF16)
                copy.start()

    def add_bit(b, step):
        for slot, filled, copy in hops[b]:
            if filled - slot == step:
                copy.wait_recv()
                d_kv[b, slot] = d_kv[b, slot] + d_kv_in[b, filled].astype(F32)

    def share_pair(b):
        share_out[b] = d_kv[b, 0, n:].astype(BF16)
        share[b].start()

    def finish_pair(b):
        share[b].wait_recv()
        total = d_kv[b, 0, :n] + share_in[b].astype(F32)
        at = pl.ds(b * tokens, n)
        d_pair[pl.ds(b * n, n), :HEAD] = turn(total[:, :HEAD], cos_ref[at], -sin_ref[at]).astype(BF16)
        d_pair[pl.ds(b * n, n), HEAD:] = total[:, HEAD:].astype(BF16)

    def unproject(k):
        for lane, size in width_tiles(width):
            value = dot(d_query[pl.ds(k * n, n)], w_query[:, pl.ds(lane, size)], 1, 0)
            if k % 2 == 0:
                value = value + dot(
                    d_pair[pl.ds(k // 2 * n, n)], w_pair[:, pl.ds(lane, size)], 1, 0
                )
            partial[k, :, pl.ds(lane, size)] = value

    moves = run.moves
    to_low.start()
    to_high.start()
    for move in moves[:1]:
        move.advance()
    for copy in loads:
        copy.wait()
    unmix(0)
    to_low.wait_recv()
    corner_high.start()
    to_high.wait_recv()
    corner_low.start()
    for move in moves[1:2]:
        move.advance()
    unmix(1)
    unmix(2)
    corner_high.wait_recv()
    corner_low.wait_recv()
    unmix(3)
    saves = []
    save(saves, save_sem, (blocks,), (blocks_hbm,))
    attend(1)
    send_bit(1, 1)
    unproject(3)
    corner_out[...] = partial[3].astype(BF16).reshape(corner_out.shape)
    corner_b.start()
    corner_a.start()
    for move in moves[:1]:
        move.advance()
    attend(0)
    send_bit(0, 1)
    for bit in range(1, bits):
        for b in (1, 0):
            add_bit(b, 1 << (bit - 1))
            send_bit(b, 1 << bit)
    unproject(1)
    corner_b.wait_recv()
    edge_out[0, :h] = (partial[1, :h] + corner_in[0].astype(F32)).astype(BF16)
    edge_out[0, h:] = partial[1, h:].astype(BF16)
    edge_a.start()
    for b in (1, 0):
        add_bit(b, 1 << (bits - 1))
        share_pair(b)
    finish_pair(1)
    unproject(2)
    corner_a.wait_recv()
    edge_out[1, :h] = partial[2, :h].astype(BF16)
    edge_out[1, h:] = (partial[2, h:] + corner_in[1].astype(F32)).astype(BF16)
    edge_b.start()
    for move in moves[2:]:
        move.advance()
    for move in moves[:2]:
        move.advance()
    finish_pair(0)
    unproject(0)
    d_bias_query_ref[...] = jnp.sum(d_query[...].astype(F32), axis=0, keepdims=True)
    d_bias_pair_ref[...] = jnp.sum(d_pair[...].astype(F32), axis=0, keepdims=True)
    edge_a.wait_recv()
    edge_b.wait_recv()
    d_normed = partial[0] + edge_in[0].astype(F32) + edge_in[1].astype(F32)
    stream = entry_ref[...].astype(F32)
    inverse = lax.rsqrt(jnp.mean(stream * stream, axis=-1, keepdims=True) + EPS)
    d_first, d_gain = norm_backward(stream, inverse, gain_ref[...], d_normed)
    d_gain_ref[...] = d_gain
    d_entry_ref[...] = (d_second_ref[...] + d_first).astype(BF16)
    while any(move.at < len(move.steps) for move in moves):
        for move in moves:
            move.advance()
    copies = [to_low, to_high, corner_high, corner_low, corner_a, corner_b, edge_a, edge_b, *share]
    wait_all([], copies + [copy for group in hops for _, _, copy in group])
    for copy in saves:
        copy.wait()


def scatter_scratch(n, width):
    return [
        pltpu.VMEM((4, n, width), F32),
        pltpu.VMEM((2, n // 2, width), BF16),
        pltpu.VMEM((2, n // 2, width), BF16),
        pltpu.VMEM((2, n, width), BF16),
        pltpu.VMEM((2, n, width), BF16),
    ]


def attention_ways(rows):
    return [COL_LOW, COL_HIGH] + [("row", 1 << bit) for bit in range(rows.bit_length() - 1)]


def attention_forward(gathers, collective_id, entry, vectors, tables, weights, after, sizes, moves):
    n, width, rows, _ = sizes
    tokens = 2 * n
    weights = loadable(weights)
    count = 2 * weights.shape[2]
    heads_width = (count - 2 * HEAD) // 2
    heads = heads_width // HEAD
    copies = 8 + 2 * (rows - 1)
    return kernel_call(
        functools.partial(attention_forward_kernel, gathers),
        collective_id,
        attention_ways(rows),
        [(array, True) for array in (entry, *vectors, *tables)] + [(weights, False)],
        after,
        [
            ((n, width), F32, True),
            ((4 * n, width), BF16, True),
            ((4 * n, heads_width), BF16, True),
            ((4 * n, heads_width), BF16, True),
            ((2, heads, tokens), F32, True),
            ((2, rows, tokens, 2 * HEAD), BF16, False),
            ((4, n, width), BF16, False),
        ],
        [
            pltpu.VMEM((count, width), BF16),
            pltpu.VMEM((4, n, width), BF16),
            pltpu.VMEM((2, rows, tokens, 2 * HEAD), BF16),
            pltpu.VMEM((rows * tokens, tokens), F32),
            *scatter_scratch(n, width),
            pltpu.SemaphoreType.DMA((2 * weights.shape[1],)),
            pltpu.SemaphoreType.DMA((4,)),
            pltpu.SemaphoreType.DMA((copies,)),
            pltpu.SemaphoreType.DMA((copies,)),
        ],
        4 * 2 * n * width * 5 * heads_width // 2,
        moves,
    )


def attention_backward(collective_id, operands, weights, after, sizes, moves):
    n, width, rows, _ = sizes
    tokens = 2 * n
    weights = loadable(weights)
    count = 2 * weights.shape[2]
    heads_width = (count - 2 * HEAD) // 2
    copies = 10 + 2 * (rows - 1)
    return kernel_call(
        attention_backward_kernel,
        collective_id,
        attention_ways(rows),
        [(array, True) for array in operands] + [(weights, False)],
        after,
        [
            ((n, width), BF16, True),
            ((1, width), F32, True),
            ((4 * n, heads_width), BF16, True),
            ((2 * n, 2 * HEAD), BF16, True),
            ((1, heads_width), F32, True),
            ((1, 2 * HEAD), F32, True),
            ((4, n, width), BF16, False),
        ],
        [
            pltpu.VMEM((count, width), BF16),
            pltpu.VMEM((4, n, width), BF16),
            pltpu.VMEM((4 * n, heads_width), BF16),
            pltpu.VMEM((rows * tokens, tokens), F32),
            pltpu.VMEM((2, rows, tokens, 2 * HEAD), F32),
            pltpu.VMEM((2, rows, tokens, 2 * HEAD), BF16),
            pltpu.VMEM((2, rows, tokens, 2 * HEAD), BF16),
            pltpu.VMEM((2, n, 2 * HEAD), BF16),
            pltpu.VMEM((2, n, 2 * HEAD), BF16),
            *scatter_scratch(n, width),
            pltpu.SemaphoreType.DMA((2 * weights.shape[1],)),
            pltpu.SemaphoreType.DMA((4,)),
            pltpu.SemaphoreType.DMA((copies,)),
            pltpu.SemaphoreType.DMA((copies,)),
        ],
        4 * 2 * n * width * 5 * heads_width // 2,
        moves,
    )


def sum_kernel(ways, run, value_ref, total_ref, outgoing, incoming, send, recv):
    run.enter()
    links = Links(send, recv)
    total = value_ref[...]
    copies = []
    for i, way in enumerate(ways):
        outgoing[i] = total
        copies.append(links.copy(outgoing.at[i], incoming.at[i], way))
        copies[-1].start()
        copies[-1].wait_recv()
        total = total + incoming[i]
        for move in run.moves:
            move.advance()
    total_ref[...] = total
    for move in run.moves:
        move.end()
    wait_all([], copies)


def sum_all(value, collective_id, moves):
    ways = [SECTION, COL_LOW, COL_HIGH] + [("row", 1 << bit) for bit in range(row_bits())]
    buffers = [pltpu.VMEM((len(ways), *value.shape), F32) for _ in range(2)]
    return kernel_call(
        functools.partial(sum_kernel, ways),
        collective_id,
        ways,
        [(value, True)],
        (),
        [(value.shape, F32, True)],
        buffers + semaphores(len(ways), len(ways)),
        1 << 20,
        moves,
    )


def exchange_halves(parts, section):
    return pick(parts, section), swap(pick(parts, 1 - section), *SECTION)


def of_layer(layer, parts, section, token):
    own, other = parts
    return jnp.where(section + token == layer, own, other)


def to_owner(first, second, section):
    keep = jnp.where(section == 0, first, second)
    away = jnp.where(section == 0, second, first)
    other = swap(away, *SECTION)
    return jnp.where(section == 0, keep, other), jnp.where(section == 0, other, keep)


def local(
    tokens,
    cotangent,
    lengths,
    norm_attn,
    w_query,
    b_query,
    w_keyval,
    b_keyval,
    w_out,
    norm_ffn,
    w_gate,
    w_up,
    w_down,
):
    section = lax.axis_index("section")
    row = lax.axis_index("row")
    col = lax.axis_index("col")
    rows = lax.axis_size("row")
    cols = lax.axis_size("col")
    low, high = bit_of(col, 0), bit_of(col, 1)
    place = (section, row, low, high)
    row_count = tokens.shape[1]
    width = tokens.shape[2]
    half = row_count // 2
    depth = w_query.shape[1]
    heads_width = w_query.shape[2]

    def blocks_of(array):
        return jnp.concatenate(
            [
                lax.dynamic_slice(
                    array, (2 * section + (high ^ j), (low ^ k) * half, 0), (1, half, width)
                )
                for j in range(2)
                for k in range(2)
            ]
        )

    small = jnp.concatenate([norm_attn[0], norm_ffn[0], b_keyval[0], b_query[0]])
    small = (small, swap(small, *SECTION))
    small = [of_layer(layer, small, section, 0).astype(F32) for layer in range(2)]

    pair_cols = w_keyval[0].reshape(-1, 2, KV, HEAD)
    mine = pick(pair_cols, high, 2).reshape(-1, 2 * HEAD)
    away = pick(pair_cols, 1 - high, 2).reshape(-1, 2 * HEAD)
    pair_rows = ordered(mine[None, None], swap(away, *COL_HIGH)[None, None], high, 0)
    pair_rows = ordered(pair_rows, swap(pair_rows, *COL_LOW), low, 1)
    pair_rows = pair_rows.reshape(depth, 2 * HEAD)
    attn_own = jnp.concatenate([w_query[0].T, w_out[0], pair_rows.T])
    attn_halves = exchange_halves(attn_own.reshape(2, -1, depth), section)

    def ffn_parts(shard):
        hidden = shard.shape[0]
        parts = shard.reshape(2, 2, hidden // 4, shard.shape[1]).transpose(1, 0, 2, 3)
        return exchange_halves(parts, section)

    parts = [ffn_parts(shard) for shard in (w_gate[0].T, w_up[0].T, w_down[0])]
    ways = [(COL_LOW, COL_HIGH), (COL_HIGH, COL_LOW)]

    hidden = w_gate.shape[2] // 2

    tables = layout(lengths, place, row_count)
    sizes = (half, width, rows, hidden)
    entry = blocks_of(tokens)
    saved = []

    def vectors_of(layer):
        gain_attn = small[layer][None, :width]
        gain_ffn = small[layer][None, width : 2 * width]
        bias_pair = small[layer][2 * width : 2 * width + 2 * KV * HEAD].reshape(2, KV, HEAD)
        bias_pair = pick(bias_pair, high, 1).reshape(1, -1)
        bias_query = small[layer][None, 2 * width + 2 * KV * HEAD :]
        return gain_attn, gain_ffn, bias_query, bias_pair

    def attend(layer, entry, weights, moves):
        gain_attn, _, bias_query, bias_pair = vectors_of(layer)
        return attention_forward(
            layer > 0, 4 + layer, entry, (gain_attn, bias_query, bias_pair), tables, weights, (), sizes, moves
        )

    def feed(layer, second, weights, moves):
        return ffn_call(
            ffn_forward_kernel,
            ways[layer][0],
            ROW_LOW,
            layer,
            (second, vectors_of(layer)[1]),
            (),
            weights,
            (),
            sizes,
            [(half, width)],
            3,
            moves,
        )

    def ffn_gather(layer, kind):
        return FfnGather(of_layer(layer, parts[kind], section, 0), ways[layer][1])

    _, _, ((attn_zero,),) = kernel_call(
        move_kernel, 9, (), (), (), (), (), 0, [AttnGather(of_layer(0, attn_halves, section, 0))]
    )
    _, (second, *kept, _), weights_zero = attend(
        0, entry, attn_zero, [ffn_gather(0, kind) for kind in range(3)]
    )
    _, (result, *kept_ffn), ((attn_one,), *weights_one) = feed(
        0, second, weights_zero, [AttnGather(of_layer(1, attn_halves, section, 0)), ffn_gather(1, 0)]
    )
    saved.append((entry[0], attn_zero, weights_zero, second, kept, kept_ffn))
    _, (second, *kept, first_result), more_weights = attend(
        1, result, attn_one, [ffn_gather(1, kind) for kind in (1, 2)]
    )
    weights_one += more_weights
    entry = result.astype(BF16)
    grad_own = lax.dynamic_slice(
        cotangent, (2 * section + high, low * half, 0), (1, half, width)
    )[0]
    _, (result, *kept_ffn), ((grad_all,),) = feed(
        1, second, weights_one, [TokenGather(grad_own, ways[1][0], ROW_LOW, True)]
    )
    saved.append((entry, attn_one, weights_one, second, kept, kept_ffn))
    last_result = result.astype(BF16)

    unit = hidden // 2

    def grad_of(left, right):
        return dot(left, right.reshape(-1, width), 0, 0).astype(BF16)

    def blocked(grad, arrived):
        total = (grad[:unit].astype(F32) + arrived.astype(F32)).astype(BF16)
        return jnp.stack([total[:, i * depth : (i + 1) * depth] for i in range(rows)])

    def feed_back(layer, grad_own, gathered, after, moves):
        _, _, weights, second, _, (normed_two, gate, up, act) = saved[layer]
        return ffn_call(
            functools.partial(ffn_backward_kernel, gathered is None),
            ways[layer][0],
            ROW_LOW,
            2 + layer,
            (grad_own, second, vectors_of(layer)[1]),
            (gate, up) if gathered is None else (gate, up, gathered),
            weights,
            after,
            sizes,
            [(half, width), (1, width)],
            2,
            moves,
        )

    def attend_back(layer, d_second, after, moves):
        own, weights, _, _, (normed, query, mixed, lse, kv), _ = saved[layer]
        _, outs, moved = attention_backward(
            6 + layer,
            (d_second, own, vectors_of(layer)[0], *tables, query, kv, lse),
            weights,
            after,
            sizes,
            moves,
        )
        d_own, d_gain, d_query, d_pair, d_bias_query, d_bias_pair, d_attn = outs
        normed_own = normed.reshape(2, 2, half, width)[:, 0].reshape(-1, width)
        grads = jnp.concatenate(
            [grad_of(d_query, normed), grad_of(mixed, d_attn), grad_of(d_pair, normed_own)]
        )
        return d_own, grads, (d_gain[0], d_bias_query[0], d_bias_pair[0]), moved

    normed_two, _, _, act = saved[1][5]
    down_one = grad_of(act, grad_all)
    _, (d_second, d_gain_one, _, d_gate, d_up), ((down_across,),) = feed_back(
        1, grad_own, grad_all, (), [Across(down_one, unit, ways[1][1])]
    )
    gate_one, up_one = grad_of(d_gate, normed_two), grad_of(d_up, normed_two)
    down_one = blocked(down_one, down_across)
    grad_one, attn_grad_one, small_one, ((down_rows,), (gate_across,), (up_across,)) = attend_back(
        1,
        d_second,
        (),
        [Rows(down_one), Across(gate_one, unit, ways[1][1]), Across(up_one, unit, ways[1][1])],
    )
    gate_one, up_one = blocked(gate_one, gate_across), blocked(up_one, up_across)
    normed_two, _, _, act = saved[0][5]
    _, (d_second, d_gain_zero, grad_all, d_gate, d_up), ((gate_rows,), (last_blocks,), (grad_one_blocks,)) = feed_back(
        0,
        grad_one,
        None,
        (attn_grad_one, up_one),
        [
            Rows(gate_one),
            TokenGather(last_result, COL_LOW, COL_HIGH, False),
            TokenGather(grad_one, COL_LOW, COL_HIGH, False),
        ],
    )
    zero_grads = [grad_of(act, grad_all), grad_of(d_gate, normed_two), grad_of(d_up, normed_two)]
    grad_zero, attn_grad_zero, small_zero, moved = attend_back(
        0,
        d_second,
        (),
        [Rows(up_one)] + [GradScatter(grad, unit, ways[0][1]) for grad in zero_grads] + [AttnScatter(attn_grad_one)],
    )
    (up_rows,), *scattered, (attn_one_half,) = moved
    near_far_zero = [scattered[i] for i in (1, 2, 0)]
    near_far_one = [(pick(total, row), arrived) for total, arrived in ((gate_one, gate_rows), (up_one, up_rows), (down_one, down_rows))]

    def by_row_bit(own, arrived):
        near, far = own.astype(F32), 0.0
        for flip in range(1, rows):
            if flip & 1:
                far = far + arrived[flip].astype(F32)
            else:
                near = near + arrived[flip].astype(F32)
        return ordered(near.astype(BF16)[None], far.astype(BF16)[None], row & 1, 0)

    ffn_grads = [[by_row_bit(*pair) for pair in pairs] for pairs in (near_far_zero, near_far_one)]

    vectors = []
    for (d_gain, d_bias_query, d_bias_pair), d_gain_two in ((small_zero, d_gain_zero), (small_one, d_gain_one)):
        spread_query = jnp.where(
            (jnp.arange(cols) == col)[:, None], d_bias_query[None], 0.0
        ).reshape(-1)
        spread_pair = jnp.where(
            (jnp.arange(2) == high)[None, :, None],
            d_bias_pair.reshape(2, 1, HEAD),
            0.0,
        ).reshape(-1)
        vectors.append(jnp.concatenate([d_gain, d_gain_two[0], spread_query, spread_pair]))
    _, (sums,), ((attn_zero_half,), (grad_zero_blocks,)) = sum_all(
        jnp.stack(vectors).reshape(-1, 128),
        8,
        [AttnScatter(attn_grad_zero), TokenGather(grad_zero, COL_LOW, COL_HIGH, False)],
    )
    sums = sums.reshape(2, -1)
    sums = jnp.where(section == 0, sums[0], sums[1])
    grad_norm_attn = sums[:width]
    grad_norm_ffn = sums[width : 2 * width]
    spread = sums[2 * width : 2 * width + cols * heads_width].reshape(cols, -1)
    grad_b_query = pick(spread, col)
    grad_b_keyval = sums[2 * width + cols * heads_width :]

    def assemble(first, second):
        def placed(blocks):
            blocks = blocks.reshape(2, 2, half, width)
            blocks = jnp.where(high == 0, blocks, blocks[::-1])
            blocks = jnp.where(low == 0, blocks, blocks[:, ::-1])
            return blocks.reshape(2, row_count, width)

        zeroth, later = to_owner(placed(first), placed(second), section)
        return jnp.concatenate([zeroth, later])[None]

    outputs = assemble(first_result, last_blocks)
    grads_in = assemble(grad_zero_blocks, grad_one_blocks)

    def ffn_grad(kind):
        zeroth, later = to_owner(ffn_grads[0][kind], ffn_grads[1][kind], section)
        whole = jnp.stack([zeroth, later], axis=1)
        return whole.reshape(-1, whole.shape[-1])

    grad_gate = ffn_grad(0).T.astype(F32)
    grad_up = ffn_grad(1).T.astype(F32)
    grad_down = ffn_grad(2).astype(F32)

    total = jnp.concatenate(to_owner(attn_zero_half, attn_one_half, section)).astype(F32)
    grad_query = total[:heads_width].T
    grad_out = total[heads_width : 2 * heads_width]
    pair = total[2 * heads_width :].T.reshape(2, 2, depth // 4, 2 * HEAD)
    pair = pick(pair, low, 1) + swap(pick(pair, 1 - low, 1).astype(BF16), *COL_LOW).astype(F32)
    pair = pair.astype(BF16)
    pair = ordered(
        pick(pair, high)[:, None], swap(pick(pair, 1 - high), *COL_HIGH)[:, None], high, 1
    )
    grad_keyval = (
        pair.reshape(-1, 2, 2, HEAD).transpose(0, 2, 1, 3).reshape(-1, 2 * KV * HEAD).astype(F32)
    )

    return (
        outputs,
        grads_in,
        grad_norm_attn[None],
        grad_query[None],
        grad_b_query[None],
        grad_keyval[None],
        grad_b_keyval[None],
        grad_out[None],
        grad_norm_ffn[None],
        grad_gate[None],
        grad_up[None],
        grad_down[None],
    )


def solution(mesh):
    in_specs = (
        P(None, "row", None),
        P(None, "row", None),
        P(),
        P("section", None),
        P("section", "row", "col"),
        P("section", "col"),
        P("section", ("row", "col"), None),
        P("section", None),
        P("section", "col", "row"),
        P("section", None),
        P("section", "row", "col"),
        P("section", "row", "col"),
        P("section", "col", "row"),
    )
    out_specs = (
        P("section", None, "row", None),
        P("section", None, "row", None),
        P("section", None),
        P("section", "row", "col"),
        P("section", "col"),
        P("section", ("row", "col"), None),
        P("section", None),
        P("section", "col", "row"),
        P("section", None),
        P("section", "row", "col"),
        P("section", "row", "col"),
        P("section", "col", "row"),
    )
    return jax.shard_map(local, mesh=mesh, in_specs=in_specs, out_specs=out_specs, check_vma=False)
```

```python
import functools
import math

import jax
import jax.numpy as jnp
from jax import lax
from jax.experimental import pallas as pl
from jax.experimental.pallas import tpu as pltpu
from jax.sharding import PartitionSpec as P

HEADS = 12
KV = 2
HEAD = 128

EPS = 1e-06
THETA = 1000000.0

ROW, SEC, COL = "row", "section", "col"

F32 = jnp.float32
BF16 = jnp.bfloat16

COL_LOW = (COL, 1)
COL_HIGH = (COL, 2)
ROW_LOW = (ROW, 1)
SECTION = (SEC, 1)


def swap(value, axis, flip):
    pairs = [(i, i ^ flip) for i in range(lax.axis_size(axis))]
    return lax.ppermute(value, axis, pairs)


def bit_of(index, bit):
    return (index >> bit) & 1


def pick(array, index, axis=0):
    return lax.dynamic_index_in_dim(array, index, axis, keepdims=False)


def ordered(mine, other, bit, axis):
    first = jnp.where(bit == 0, mine, other)
    second = jnp.where(bit == 0, other, mine)
    return jnp.concatenate([first, second], axis=axis)


def row_bits():
    return lax.axis_size(ROW).bit_length() - 1


def norm_backward(stream, inverse, gain, gradient):
    inner = jnp.mean(gradient * gain * stream, axis=-1, keepdims=True)
    d_stream = gain * gradient * inverse - stream * (inverse * inverse * inverse) * inner
    return (d_stream, jnp.sum(gradient * stream * inverse, axis=0, keepdims=True))


def dot(left, right, left_dim, right_dim):
    return lax.dot_general(
        left, right, (((left_dim,), (right_dim,)), ((), ())), preferred_element_type=F32
    )


def layout(lengths, place, row_count):
    section, row, low, high = place
    rows = lax.axis_size(ROW)
    half = row_count // 2
    inside = jnp.arange(row_count, dtype=jnp.int32)
    inside = (((inside // half) ^ low) * half) + inside % half
    own_index = row * row_count + inside
    key_index = ((jnp.arange(rows, dtype=jnp.int32) ^ row) * row_count)[:, None] + inside[None, :]
    slots = 2 * section + (jnp.arange(2, dtype=jnp.int32) ^ high)
    picked = jnp.stack([pick(lengths, slots[0]), pick(lengths, slots[1])])
    ends = jnp.cumsum(picked, axis=1)
    starts = ends - picked
    inside_piece = (own_index[None, None, :] >= starts[:, :, None]) & (
        own_index[None, None, :] < ends[:, :, None]
    )
    first = jnp.sum(jnp.where(inside_piece, starts[:, :, None], 0), axis=1)
    inverse = THETA ** (-(jnp.arange(HEAD // 2, dtype=F32) * 2.0 / HEAD))
    angle = (own_index[None, :] - first).astype(F32).reshape(-1, 1) * inverse
    cosine, sine = jnp.cos(angle), jnp.sin(angle)
    return (
        jnp.concatenate([cosine, cosine], axis=1),
        jnp.concatenate([-sine, sine], axis=1),
        first,
        own_index[None, :],
        key_index.reshape(-1, 1),
    )


MESH = pl.DeviceIdType.MESH
VMEM_LIMIT = 62 * 1024 * 1024


def partner_of(way):
    axis, flip = way
    return {axis: lax.axis_index(axis) ^ flip}


def enter(ways):
    barrier = pltpu.get_barrier_semaphore()
    for way in ways:
        pl.semaphore_signal(barrier, inc=1, device_id=partner_of(way), device_id_type=MESH)
    pl.semaphore_wait(barrier, len(ways))


def remote(source, target, send, recv, way):
    return pltpu.make_async_remote_copy(
        src_ref=source,
        dst_ref=target,
        send_sem=send,
        recv_sem=recv,
        device_id=partner_of(way),
        device_id_type=MESH,
    )


class Links:
    def __init__(self, sems):
        self.send, self.recv = sems
        self.used = 0

    def copy(self, source, target, way):
        slot = self.used
        self.used += 1
        return remote(source, target, self.send.at[slot], self.recv.at[slot], way)


def semaphores(*counts):
    return [pltpu.SemaphoreType.DMA((count,)) for count in counts]


def wait_all(arriving, leaving):
    for copy in arriving:
        copy.wait_recv()
    for copy in leaving:
        copy.wait_send()


class Refs:
    def __init__(self, named, layer=None):
        self.named, self.layer = named, layer

    def __getattr__(self, name):
        return self.named[name] if name in self.named else self.named[name + str(self.layer)]

    def of(self, layer):
        return Refs(self.named, layer)


def layered(layer, **values):
    return {name + str(layer): value for name, value in values.items()}


class Pump:
    def __init__(self, schedule, number=None):
        self.schedule, self.number = schedule, number

    def __call__(self, number):
        return Pump(self.schedule, number)

    def __getattr__(self, point):
        def run():
            for move in self.schedule.get(point[0] + str(self.number) + point[1:], ()):
                move.advance()

        return run


def kernel_call(kernel, collective_id, ways, operands, outs, scratch, flops, moves, schedule):
    vmem = pl.BlockSpec(memory_space=pltpu.VMEM)
    hbm = pl.BlockSpec(memory_space=pl.ANY)
    moved_in = [array for move in moves for array in move.operands]
    moved_out = [out for move in moves for out in move.outs]
    every = list(ways)
    for move in moves:
        every += [way for way in move.ways if way not in every]
    scratch_list = []
    for spec in scratch.values():
        scratch_list += spec if isinstance(spec, list) else [spec]

    def body(*refs):
        refs = list(refs)

        def take(count):
            taken, refs[:] = refs[:count], refs[count:]
            return taken

        named = dict(zip(operands, take(len(operands))))
        sources = [take(len(move.operands)) for move in moves]
        named.update(zip(outs, take(len(outs))))
        targets = [take(len(move.outs)) for move in moves]
        for name, spec in scratch.items():
            named[name] = take(len(spec)) if isinstance(spec, list) else take(1)[0]
        for move, source, target in zip(moves, sources, targets, strict=True):
            if move.name:
                source = [named[move.name]]
            move.bind(source, target, take(len(move.scratch)))

        enter(every)
        kernel(Refs(named), Pump(schedule))
        while any(move.at < len(move.steps) for move in moves):
            for move in moves:
                move.advance()

    results = pl.pallas_call(
        body,
        out_shape=[jax.ShapeDtypeStruct(shape, dtype) for shape, dtype, _ in outs.values()]
        + [jax.ShapeDtypeStruct(shape, BF16) for shape in moved_out],
        in_specs=[vmem if inside else hbm for _, inside in operands.values()] + [hbm] * len(moved_in),
        out_specs=[vmem if inside else hbm for _, _, inside in outs.values()] + [hbm] * len(moved_out),
        scratch_shapes=scratch_list + [ref for move in moves for ref in move.scratch],
        compiler_params=pltpu.CompilerParams(
            collective_id=collective_id, has_side_effects=True, vmem_limit_bytes=VMEM_LIMIT
        ),
        cost_estimate=pl.CostEstimate(flops=flops, bytes_accessed=32 << 20, transcendentals=1 << 20),
    )(*[array for array, _ in operands.values()], *moved_in)
    moved = results[len(outs) :]
    for move in moves:
        move.results, moved = moved[: len(move.outs)], moved[len(move.outs) :]
    return Refs(dict(zip(outs, results)))


def row_hops(bits):
    hops, known = [], [0]
    for bit in reversed(range(bits)):
        step = 1 << bit
        hops += [(slot, slot | step, bit) for slot in known]
        known += [slot | step for slot in known]
    return hops


class Move:
    def __init__(self, source, outs, scratch, ways):
        self.name = source if isinstance(source, str) else None
        self.operands = [] if self.name else [source]
        self.outs, self.scratch, self.ways = outs, scratch, ways
        self.steps, self.at = [], 0

    def advance(self):
        if self.at < len(self.steps):
            self.steps[self.at]()
            self.at += 1


class FfnGather(Move):
    def __init__(self, part, across):
        rows = lax.axis_size(ROW)
        self.flips, self.across = list(range(rows - 1, 0, -1)), across
        outs = [(rows, *part.shape[1:])] * 2
        ways = [(ROW, flip) for flip in self.flips] + [across]
        super().__init__(part, outs, semaphores(rows, rows, rows, rows, 1), ways)

    def bind(self, sources, targets, scratch):
        (part,), (own, other) = sources, targets
        self.blocks = [own, other]
        row_send, row_recv, far_send, far_recv, local_sem = scratch
        row = lax.axis_index(ROW)
        near = part.at[row & 1]
        local = pltpu.make_async_copy(near, own.at[row], local_sem.at[0])
        hops = {
            flip: remote(
                part.at[(row ^ flip) & 1], own.at[row], row_send.at[flip], row_recv.at[flip], (ROW, flip)
            )
            for flip in self.flips
        }
        far = {
            flip: remote(
                own.at[row ^ flip] if flip else near,
                other.at[row ^ flip],
                far_send.at[flip],
                far_recv.at[flip],
                self.across,
            )
            for flip in [0] + self.flips
        }

        def start():
            local.start()
            hops[self.flips[0]].start()

        def start_rest():
            for flip in self.flips[1:]:
                hops[flip].start()

        def forward(flip):
            def step():
                if flip:
                    hops[flip].wait_recv()
                far[flip].start()

            return step

        def finish():
            local.wait()
            wait_all(far.values(), [*hops.values(), *far.values()])

        self.steps = [start, start_rest, *[forward(flip) for flip in [0] + self.flips], finish]


class AttnGather(Move):
    def __init__(self, part):
        rows = lax.axis_size(ROW)
        self.bits = rows.bit_length() - 1
        ways = [(ROW, 1 << bit) for bit in range(self.bits)] + [SECTION]
        super().__init__(part, [(2, rows, *part.shape)], semaphores(rows, rows, rows, rows, 1), ways)

    def bind(self, sources, targets, scratch):
        (part,), (blocks,) = sources, targets
        self.blocks = [blocks.at[0], blocks.at[1]]
        row_send, row_recv, side_send, side_recv, local_sem = scratch
        section, row = lax.axis_index(SEC), lax.axis_index(ROW)

        def place(slot):
            return blocks.at[section, row ^ slot]

        def source(slot):
            return place(slot) if slot else part

        local = pltpu.make_async_copy(part, place(0), local_sem.at[0])
        hops = [
            (slot, filled, remote(source(slot), place(slot), row_send.at[filled], row_recv.at[filled], (ROW, 1 << bit)))
            for slot, filled, bit in row_hops(self.bits)
        ]
        sides = [
            remote(source(slot), place(slot), side_send.at[slot], side_recv.at[slot], SECTION)
            for slot in range(1 << self.bits)
        ]
        arrived = {0}

        def arrive(slot):
            if slot not in arrived:
                arrived.add(slot)
                for _, filled, copy in hops:
                    if filled == slot:
                        copy.wait_recv()
                sides[slot].start()

        def start():
            local.start()
            for slot, _, copy in hops:
                if slot == 0:
                    copy.start()
            sides[0].start()

        def forward():
            for slot, _, copy in hops:
                if slot:
                    arrive(slot)
                    copy.start()

        def finish():
            for slot in range(len(sides)):
                arrive(slot)
            local.wait()
            wait_all(sides, [copy for _, _, copy in hops] + sides)

        self.steps = [start, forward, finish]


class TokenGather(Move):
    def __init__(self, own, shape, a, b, sides):
        self.a, self.b, self.sides = a, b, sides
        ways = [a, b] + ([SECTION] if sides else [])
        super().__init__(own, [(4, 1 + sides, *shape)], semaphores(8, 8, 1), ways)

    def bind(self, sources, targets, scratch):
        (own,), (blocks,) = sources, targets
        send, recv, local_sem = scratch
        local = pltpu.make_async_copy(own, blocks.at[0, 0], local_sem.at[0])
        gather = BlockGather(Links((send, recv)), blocks, self.a, self.b, self.sides, own)

        def start():
            local.start()
            for copy in (gather.a, gather.b, gather.sides[0]):
                copy.start()

        def forward():
            gather.a.wait_recv()
            gather.ab.start()
            gather.sides[1].start()
            gather.b.wait_recv()
            gather.ba.start()
            gather.sides[2].start()

        def last():
            gather.ab.wait_recv()
            gather.ba.wait_recv()
            gather.sides[3].start()

        def finish():
            local.wait()
            wait_all(gather.sides, gather.copies)

        self.steps = [start, forward, last, finish]


class Across(Move):
    def __init__(self, grad, n, way):
        self.n, self.way = n, way
        super().__init__(grad, [(n, grad.shape[1])], semaphores(1, 1), [way])

    def bind(self, sources, targets, scratch):
        (grad,), (arrived,) = sources, targets
        send, recv = scratch
        copy = remote(grad.at[pl.ds(self.n, self.n)], arrived, send.at[0], recv.at[0], self.way)
        self.steps = [copy.start, lambda: wait_all([copy], [copy])]


class Rows(Move):
    def __init__(self, total):
        rows = total.shape[0]
        self.flips = list(range(1, rows))
        ways = [(ROW, flip) for flip in self.flips]
        super().__init__(total, [total.shape], semaphores(rows, rows), ways)

    def bind(self, sources, targets, scratch):
        (total,), (arrived,) = sources, targets
        send, recv = scratch
        copies = row_copies(total, arrived, send, recv, self.flips)

        def start():
            for copy in copies:
                copy.start()

        self.steps = [start, lambda: wait_all(copies, copies)]


def row_copies(total, arrived, send, recv, flips):
    row = lax.axis_index(ROW)
    return [
        remote(total.at[row ^ flip], arrived.at[flip], send.at[flip], recv.at[flip], (ROW, flip))
        for flip in flips
    ]


class GradScatter(Move):
    def __init__(self, grad, n, way):
        rows, width = lax.axis_size(ROW), grad.shape[1]
        self.n, self.way, self.flips = n, way, list(range(1, rows))
        shape = (rows, n, width // rows)
        scratch = [pltpu.VMEM((n, width), BF16), pltpu.VMEM((n, width), BF16), pltpu.VMEM(shape, BF16)]
        scratch += semaphores(1, 1, 1, 1, rows, rows)
        ways = [way] + [(ROW, flip) for flip in self.flips]
        super().__init__(grad, [shape[1:], shape], scratch, ways)

    def bind(self, sources, targets, scratch):
        (grad,), (own, arrived) = sources, targets
        mine, theirs, total, local_sem, own_sem, far_send, far_recv, row_send, row_recv = scratch
        n, row = self.n, lax.axis_index(ROW)
        depth = total.shape[2]
        local = pltpu.make_async_copy(grad.at[pl.ds(0, n)], mine, local_sem.at[0])
        far = remote(grad.at[pl.ds(n, n)], theirs, far_send.at[0], far_recv.at[0], self.way)
        keep = pltpu.make_async_copy(total.at[row], own, own_sem.at[0])
        copies = row_copies(total, arrived, row_send, row_recv, self.flips)

        def start():
            local.start()
            far.start()

        def forward():
            local.wait()
            far.wait_recv()
            for block in range(total.shape[0]):
                at = slice(block * depth, (block + 1) * depth)
                total[block] = (mine[:, at].astype(F32) + theirs[:, at].astype(F32)).astype(BF16)
            for copy in copies + [keep]:
                copy.start()

        def finish():
            keep.wait()
            wait_all(copies, copies + [far])

        self.steps = [start, forward, finish]


class AttnScatter(Move):
    def __init__(self, name, shape):
        rows, width, m = lax.axis_size(ROW), shape[1], shape[0] // 2
        self.bits, self.m = rows.bit_length() - 1, m
        blocks = (rows, m, width // rows)
        scratch = [
            pltpu.VMEM((m, width), BF16),
            pltpu.VMEM(blocks, F32),
            pltpu.VMEM(blocks, BF16),
            pltpu.VMEM(blocks, BF16),
        ]
        scratch += semaphores(1, 1, 1, rows, rows)
        ways = [SECTION] + [(ROW, 1 << bit) for bit in range(self.bits)]
        super().__init__(name, [blocks[1:]], scratch, ways)

    def bind(self, sources, targets, scratch):
        (grad,), (out,) = sources, targets
        theirs, total, going, coming, out_sem, side_send, side_recv, send, recv = scratch
        m, row, section = self.m, lax.axis_index(ROW), lax.axis_index(SEC)
        depth = total.shape[2]
        mine = grad.at[pl.ds(pl.multiple_of(section * m, m), m)]
        side = remote(
            grad.at[pl.ds(pl.multiple_of((1 - section) * m, m), m)],
            theirs,
            side_send.at[0],
            side_recv.at[0],
            SECTION,
        )
        keep = pltpu.make_async_copy(going.at[0], out, out_sem.at[0])
        hops = [
            (slot, filled, remote(going.at[filled], coming.at[filled], send.at[filled], recv.at[filled], (ROW, 1 << bit)))
            for slot, filled, bit in reversed(row_hops(self.bits))
        ]

        def sum_sides():
            side.wait_recv()
            for block in range(total.shape[0]):
                at = slice(block * depth, (block + 1) * depth)
                total[row ^ block] = mine[:, at].astype(F32) + theirs[:, at].astype(F32)
            send_bit(0)

        def send_bit(bit):
            for slot, filled, copy in hops:
                if filled - slot == 1 << bit:
                    going[filled] = total[filled].astype(BF16)
                    copy.start()

        def add_bit(bit):
            for slot, filled, copy in hops:
                if filled - slot == 1 << bit:
                    copy.wait_recv()
                    total[slot] = total[slot] + coming[filled].astype(F32)

        def hop(bit):
            def step():
                add_bit(bit - 1)
                send_bit(bit)

            return step

        def finish():
            add_bit(self.bits - 1)
            going[0] = total[0].astype(BF16)
            keep.start()
            keep.wait()
            wait_all([], [copy for _, _, copy in hops] + [side])

        self.steps = [side.start, sum_sides, *[hop(bit) for bit in range(1, self.bits)], finish]


class NoCopy:
    def start(self):
        pass

    wait_recv = wait_send = start


class BlockGather:
    def __init__(self, links, blocks, a, b, sides=True, own=None, there=False):
        h = blocks.shape[2] // 2
        own = blocks.at[0, 0] if own is None else own
        if there:
            self.a = self.b = self.ab = self.ba = NoCopy()
        else:
            self.a = links.copy(own, blocks.at[1, 0], a)
            self.b = links.copy(own, blocks.at[2, 0], b)
            self.ab = links.copy(blocks.at[1, 0, pl.ds(0, h)], blocks.at[3, 0, pl.ds(0, h)], b)
            self.ba = links.copy(blocks.at[2, 0, pl.ds(h, h)], blocks.at[3, 0, pl.ds(h, h)], a)
        self.sides = [NoCopy()] * 4
        if sides and not there:
            self.sides = [
                links.copy(blocks.at[k, 0] if k else own, blocks.at[k, 1], SECTION) for k in range(4)
            ]
        self.copies = [self.a, self.b, self.ab, self.ba, *self.sides]


class Scatter:
    def __init__(self, links, r, corner_in, edge_in, a, b):
        self.r, self.corner_in, self.edge_in = r, corner_in, edge_in
        self.corner_b = links.copy(r.corner_out.at[0], corner_in.at[0], b)
        self.corner_a = links.copy(r.corner_out.at[1], corner_in.at[1], a)
        self.edge_a = links.copy(r.edge_out.at[0], edge_in.at[0], a)
        self.edge_b = links.copy(r.edge_out.at[1], edge_in.at[1], b)
        self.copies = [self.corner_b, self.corner_a, self.edge_a, self.edge_b]

    def send_corner(self, value):
        corner = self.r.corner_out
        corner[...] = value.astype(BF16).reshape(corner.shape)
        self.corner_b.start()
        self.corner_a.start()

    def send_edge_a(self, value):
        edge, h = self.r.edge_out, value.shape[0] // 2
        self.corner_b.wait_recv()
        edge[0, :h] = (value[:h] + self.corner_in[0].astype(F32)).astype(BF16)
        edge[0, h:] = value[h:].astype(BF16)
        self.edge_a.start()

    def send_edge_b(self, value):
        edge, h = self.r.edge_out, value.shape[0] // 2
        self.corner_a.wait_recv()
        edge[1, :h] = value[:h].astype(BF16)
        edge[1, h:] = (value[h:] + self.corner_in[1].astype(F32)).astype(BF16)
        self.edge_b.start()

    def total(self, value):
        self.edge_a.wait_recv()
        self.edge_b.wait_recv()
        return value + self.edge_in[0].astype(F32) + self.edge_in[1].astype(F32)


def save(started, sems, pairs):
    for source, target in pairs:
        started.append(pltpu.make_async_copy(source, target, sems.at[len(started)]))
        started[-1].start()


class Load:
    def __init__(self, sources, target, stage, sems):
        self.sources, self.target, self.stage, self.copies, self.sems = sources, target, stage, [], sems
        if stage is None:
            for i, source in enumerate(sources):
                blocks, rows, columns = source.shape
                for block in range(blocks):
                    place = target.at[pl.ds(i * rows, rows), pl.ds(block * columns, columns)]
                    self.copies.append(
                        pltpu.make_async_copy(source.at[block], place, sems.at[len(self.copies)])
                    )

    def start(self):
        for copy in self.copies:
            copy.start()
        filled = sum(source.shape[1] for source in self.sources)
        if filled < self.target.shape[0]:
            self.target[filled:] = jnp.zeros((self.target.shape[0] - filled, self.target.shape[1]), BF16)

    def wait(self):
        for copy in self.copies:
            copy.wait()
        if self.stage is not None:
            for i, source in enumerate(self.sources):
                blocks, rows, columns = source.shape
                buffer = self.stage.at[:, pl.ds(0, rows)]
                copy = pltpu.make_async_copy(source, buffer, self.sems.at[0])
                copy.start()
                copy.wait()
                for block in range(blocks):
                    self.target[i * rows : (i + 1) * rows, block * columns : (block + 1) * columns] = (
                        self.stage[block, :rows]
                    )


def stage_of(sizes):
    if sizes.depth % 128 == 0:
        return {}
    return dict(stage=pltpu.VMEM((sizes.rows, max(sizes.unit, sizes.attn // 2), sizes.depth), BF16))


def stage_in(r):
    return r.named.get("stage")


def hidden_tiles(hidden):
    return [(at, min(384, hidden - at)) for at in range(0, hidden, 384)]


def padded(hidden):
    return -(-hidden // 128) * 128


def width_tiles(width):
    return [(at, 512) for at in range(0, width, 512)]


def put_partial(r, k, at, size, value):
    n = value.shape[0] // 2
    r.partial[k, :, pl.ds(at, size)] = value[:n]
    r.side_out[k, :, pl.ds(at, size)] = value[n:].astype(BF16)


def side_copies(links, r):
    return [links.copy(r.side_out.at[k], r.side_in.at[k], SECTION) for k in range(4)]


def with_side(r, k):
    return r.partial[k] + r.side_in[k].astype(F32)


def ffn_forward(r, layer, a, at, weights):
    r = r.of(layer)
    links = Links(r.f_sems)
    blocks, result_ref, second_ref = r.f_blocks, r.result, r.second
    gate_out, up_out, act_out = r.hidden[0], r.hidden[1], r.hidden[2]
    n, width = blocks.shape[2:]
    hidden = r.w_gate.shape[0]
    second = second_ref[...]
    inverse = lax.rsqrt(jnp.mean(second * second, axis=-1, keepdims=True) + EPS)
    blocks[0, 0] = (second * inverse * r.gain_ffn[...]).astype(BF16)
    gather = BlockGather(links, blocks, a, ROW_LOW)
    sides = side_copies(links, r)
    scatter = Scatter(links, r, r.f_corner_in, r.f_edge_in, a, ROW_LOW)
    gather.a.start()
    gather.b.start()
    gather.sides[0].start()
    at(layer).f_sent()
    gather.a.wait_recv()
    gather.ab.start()
    gather.sides[1].start()
    gather.b.wait_recv()
    gather.ba.start()
    gather.sides[2].start()
    gather.ab.wait_recv()
    gather.ba.wait_recv()
    gather.sides[3].start()
    at(layer).f_gathered()
    stage = stage_in(r)
    loads = [
        Load(move.blocks, weight, stage, sems)
        for move, weight, sems in zip(weights, (r.w_gate, r.w_up, r.w_down), r.f_load_sems, strict=True)
    ]
    loads[0].start()
    loads[1].start()
    loads[0].wait()
    loads[1].wait()
    saves = []
    for k in range(4):
        gather.sides[k].wait_recv()
        x = blocks[k].reshape(2 * n, width)
        rows = pl.ds(k * 2 * n, 2 * n)
        for lane, size in hidden_tiles(hidden):
            lanes = pl.ds(lane, size)
            gate = dot(x, r.w_gate[lanes], 1, 1)
            up = dot(x, r.w_up[lanes], 1, 1)
            act = gate / (1.0 + jnp.exp(-gate)) * up
            gate_out[rows, lanes] = gate.astype(BF16)
            up_out[rows, lanes] = up.astype(BF16)
            act_out[rows, lanes] = act.astype(BF16)
        pairs = [(blocks.at[k], r.f_blocks_hbm.at[k])]
        for source, target in ((gate_out, r.gate), (up_out, r.up), (act_out, r.act)):
            pairs.append((source.at[rows], target.at[rows]))
        save(saves, r.f_save_sem, pairs)
        getattr(at(layer), "f_up" + str(k))()
    at(layer).f_up()
    loads[2].start()
    loads[2].wait()

    def down(k):
        act = act_out[pl.ds(k * 2 * n, 2 * n)]
        for lane, size in width_tiles(width):
            put_partial(r, k, lane, size, dot(act, r.w_down[:, pl.ds(lane, size)], 1, 0))
        sides[k].start()

    down(3)
    down(1)
    sides[3].wait_recv()
    scatter.send_corner(with_side(r, 3))
    down(2)
    sides[1].wait_recv()
    scatter.send_edge_a(with_side(r, 1))
    sides[2].wait_recv()
    scatter.send_edge_b(with_side(r, 2))
    down(0)
    at(layer).f_edges()
    sides[0].wait_recv()
    result_ref[...] = second_ref[...] + scatter.total(with_side(r, 0))
    at(layer).f_end()
    wait_all([], [*gather.copies, *sides, *scatter.copies])
    for copy in saves:
        copy.wait()


def ffn_backward(r, layer, a, at, gathers):
    r = r.of(layer)
    links = Links(r.f_sems)
    blocks, second_ref, grad_ref = r.f_blocks, r.second, r.of(layer + 1).d_entry
    gate_in, up_in = r.hidden
    d_gate_out, d_up_out = r.hidden
    n, width = blocks.shape[2:]
    hidden = r.w_gate.shape[0]
    stage = stage_in(r)
    loads = [
        Load(halves, weight, stage, sems)
        for halves, weight, sems in zip(
            ([r.gate_own, r.gate_other], [r.up_own, r.up_other], [r.down_own, r.down_other]),
            (r.w_gate, r.w_up, r.w_down),
            r.f_load_sems,
            strict=True,
        )
    ]
    for load in loads:
        load.start()
    more = [(r.gate, gate_in), (r.up, up_in)]
    if not gathers:
        more.append((r.gathered, blocks))
    extra = []
    save(extra, r.f_extra_sem, more)
    if gathers:
        blocks[0, 0] = grad_ref[...]
    gather = BlockGather(links, blocks, a, ROW_LOW, there=not gathers)
    sides = side_copies(links, r)
    scatter = Scatter(links, r, r.f_corner_in, r.f_edge_in, a, ROW_LOW)
    saves = []

    def step(k):
        g = blocks[k].reshape(2 * n, width)
        rows = pl.ds(k * 2 * n, 2 * n)
        for lane, size in hidden_tiles(hidden):
            lanes = pl.ds(lane, size)
            d_act = dot(g, r.w_down[lanes], 1, 1)
            gate = gate_in[rows, lanes].astype(F32)
            up = up_in[rows, lanes].astype(F32)
            sigma = 1.0 / (1.0 + jnp.exp(-gate))
            d_gate_out[rows, lanes] = (d_act * up * sigma * (1.0 + gate * (1.0 - sigma))).astype(BF16)
            d_up_out[rows, lanes] = (d_act * gate * sigma).astype(BF16)
        pairs = [(d_gate_out.at[rows], r.d_gate.at[rows]), (d_up_out.at[rows], r.d_up.at[rows])]
        if gathers:
            pairs.append((blocks.at[k], r.f_blocks_hbm.at[k]))
        save(saves, r.f_save_sem, pairs)
        d_gate = d_gate_out[rows]
        d_up = d_up_out[rows]
        for lane, size in width_tiles(width):
            lanes = pl.ds(lane, size)
            value = dot(d_gate, r.w_gate[:, lanes], 1, 0) + dot(d_up, r.w_up[:, lanes], 1, 0)
            put_partial(r, k, lane, size, value)
        sides[k].start()

    gather.a.start()
    gather.b.start()
    gather.sides[0].start()
    at(layer).f_sent()
    for load in loads:
        load.wait()
    for copy in extra:
        copy.wait()
    gather.sides[0].wait_recv()
    step(0)
    gather.a.wait_recv()
    gather.ab.start()
    gather.sides[1].start()
    gather.b.wait_recv()
    gather.ba.start()
    gather.sides[2].start()
    gather.sides[1].wait_recv()
    step(1)
    gather.ab.wait_recv()
    gather.ba.wait_recv()
    gather.sides[3].start()
    gather.sides[3].wait_recv()
    step(3)
    sides[3].wait_recv()
    scatter.send_corner(with_side(r, 3))
    at(layer).f_corner()
    gather.sides[2].wait_recv()
    step(2)
    sides[1].wait_recv()
    scatter.send_edge_a(with_side(r, 1))
    sides[2].wait_recv()
    scatter.send_edge_b(with_side(r, 2))
    at(layer).f_edges()
    sides[0].wait_recv()
    d_normed = scatter.total(with_side(r, 0))
    second = second_ref[...]
    inverse = lax.rsqrt(jnp.mean(second * second, axis=-1, keepdims=True) + EPS)
    d_second, d_gain = norm_backward(second, inverse, r.gain_ffn[...], d_normed)
    r.d_gain_ffn[...] = d_gain
    r.d_second[...] = grad_ref[...].astype(F32) + d_second
    at(layer).f_end()
    wait_all([], [*gather.copies, *sides, *scatter.copies])
    for copy in saves:
        copy.wait()


def turn(vectors, cosine, sine):
    return vectors * cosine + pltpu.roll(vectors, HEAD // 2, 1) * sine


def seen(r, slot):
    key = r.key[...]
    visible = (key >= r.start[pl.ds(slot, 1)]) & (key <= r.own[...])
    return jnp.where(visible, 0.0, -1e30)


def attention_weights(r):
    weights = r.w_attn
    heads_width = (weights.shape[0] - 2 * HEAD) // 2
    return (
        weights.at[pl.ds(0, heads_width)],
        weights.at[pl.ds(heads_width, heads_width)],
        weights.at[pl.ds(2 * heads_width, 2 * HEAD)],
    )


def column_gather(links, blocks):
    h = blocks.shape[1] // 2
    return (
        links.copy(blocks.at[0], blocks.at[1], COL_LOW),
        links.copy(blocks.at[0], blocks.at[2], COL_HIGH),
        links.copy(blocks.at[1, pl.ds(0, h)], blocks.at[3, pl.ds(0, h)], COL_HIGH),
        links.copy(blocks.at[2, pl.ds(h, h)], blocks.at[3, pl.ds(h, h)], COL_LOW),
    )


def attention_forward(r, layer, at, gather):
    r = r.of(layer)
    links = Links(r.a_sems)
    entry, kv, bias, partial = r.entry, r.kv, r.bias, r.partial
    normed, query, mixed, lse_ref = r.normed, r.query, r.mixed, r.lse
    cos_ref, sin_ref = r.cos, r.sin
    n, width = entry.shape[1:]
    tokens = 2 * n
    rows = kv.shape[1]
    w_query, w_out, w_pair = attention_weights(r)
    heads = w_query.shape[0] // HEAD
    bits = rows.bit_length() - 1
    scale = 1.0 / math.sqrt(HEAD)
    stage = stage_in(r)
    load = Load(gather.blocks, r.w_attn, stage, r.a_load_sem)
    scatter = Scatter(links, r, r.a_corner_in, r.a_edge_in, COL_LOW, COL_HIGH)
    hops = [
        [(slot, filled, links.copy(kv.at[b, slot], kv.at[b, filled], (ROW, 1 << bit)))
         for slot, filled, bit in row_hops(bits)]
        for b in range(2)
    ]
    copies = scatter.copies + [copy for group in hops for _, _, copy in group]

    def normalise(k):
        x = entry[k].astype(F32)
        inverse = lax.rsqrt(jnp.mean(x * x, axis=-1, keepdims=True) + EPS)
        normed[pl.ds(k * n, n)] = (x * inverse * r.gain_attn[...]).astype(BF16)

    def project_pair(b):
        where = pl.ds(b * tokens, tokens)
        pair = dot(normed[where], w_pair[...], 1, 1) + r.b_pair[...]
        kv[b, 0, :, :HEAD] = turn(pair[:, :HEAD], cos_ref[where], sin_ref[where]).astype(BF16)
        kv[b, 0, :, HEAD:] = pair[:, HEAD:].astype(BF16)
        for slot, _, copy in hops[b]:
            if slot == 0:
                copy.start()

    def project_query(b):
        where = pl.ds(b * tokens, tokens)
        projected = dot(normed[where], w_query[...], 1, 1) + r.b_query[...]
        for head in range(heads):
            lanes = slice(head * HEAD, (head + 1) * HEAD)
            query[where, lanes] = turn(projected[:, lanes], cos_ref[where], sin_ref[where]).astype(BF16)

    arrived = [set(), set()]

    def arrive(b, slot):
        for _, filled, copy in hops[b]:
            if filled == slot and slot not in arrived[b]:
                copy.wait_recv()
                arrived[b].add(slot)

    if layer:
        entry[0] = r.result0[...].astype(BF16)
        to_low, to_high, corner_high, corner_low = column_gather(links, entry)
        copies += [to_low, to_high, corner_high, corner_low]
        to_low.start()
        to_high.start()
        at(layer).a_begin()
        load.start()
        normalise(0)
        to_low.wait_recv()
        corner_high.start()
        to_high.wait_recv()
        corner_low.start()
        normalise(1)
        normalise(2)
        load.wait()
        project_pair(0)
        corner_high.wait_recv()
        corner_low.wait_recv()
        normalise(3)
        project_pair(1)
    else:
        at(layer).a_begin()
        for k in range(4):
            normalise(k)
        at(layer).a_normed()
        load.start()
        load.wait()
        project_pair(1)
        project_pair(0)
    at(layer).a_pairs()
    project_query(1)
    project_query(0)
    at(layer).a_queries()
    for b in (1, 0):
        for slot, _, copy in hops[b]:
            if slot:
                arrive(b, slot)
                copy.start()
    at(layer).a_relayed()
    saves = []
    for b in (1, 0):
        for slot in range(1, rows):
            arrive(b, slot)
        save(saves, r.a_save_sem, [(kv.at[b], r.kv_hbm.at[b])])
        keys = kv[b, :, :, :HEAD].reshape(rows * tokens, HEAD)
        values = kv[b, :, :, HEAD:].reshape(rows * tokens, HEAD)
        where = pl.ds(b * tokens, tokens)
        bias[...] = seen(r, b)
        for head in range(heads):
            lanes = slice(head * HEAD, (head + 1) * HEAD)
            scores = dot(keys, query[where, lanes], 1, 1) * scale + bias[...]
            top = jnp.max(scores, axis=0, keepdims=True)
            raised = jnp.exp(scores - top)
            total = jnp.sum(raised, axis=0, keepdims=True)
            lse_ref[b, pl.ds(head, 1)] = top + jnp.log(total)
            probs = (raised * (1.0 / total)).astype(BF16)
            mixed[where, lanes] = dot(probs, values, 0, 0).astype(BF16)
            if b == 0:
                getattr(at(layer), "a_head" + str(head))()
        for k in (2 * b + 1, 2 * b):
            for lane, size in width_tiles(width):
                partial[k, :, pl.ds(lane, size)] = dot(
                    mixed[pl.ds(k * n, n)], w_out[:, pl.ds(lane, size)], 1, 0
                )
        if b == 1:
            scatter.send_corner(partial[3])
            at(layer).a_half()
    scatter.send_edge_b(partial[2])
    scatter.send_edge_a(partial[1])
    if layer:
        save(saves, r.a_save_sem, [(entry, r.entry_hbm)])
    at(layer).a_edges()
    r.second[...] = entry[0].astype(F32) + scatter.total(partial[0])
    at(layer).a_end()
    wait_all([], copies)
    for copy in saves:
        copy.wait()


def attention_backward(r, layer, at):
    r = r.of(layer)
    links = Links(r.a_sems)
    blocks, kv, bias, partial = r.a_blocks, r.kv, r.bias, r.partial
    d_mixed, d_kv, d_kv_out, d_kv_in = r.d_mixed, r.d_kv, r.d_kv_out, r.d_kv_in
    query, d_query, d_pair = r.query, r.d_query, r.d_pair
    share_out, share_in = r.share_out, r.share_in
    cos_ref, sin_ref = r.cos, r.sin
    n, width = blocks.shape[1:]
    tokens = 2 * n
    rows = kv.shape[1]
    w_query, w_out, w_pair = attention_weights(r)
    heads_width = w_query.shape[0]
    heads = heads_width // HEAD
    bits = rows.bit_length() - 1
    scale = 1.0 / math.sqrt(HEAD)
    stage = stage_in(r)
    load = Load([r.attn_blocks.at[0], r.attn_blocks.at[1]], r.w_attn, stage, r.a_load_sem)
    load.start()
    blocks[0] = r.d_second[...].astype(BF16)
    to_low, to_high, corner_high, corner_low = column_gather(links, blocks)
    hops = [
        [(slot, filled, links.copy(d_kv_out.at[b, filled], d_kv_in.at[b, filled], (ROW, 1 << bit)))
         for slot, filled, bit in reversed(row_hops(bits))]
        for b in range(2)
    ]
    share = [links.copy(share_out.at[b], share_in.at[b], COL_LOW) for b in range(2)]
    scatter = Scatter(links, r, r.a_corner_in, r.a_edge_in, COL_LOW, COL_HIGH)

    def unmix(k):
        d_mixed[pl.ds(k * n, n)] = dot(blocks[k], w_out[...], 1, 1).astype(BF16)

    def attend(b):
        keys = kv[b, :, :, :HEAD].reshape(rows * tokens, HEAD)
        values = kv[b, :, :, HEAD:].reshape(rows * tokens, HEAD)
        where = pl.ds(b * tokens, tokens)
        bias[...] = seen(r, b)
        for head in range(heads):
            lanes = slice(head * HEAD, (head + 1) * HEAD)
            q = query[where, lanes]
            d_o = d_mixed[where, lanes]
            scores = dot(keys, q, 1, 1) * scale + bias[...]
            probs = jnp.exp(scores - r.lse[b, pl.ds(head, 1)])
            d_probs = dot(values, d_o, 1, 1)
            delta = jnp.sum(d_probs * probs, axis=0, keepdims=True)
            d_scores = (probs * (d_probs - delta)).astype(BF16)
            d_keys = (dot(d_scores, q, 1, 0) * scale).reshape(rows, tokens, HEAD)
            d_values = dot(probs.astype(BF16), d_o, 1, 0).reshape(rows, tokens, HEAD)
            if head:
                d_keys = d_keys + d_kv[b, :, :, :HEAD]
                d_values = d_values + d_kv[b, :, :, HEAD:]
            d_kv[b, :, :, :HEAD] = d_keys
            d_kv[b, :, :, HEAD:] = d_values
            turned = dot(d_scores, keys, 0, 0) * scale
            d_query[where, lanes] = turn(turned, cos_ref[where], -sin_ref[where]).astype(BF16)

    def send_bit(b, step):
        for slot, filled, copy in hops[b]:
            if filled - slot == step:
                d_kv_out[b, filled] = d_kv[b, filled].astype(BF16)
                copy.start()

    def add_bit(b, step):
        for slot, filled, copy in hops[b]:
            if filled - slot == step:
                copy.wait_recv()
                d_kv[b, slot] = d_kv[b, slot] + d_kv_in[b, filled].astype(F32)

    def share_pair(b):
        share_out[b] = d_kv[b, 0, n:].astype(BF16)
        share[b].start()

    def finish_pair(b):
        share[b].wait_recv()
        total = d_kv[b, 0, :n] + share_in[b].astype(F32)
        where = pl.ds(b * tokens, n)
        rows_of = pl.ds(b * n, n)
        d_pair[rows_of, :HEAD] = turn(total[:, :HEAD], cos_ref[where], -sin_ref[where]).astype(BF16)
        d_pair[rows_of, HEAD:] = total[:, HEAD:].astype(BF16)

    def unproject(k):
        for lane, size in width_tiles(width):
            lanes = pl.ds(lane, size)
            value = dot(d_query[pl.ds(k * n, n)], w_query[:, lanes], 1, 0)
            if k % 2 == 0:
                value = value + dot(d_pair[pl.ds(k // 2 * n, n)], w_pair[:, lanes], 1, 0)
            partial[k, :, lanes] = value

    to_low.start()
    to_high.start()
    at(layer).a_sent()
    load.wait()
    unmix(0)
    to_low.wait_recv()
    corner_high.start()
    to_high.wait_recv()
    corner_low.start()
    at(layer).a_relayed()
    unmix(1)
    unmix(2)
    corner_high.wait_recv()
    corner_low.wait_recv()
    unmix(3)
    attend(1)
    send_bit(1, 1)
    unproject(3)
    scatter.send_corner(partial[3])
    attend(0)
    send_bit(0, 1)
    for bit in range(1, bits):
        for b in (1, 0):
            add_bit(b, 1 << (bit - 1))
            send_bit(b, 1 << bit)
    at(layer).a_hops()
    unproject(1)
    scatter.send_edge_a(partial[1])
    for b in (1, 0):
        add_bit(b, 1 << (bits - 1))
        share_pair(b)
    finish_pair(1)
    unproject(2)
    scatter.send_edge_b(partial[2])
    at(layer).a_edges()
    finish_pair(0)
    unproject(0)
    r.d_bias_query[...] = jnp.sum(d_query[...].astype(F32), axis=0, keepdims=True)
    r.d_bias_pair[...] = jnp.sum(d_pair[...].astype(F32), axis=0, keepdims=True)
    a_grad, normed = r.a_grad, r.normed
    own_blocks = blocks[...].reshape(4 * n, width)
    for lane, size in width_tiles(width):
        lanes = pl.ds(lane, size)
        a_grad[:heads_width, lanes] = dot(d_query[...], normed[:, lanes], 0, 0).astype(BF16)
        a_grad[heads_width : 2 * heads_width, lanes] = dot(
            r.mixed[...], own_blocks[:, lane : lane + size], 0, 0
        ).astype(BF16)
        normed_own = jnp.concatenate([normed[:n, lanes], normed[tokens : tokens + n, lanes]])
        a_grad[2 * heads_width :, lanes] = dot(d_pair[...], normed_own, 0, 0).astype(BF16)
    at(layer).a_grads()
    d_normed = scatter.total(partial[0])
    stream = r.entry[...].astype(F32)
    inverse = lax.rsqrt(jnp.mean(stream * stream, axis=-1, keepdims=True) + EPS)
    d_first, d_gain = norm_backward(stream, inverse, r.gain_attn[...], d_normed)
    r.d_gain_attn[...] = d_gain
    r.d_entry[...] = (r.d_second[...] + d_first).astype(BF16)
    at(layer).a_end()
    copies = [to_low, to_high, corner_high, corner_low, *share, *scatter.copies]
    wait_all([], copies + [copy for group in hops for _, _, copy in group])


def sum_vectors(r, at, links):
    vector = r.vector
    vector[...] = jnp.zeros_like(vector)
    col = lax.axis_index(COL)
    lanes = r.d_gain_ffn0.shape[1] // HEAD
    heads = r.d_bias_query0.shape[1] // HEAD
    each = vector.shape[0] // 2
    for layer in range(2):
        of = r.of(layer)
        for gain, first in ((of.d_gain_attn, 0), (of.d_gain_ffn, lanes)):
            for i in range(lanes):
                vector[pl.ds(layer * each + first + i, 1)] = gain[:, i * HEAD : (i + 1) * HEAD]
        for i in range(heads):
            place = layer * each + 2 * lanes + col * heads + i
            vector[pl.ds(place, 1)] = of.d_bias_query[:, i * HEAD : (i + 1) * HEAD]
        for i in range(2):
            place = layer * each + 3 * lanes + i * KV + (col >> 1)
            vector[pl.ds(place, 1)] = of.d_bias_pair[:, i * HEAD : (i + 1) * HEAD]
    ways = [SECTION, COL_LOW, COL_HIGH] + [(ROW, 1 << bit) for bit in range(row_bits())]
    copies = []
    for i, way in enumerate(ways):
        r.vector_out[i] = vector[...]
        copies.append(links.copy(r.vector_out.at[i], r.vector_in.at[i], way))
        copies[-1].start()
        at(i).s_step()
        copies[-1].wait_recv()
        vector[...] = vector[...] + r.vector_in[i]
    r.sums[...] = vector[...]
    wait_all([], copies)


class Sizes:
    def __init__(self, n, width, rows, hidden, attn, depth):
        self.n, self.width, self.rows, self.depth = n, width, rows, depth
        self.unit, self.hidden, self.attn = hidden // 2, padded(hidden), attn
        self.heads_width = (attn - 2 * HEAD) // 2
        self.heads = self.heads_width // HEAD


def common_scratch(sizes):
    n, width = sizes.n, sizes.width
    return dict(
        partial=pltpu.VMEM((4, n, width), F32),
        corner_out=pltpu.VMEM((2, n // 2, width), BF16),
        edge_out=pltpu.VMEM((2, n, width), BF16),
        **stage_of(sizes),
    )


def ffn_scratch(sizes, count, saves):
    n, width, hidden = sizes.n, sizes.width, sizes.hidden
    each = 2 * sizes.rows
    return dict(
        w_gate=pltpu.VMEM((hidden, width), BF16),
        w_up=pltpu.VMEM((hidden, width), BF16),
        w_down=pltpu.VMEM((hidden, width), BF16),
        hidden=[pltpu.VMEM((8 * n, hidden), BF16) for _ in range(count)],
        side_out=pltpu.VMEM((4, n, width), BF16),
        f_load_sems=semaphores(each, each, each),
        f_extra_sem=pltpu.SemaphoreType.DMA((3,)),
        f_save_sem=pltpu.SemaphoreType.DMA((4 * saves,)),
    )


def ffn_buffers(sizes, layer):
    n, width = sizes.n, sizes.width
    return layered(
        layer,
        f_blocks=pltpu.VMEM((4, 2, n, width), BF16),
        side_in=pltpu.VMEM((4, n, width), BF16),
        f_corner_in=pltpu.VMEM((2, n // 2, width), BF16),
        f_edge_in=pltpu.VMEM((2, n, width), BF16),
        f_sems=semaphores(16, 16),
    )


def attention_scratch(sizes):
    tokens = 2 * sizes.n
    return dict(
        w_attn=pltpu.VMEM((sizes.attn, sizes.width), BF16),
        bias=pltpu.VMEM((sizes.rows * tokens, tokens), F32),
        a_load_sem=pltpu.SemaphoreType.DMA((2 * sizes.rows,)),
        a_save_sem=pltpu.SemaphoreType.DMA((3,)),
    )


def attention_buffers(sizes, layer, backward):
    n, width, rows = sizes.n, sizes.width, sizes.rows
    pairs = (2, rows, 2 * n, 2 * HEAD)
    count = 10 + 2 * (rows - 1)
    buffers = dict(
        a_corner_in=pltpu.VMEM((2, n // 2, width), BF16),
        a_edge_in=pltpu.VMEM((2, n, width), BF16),
        a_sems=semaphores(count, count),
    )
    if backward:
        buffers.update(a_blocks=pltpu.VMEM((4, n, width), BF16))
        buffers.update(d_kv_in=pltpu.VMEM(pairs, BF16))
        buffers.update(share_in=pltpu.VMEM((2, n, 2 * HEAD), BF16))
    else:
        buffers.update(kv=pltpu.VMEM(pairs, BF16))
    return layered(layer, **buffers)


def attention_back_scratch(sizes):
    n, rows = sizes.n, sizes.rows
    pairs = (2, rows, 2 * n, 2 * HEAD)
    return dict(
        **attention_scratch(sizes),
        d_mixed=pltpu.VMEM((4 * n, sizes.heads_width), BF16),
        d_kv=pltpu.VMEM(pairs, F32),
        d_kv_out=pltpu.VMEM(pairs, BF16),
        share_out=pltpu.VMEM((2, n, 2 * HEAD), BF16),
        d_query=pltpu.VMEM((4 * n, sizes.heads_width), BF16),
        d_pair=pltpu.VMEM((2 * n, 2 * HEAD), BF16),
        a_grad=pltpu.VMEM((sizes.attn, sizes.width), BF16),
    )


def small_outs(sizes, layer):
    return layered(
        layer,
        d_gain_attn=((1, sizes.width), F32, True),
        d_bias_query=((1, sizes.heads_width), F32, True),
        d_bias_pair=((1, 2 * HEAD), F32, True),
    )


def exchange_halves(parts, section):
    return pick(parts, section), swap(pick(parts, 1 - section), *SECTION)


def of_layer(layer, parts, section, token):
    own, other = parts
    return jnp.where(section + token == layer, own, other)


def to_owner(first, second, section):
    keep = jnp.where(section == 0, first, second)
    away = jnp.where(section == 0, second, first)
    other = swap(away, *SECTION)
    return jnp.where(section == 0, keep, other), jnp.where(section == 0, other, keep)


def local(
    tokens,
    cotangent,
    lengths,
    norm_attn,
    w_query,
    b_query,
    w_keyval,
    b_keyval,
    w_out,
    norm_ffn,
    w_gate,
    w_up,
    w_down,
):
    section = lax.axis_index(SEC)
    row = lax.axis_index(ROW)
    col = lax.axis_index(COL)
    rows = lax.axis_size(ROW)
    cols = lax.axis_size(COL)
    low, high = bit_of(col, 0), bit_of(col, 1)
    place = (section, row, low, high)
    row_count = tokens.shape[1]
    width = tokens.shape[2]
    half = row_count // 2
    depth = w_query.shape[1]
    heads_width = w_query.shape[2]

    def blocks_of(array):
        return jnp.concatenate(
            [
                lax.dynamic_slice(
                    array, (2 * section + (high ^ j), (low ^ k) * half, 0), (1, half, width)
                )
                for j in range(2)
                for k in range(2)
            ]
        )

    small = jnp.concatenate([norm_attn[0], norm_ffn[0], b_keyval[0], b_query[0]])
    small = (small, swap(small, *SECTION))
    small = [of_layer(layer, small, section, 0).astype(F32) for layer in range(2)]

    pair_cols = w_keyval[0].reshape(-1, 2, KV, HEAD)
    mine = pick(pair_cols, high, 2).reshape(-1, 2 * HEAD)
    away = pick(pair_cols, 1 - high, 2).reshape(-1, 2 * HEAD)
    pair_rows = ordered(mine[None, None], swap(away, *COL_HIGH)[None, None], high, 0)
    pair_rows = ordered(pair_rows, swap(pair_rows, *COL_LOW), low, 1)
    pair_rows = pair_rows.reshape(depth, 2 * HEAD)
    attn_own = jnp.concatenate([w_query[0].T, w_out[0], pair_rows.T])
    attn_halves = exchange_halves(attn_own.reshape(2, -1, depth), section)

    def ffn_parts(shard):
        hidden = shard.shape[0]
        parts = shard.reshape(2, 2, hidden // 4, shard.shape[1]).transpose(1, 0, 2, 3)
        return exchange_halves(parts, section)

    parts = [ffn_parts(shard) for shard in (w_gate[0].T, w_up[0].T, w_down[0])]
    ways = [(COL_LOW, COL_HIGH), (COL_HIGH, COL_LOW)]

    hidden = w_gate.shape[2] // 2

    tables = layout(lengths, place, row_count)
    sizes = Sizes(half, width, rows, hidden, 2 * attn_halves[0].shape[0], depth)
    entry = blocks_of(tokens)

    ffn_ways = [way for way, _ in ways]
    across = [way for _, way in ways]
    cosine, sine, start, own_index, key_index = tables
    shared = dict(
        cos=(cosine, True),
        sin=(sine, True),
        start=(start, True),
        own=(own_index, True),
        key=(key_index, True),
    )
    gains_attn, gains_ffn, vectors = [], [], []
    for layer in range(2):
        bias_pair = small[layer][2 * width : 2 * width + 2 * KV * HEAD].reshape(2, KV, HEAD)
        gains_attn.append(layered(layer, gain_attn=(small[layer][None, :width], True)))
        gains_ffn.append(layered(layer, gain_ffn=(small[layer][None, width : 2 * width], True)))
        vectors.append(
            layered(
                layer,
                b_query=(small[layer][None, 2 * width + 2 * KV * HEAD :], True),
                b_pair=(pick(bias_pair, high, 1).reshape(1, -1), True),
            )
        )
    chip_ways = [COL_LOW, COL_HIGH, SECTION] + [(ROW, 1 << bit) for bit in range(row_bits())]

    attn_moves = [AttnGather(of_layer(layer, attn_halves, section, 0)) for layer in range(2)]
    ffn_moves = [
        [FfnGather(of_layer(layer, parts[kind], section, 0), across[layer]) for kind in range(3)]
        for layer in range(2)
    ]
    grad_own = lax.dynamic_slice(
        cotangent, (2 * section + high, low * half, 0), (1, half, width)
    )[0]
    grad_move = TokenGather(grad_own, grad_own.shape, ffn_ways[1], ROW_LOW, True)
    (attn_a, attn_b), ((gate_a, up_a, down_a), (gate_b, up_b, down_b)) = attn_moves, ffn_moves
    some, rest = rows // 2, rows - rows // 2
    schedule = dict(
        a0_begin=[attn_a],
        a0_normed=[attn_a, gate_a, gate_a, attn_a],
        a0_queries=[gate_a] * rows,
        a0_relayed=[up_a, up_a, down_a, down_a],
        a0_head0=[up_a] * some,
        a0_head1=[up_a] * rest,
        f0_sent=[down_a] * some + [attn_b],
        f0_gathered=[gate_a] + [down_a] * rest + [up_a],
        f0_up=[down_a, attn_b],
        f0_edges=[gate_b, gate_b],
        f0_end=[attn_b],
        a1_queries=[gate_b] * rows,
        a1_relayed=[up_b, up_b, down_b, down_b],
        a1_head0=[up_b] * some,
        a1_head1=[up_b] * rest,
        f1_sent=[down_b] * some,
        f1_gathered=[gate_b] + [down_b] * rest + [up_b, grad_move],
        f1_up=[down_b, grad_move],
        f1_edges=[grad_move],
    )

    def forward_kernel(r, at):
        for layer in range(2):
            attention_forward(r, layer, at, attn_moves[layer])
            ffn_forward(r, layer, ffn_ways[layer], at, ffn_moves[layer])

    tokens_here = 4 * half
    outs = dict(entry_hbm1=((4, half, width), BF16, False), result1=((half, width), F32, True))
    buffers = dict(
        entry1=pltpu.VMEM((4, half, width), BF16), result0=pltpu.VMEM((half, width), F32)
    )
    units = ((8 * half, sizes.hidden), BF16, False)
    for layer in range(2):
        outs.update(
            layered(
                layer,
                second=((half, width), F32, True),
                normed=((tokens_here, width), BF16, True),
                query=((tokens_here, heads_width), BF16, True),
                mixed=((tokens_here, heads_width), BF16, True),
                lse=((2, sizes.heads, 2 * half), F32, True),
                kv_hbm=((2, rows, 2 * half, 2 * HEAD), BF16, False),
                f_blocks_hbm=((4, 2, half, width), BF16, False),
                gate=units,
                up=units,
                act=units,
            )
        )
        buffers.update(ffn_buffers(sizes, layer))
        buffers.update(attention_buffers(sizes, layer, False))
    done = kernel_call(
        forward_kernel,
        0,
        chip_ways,
        dict(
            entry0=(entry, True),
            **shared,
            **gains_attn[0],
            **gains_attn[1],
            **gains_ffn[0],
            **gains_ffn[1],
            **vectors[0],
            **vectors[1],
        ),
        outs,
        {**common_scratch(sizes), **ffn_scratch(sizes, 3, 4), **attention_scratch(sizes), **buffers},
        1 << 34,
        [*attn_moves, *ffn_moves[0], *ffn_moves[1], grad_move],
        schedule,
    )
    (grad_all,) = grad_move.results
    last_result = done.result1.astype(BF16)

    def grad_of(left, right):
        return dot(left, right.reshape(-1, width), 0, 0).astype(BF16)

    unit = sizes.unit

    def blocked(grad, arrived):
        total = (grad[:unit].astype(F32) + arrived.astype(F32)).astype(BF16)
        return jnp.stack([total[:, i * depth : (i + 1) * depth] for i in range(rows)])

    def ffn_back_operands(layer):
        of = done.of(layer)
        (gate, gate_far), (up, up_far), (down, down_far) = (move.results for move in ffn_moves[layer])
        return {
            **gains_ffn[layer],
            **layered(
                layer,
                second=(of.second, True),
                gate=(of.gate, False),
                up=(of.up, False),
                gate_own=(gate, False),
                gate_other=(gate_far, False),
                up_own=(up, False),
                up_other=(up_far, False),
                down_own=(down, False),
                down_other=(down_far, False),
            ),
        }

    def ffn_back_outs(layer):
        return layered(
            layer,
            d_second=((half, width), F32, True),
            d_gain_ffn=((1, width), F32, True),
            d_gate=units,
            d_up=units,
        )

    def attention_back_operands(layer, own):
        of = done.of(layer)
        return {
            **gains_attn[layer],
            **shared,
            **layered(
                layer,
                entry=(own, True),
                attn_blocks=(attn_moves[layer].results[0], False),
                kv=(of.kv_hbm, True),
                normed=(of.normed, True),
                query=(of.query, True),
                mixed=(of.mixed, True),
                lse=(of.lse, True),
            ),
        }

    down_grad = grad_of(done.act1, grad_all)
    down_move = Across(down_grad, unit, across[1])
    back = kernel_call(
        lambda r, at: ffn_backward(r, 1, ffn_ways[1], at, False),
        1,
        [ffn_ways[1], ROW_LOW, SECTION],
        dict(d_entry2=(grad_own, True), gathered1=(grad_all, False), **ffn_back_operands(1)),
        ffn_back_outs(1),
        {**common_scratch(sizes), **ffn_scratch(sizes, 2, 2), **ffn_buffers(sizes, 1)},
        1 << 33,
        [down_move],
        dict(f1_sent=[down_move]),
    )
    gate_grad = grad_of(back.d_gate1, done.f_blocks_hbm1)
    up_grad = grad_of(back.d_up1, done.f_blocks_hbm1)
    down_one = blocked(down_grad, down_move.results[0])

    down_rows = Rows(down_one)
    gate_move = GradScatter(gate_grad, unit, across[1])
    up_move = Across(up_grad, unit, across[1])
    last_move = TokenGather(last_result, last_result.shape, COL_LOW, COL_HIGH, False)
    entry_move = TokenGather("d_entry1", (half, width), COL_LOW, COL_HIGH, False)
    attn_move_one = AttnScatter("a_grad", (sizes.attn, width))

    def middle_kernel(r, at):
        attention_backward(r, 1, at)
        ffn_backward(r, 0, ffn_ways[0], at, True)

    middle = kernel_call(
        middle_kernel,
        2,
        chip_ways,
        dict(
            d_second1=(back.d_second1, True),
            **attention_back_operands(1, done.entry_hbm1[0]),
            **ffn_back_operands(0),
        ),
        dict(
            d_entry1=((half, width), BF16, True),
            f_blocks_hbm0=((4, 2, half, width), BF16, False),
            **small_outs(sizes, 1),
            **ffn_back_outs(0),
        ),
        {
            **common_scratch(sizes),
            **attention_back_scratch(sizes),
            **attention_buffers(sizes, 1, True),
            **ffn_scratch(sizes, 2, 3),
            **ffn_buffers(sizes, 0),
        },
        1 << 33,
        [down_rows, gate_move, up_move, last_move, entry_move, attn_move_one],
        dict(
            a1_relayed=[down_rows, gate_move],
            a1_grads=[attn_move_one],
            f0_edges=[gate_move, up_move, attn_move_one, last_move, entry_move],
        ),
    )
    up_one = blocked(up_grad, up_move.results[0])
    zero_grads = [
        grad_of(done.act0, middle.f_blocks_hbm0),
        grad_of(middle.d_gate0, done.f_blocks_hbm0),
        grad_of(middle.d_up0, done.f_blocks_hbm0),
    ]

    up_rows = Rows(up_one)
    zero_moves = [GradScatter(grad, unit, across[0]) for grad in zero_grads]
    attn_move_zero = AttnScatter("a_grad", (sizes.attn, width))
    first_move = TokenGather("d_entry0", (half, width), COL_LOW, COL_HIGH, False)
    sum_rows = 2 * (3 * width // HEAD + 2 * KV)
    sum_ways = 3 + row_bits()

    def last_kernel(r, at):
        attention_backward(r, 0, at)
        sum_vectors(r, at, Links(r.sum_sems))

    down_zero, gate_zero, up_zero = zero_moves
    final = kernel_call(
        last_kernel,
        3,
        chip_ways,
        dict(
            d_second0=(middle.d_second0, True),
            d_gain_ffn0=(middle.d_gain_ffn0, True),
            d_gain_ffn1=(back.d_gain_ffn1, True),
            **attention_back_operands(0, entry[0]),
            **{name: (middle.named[name], True) for name in small_outs(sizes, 1)},
        ),
        dict(d_entry0=((half, width), BF16, True), sums=((sum_rows, HEAD), F32, True)),
        {
            **common_scratch(sizes),
            **attention_back_scratch(sizes),
            **attention_buffers(sizes, 0, True),
            **{name: pltpu.VMEM(shape, F32) for name, (shape, _, _) in small_outs(sizes, 0).items()},
            **dict(
                vector=pltpu.VMEM((sum_rows, HEAD), F32),
                vector_out=pltpu.VMEM((sum_ways, sum_rows, HEAD), F32),
                vector_in=pltpu.VMEM((sum_ways, sum_rows, HEAD), F32),
                sum_sems=semaphores(sum_ways, sum_ways),
            ),
        },
        1 << 32,
        [up_rows, *zero_moves, attn_move_zero, first_move],
        dict(
            a0_relayed=[down_zero],
            a0_hops=[up_rows],
            a0_edges=[gate_zero, up_zero],
            a0_grads=[down_zero, attn_move_zero],
            a0_end=[attn_move_zero, gate_zero, first_move],
            s1_step=[attn_move_zero],
            s2_step=[first_move],
            s3_step=[attn_move_zero],
        ),
    )

    def by_row_bit(own, arrived):
        near, far = own.astype(F32), 0.0
        for flip in range(1, rows):
            if flip & 1:
                far = far + arrived[flip].astype(F32)
            else:
                near = near + arrived[flip].astype(F32)
        return ordered(near.astype(BF16)[None], far.astype(BF16)[None], row & 1, 0)

    ffn_grads = [
        [by_row_bit(*move.results) for move in (gate_zero, up_zero, down_zero)],
        [
            by_row_bit(*gate_move.results),
            by_row_bit(pick(up_one, row), up_rows.results[0]),
            by_row_bit(pick(down_one, row), down_rows.results[0]),
        ],
    ]
    sums = final.sums.reshape(2, -1)
    sums = jnp.where(section == 0, sums[0], sums[1])
    grad_norm_attn = sums[:width]
    grad_norm_ffn = sums[width : 2 * width]
    spread = sums[2 * width : 2 * width + cols * heads_width].reshape(cols, -1)
    grad_b_query = pick(spread, col)
    grad_b_keyval = sums[2 * width + cols * heads_width :]
    first_result, (last_blocks,) = done.entry_hbm1, last_move.results
    (grad_one_blocks,), (grad_zero_blocks,) = entry_move.results, first_move.results
    (attn_one_half,), (attn_zero_half,) = attn_move_one.results, attn_move_zero.results

    def assemble(first, second):
        def placed(blocks):
            blocks = blocks.reshape(2, 2, half, width)
            blocks = jnp.where(high == 0, blocks, blocks[::-1])
            blocks = jnp.where(low == 0, blocks, blocks[:, ::-1])
            return blocks.reshape(2, row_count, width)

        zeroth, later = to_owner(placed(first), placed(second), section)
        return jnp.concatenate([zeroth, later])[None]

    outputs = assemble(first_result, last_blocks)
    grads_in = assemble(grad_zero_blocks, grad_one_blocks)

    def ffn_grad(kind):
        zeroth, later = to_owner(ffn_grads[0][kind], ffn_grads[1][kind], section)
        whole = jnp.stack([zeroth, later], axis=1)
        return whole.reshape(-1, whole.shape[-1])

    grad_gate = ffn_grad(0).T.astype(F32)
    grad_up = ffn_grad(1).T.astype(F32)
    grad_down = ffn_grad(2).astype(F32)

    total = jnp.concatenate(to_owner(attn_zero_half, attn_one_half, section)).astype(F32)
    grad_query = total[:heads_width].T
    grad_out = total[heads_width : 2 * heads_width]
    pair = total[2 * heads_width :].T.reshape(2, 2, depth // 4, 2 * HEAD)
    pair = pick(pair, low, 1) + swap(pick(pair, 1 - low, 1).astype(BF16), *COL_LOW).astype(F32)
    pair = pair.astype(BF16)
    pair = ordered(
        pick(pair, high)[:, None], swap(pick(pair, 1 - high), *COL_HIGH)[:, None], high, 1
    )
    grad_keyval = (
        pair.reshape(-1, 2, 2, HEAD).transpose(0, 2, 1, 3).reshape(-1, 2 * KV * HEAD).astype(F32)
    )

    return (
        outputs,
        grads_in,
        grad_norm_attn[None],
        grad_query[None],
        grad_b_query[None],
        grad_keyval[None],
        grad_b_keyval[None],
        grad_out[None],
        grad_norm_ffn[None],
        grad_gate[None],
        grad_up[None],
        grad_down[None],
    )


def solution(mesh):
    in_specs = (
        P(None, ROW, None),
        P(None, ROW, None),
        P(),
        P(SEC, None),
        P(SEC, ROW, COL),
        P(SEC, COL),
        P(SEC, (ROW, COL), None),
        P(SEC, None),
        P(SEC, COL, ROW),
        P(SEC, None),
        P(SEC, ROW, COL),
        P(SEC, ROW, COL),
        P(SEC, COL, ROW),
    )
    out_specs = (
        P(SEC, None, ROW, None),
        P(SEC, None, ROW, None),
        P(SEC, None),
        P(SEC, ROW, COL),
        P(SEC, COL),
        P(SEC, (ROW, COL), None),
        P(SEC, None),
        P(SEC, COL, ROW),
        P(SEC, None),
        P(SEC, ROW, COL),
        P(SEC, ROW, COL),
        P(SEC, COL, ROW),
    )
    return jax.shard_map(local, mesh=mesh, in_specs=in_specs, out_specs=out_specs, check_vma=False)
```

```python
import functools
import math

import jax
import jax.numpy as jnp
from jax import lax
from jax.experimental import pallas as pl
from jax.experimental.pallas import tpu as pltpu
from jax.sharding import PartitionSpec as P

HEADS = 12
KV = 2
HEAD = 128

EPS = 1e-06
THETA = 1000000.0

ROW, SEC, COL = "row", "section", "col"

F32 = jnp.float32
BF16 = jnp.bfloat16

COL_LOW = (COL, 1)
COL_HIGH = (COL, 2)
ROW_LOW = (ROW, 1)
SECTION = (SEC, 1)


def swap(value, axis, flip):
    pairs = [(i, i ^ flip) for i in range(lax.axis_size(axis))]
    return lax.ppermute(value, axis, pairs)


def bit_of(index, bit):
    return (index >> bit) & 1


def pick(array, index, axis=0):
    return lax.dynamic_index_in_dim(array, index, axis, keepdims=False)


def ordered(mine, other, bit, axis):
    first = jnp.where(bit == 0, mine, other)
    second = jnp.where(bit == 0, other, mine)
    return jnp.concatenate([first, second], axis=axis)


def row_bits():
    return lax.axis_size(ROW).bit_length() - 1


def norm_backward(stream, inverse, gain, gradient):
    inner = jnp.mean(gradient * gain * stream, axis=-1, keepdims=True)
    d_stream = gain * gradient * inverse - stream * (inverse * inverse * inverse) * inner
    return (d_stream, jnp.sum(gradient * stream * inverse, axis=0, keepdims=True))


def dot(left, right, left_dim, right_dim):
    return lax.dot_general(
        left, right, (((left_dim,), (right_dim,)), ((), ())), preferred_element_type=F32
    )


def layout(lengths, place, row_count):
    section, row, low, high = place
    rows = lax.axis_size(ROW)
    half = row_count // 2
    inside = jnp.arange(row_count, dtype=jnp.int32)
    inside = (((inside // half) ^ low) * half) + inside % half
    own_index = row * row_count + inside
    key_index = ((jnp.arange(rows, dtype=jnp.int32) ^ row) * row_count)[:, None] + inside[None, :]
    slots = 2 * section + (jnp.arange(2, dtype=jnp.int32) ^ high)
    picked = jnp.stack([pick(lengths, slots[0]), pick(lengths, slots[1])])
    ends = jnp.cumsum(picked, axis=1)
    starts = ends - picked
    inside_piece = (own_index[None, None, :] >= starts[:, :, None]) & (
        own_index[None, None, :] < ends[:, :, None]
    )
    first = jnp.sum(jnp.where(inside_piece, starts[:, :, None], 0), axis=1)
    inverse = THETA ** (-(jnp.arange(HEAD // 2, dtype=F32) * 2.0 / HEAD))
    angle = (own_index[None, :] - first).astype(F32).reshape(-1, 1) * inverse
    cosine, sine = jnp.cos(angle), jnp.sin(angle)
    return (
        jnp.concatenate([cosine, cosine], axis=1),
        jnp.concatenate([-sine, sine], axis=1),
        first,
        own_index[None, :],
        key_index.reshape(-1, 1),
    )


MESH = pl.DeviceIdType.MESH
VMEM_LIMIT = 62 * 1024 * 1024


def partner_of(way):
    axis, flip = way
    return {axis: lax.axis_index(axis) ^ flip}


def enter(ways):
    barrier = pltpu.get_barrier_semaphore()
    for way in ways:
        pl.semaphore_signal(barrier, inc=1, device_id=partner_of(way), device_id_type=MESH)
    pl.semaphore_wait(barrier, len(ways))


def remote(source, target, send, recv, way):
    return pltpu.make_async_remote_copy(
        src_ref=source,
        dst_ref=target,
        send_sem=send,
        recv_sem=recv,
        device_id=partner_of(way),
        device_id_type=MESH,
    )


class Links:
    def __init__(self, sems):
        self.send, self.recv = sems
        self.used = 0

    def copy(self, source, target, way):
        slot = self.used
        self.used += 1
        return remote(source, target, self.send.at[slot], self.recv.at[slot], way)


def semaphores(*counts):
    return [pltpu.SemaphoreType.DMA((count,)) for count in counts]


def wait_all(arriving, leaving):
    for copy in arriving:
        copy.wait_recv()
    for copy in leaving:
        copy.wait_send()


class Refs:
    def __init__(self, named, layer=None):
        self.named, self.layer = named, layer

    def __getattr__(self, name):
        return self.named[name] if name in self.named else self.named[name + str(self.layer)]

    def of(self, layer):
        return Refs(self.named, layer)


def layered(layer, **values):
    return {name + str(layer): value for name, value in values.items()}


class Pump:
    def __init__(self, schedule, number=None):
        self.schedule, self.number = schedule, number

    def __call__(self, number):
        return Pump(self.schedule, number)

    def __getattr__(self, point):
        def run():
            for move in self.schedule.get(point[0] + str(self.number) + point[1:], ()):
                move.advance()

        return run


def kernel_call(kernel, collective_id, ways, operands, outs, scratch, flops, moves, schedule):
    vmem = pl.BlockSpec(memory_space=pltpu.VMEM)
    hbm = pl.BlockSpec(memory_space=pl.ANY)
    moved_in = [array for move in moves for array in move.operands]
    moved_out = [out for move in moves for out in move.outs]
    every = list(ways)
    for move in moves:
        every += [way for way in move.ways if way not in every]
    scratch_list = []
    for spec in scratch.values():
        scratch_list += spec if isinstance(spec, list) else [spec]

    def body(*refs):
        refs = list(refs)

        def take(count):
            taken, refs[:] = refs[:count], refs[count:]
            return taken

        named = dict(zip(operands, take(len(operands))))
        sources = [take(len(move.operands)) for move in moves]
        named.update(zip(outs, take(len(outs))))
        targets = [take(len(move.outs)) for move in moves]
        for name, spec in scratch.items():
            named[name] = take(len(spec)) if isinstance(spec, list) else take(1)[0]
        for move, source, target in zip(moves, sources, targets, strict=True):
            if move.name:
                source = [named[move.name]]
            move.bind(source, target, take(len(move.scratch)))

        enter(every)
        kernel(Refs(named), Pump(schedule))
        while any(move.at < len(move.steps) for move in moves):
            for move in moves:
                move.advance()

    results = pl.pallas_call(
        body,
        out_shape=[jax.ShapeDtypeStruct(shape, dtype) for shape, dtype, _ in outs.values()]
        + [jax.ShapeDtypeStruct(shape, BF16) for shape in moved_out],
        in_specs=[vmem if inside else hbm for _, inside in operands.values()] + [hbm] * len(moved_in),
        out_specs=[vmem if inside else hbm for _, _, inside in outs.values()] + [hbm] * len(moved_out),
        scratch_shapes=scratch_list + [ref for move in moves for ref in move.scratch],
        compiler_params=pltpu.CompilerParams(
            collective_id=collective_id, has_side_effects=True, vmem_limit_bytes=VMEM_LIMIT
        ),
        cost_estimate=pl.CostEstimate(flops=flops, bytes_accessed=32 << 20, transcendentals=1 << 20),
    )(*[array for array, _ in operands.values()], *moved_in)
    moved = results[len(outs) :]
    for move in moves:
        move.results, moved = moved[: len(move.outs)], moved[len(move.outs) :]
    return Refs(dict(zip(outs, results)))


def row_hops(bits):
    hops, known = [], [0]
    for bit in reversed(range(bits)):
        step = 1 << bit
        hops += [(slot, slot | step, bit) for slot in known]
        known += [slot | step for slot in known]
    return hops


class Move:
    def __init__(self, source, outs, scratch, ways):
        self.name = source if isinstance(source, str) else None
        self.operands = [] if self.name else [source]
        self.outs, self.scratch, self.ways = outs, scratch, ways
        self.steps, self.at = [], 0

    def advance(self):
        if self.at < len(self.steps):
            self.steps[self.at]()
            self.at += 1


class FfnGather(Move):
    def __init__(self, part, across):
        rows = lax.axis_size(ROW)
        self.flips, self.across = list(range(rows - 1, 0, -1)), across
        outs = [(rows, *part.shape[1:])] * 2
        ways = [(ROW, flip) for flip in self.flips] + [across]
        super().__init__(part, outs, semaphores(rows, rows, rows, rows, 1), ways)

    def bind(self, sources, targets, scratch):
        (part,), (own, other) = sources, targets
        self.blocks = [own, other]
        row_send, row_recv, far_send, far_recv, local_sem = scratch
        row = lax.axis_index(ROW)
        near = part.at[row & 1]
        local = pltpu.make_async_copy(near, own.at[row], local_sem.at[0])
        hops = {
            flip: remote(
                part.at[(row ^ flip) & 1], own.at[row], row_send.at[flip], row_recv.at[flip], (ROW, flip)
            )
            for flip in self.flips
        }
        far = {
            flip: remote(
                own.at[row ^ flip] if flip else near,
                other.at[row ^ flip],
                far_send.at[flip],
                far_recv.at[flip],
                self.across,
            )
            for flip in [0] + self.flips
        }

        def start():
            local.start()
            hops[self.flips[0]].start()

        def start_rest():
            for flip in self.flips[1:]:
                hops[flip].start()

        def forward(flip):
            def step():
                if flip:
                    hops[flip].wait_recv()
                far[flip].start()

            return step

        def finish():
            local.wait()
            wait_all(far.values(), [*hops.values(), *far.values()])

        self.steps = [start, start_rest, *[forward(flip) for flip in [0] + self.flips], finish]


class AttnGather(Move):
    def __init__(self, part):
        rows = lax.axis_size(ROW)
        self.bits = rows.bit_length() - 1
        ways = [(ROW, 1 << bit) for bit in range(self.bits)] + [SECTION]
        super().__init__(part, [(2, rows, *part.shape)], semaphores(rows, rows, rows, rows, 1), ways)

    def bind(self, sources, targets, scratch):
        (part,), (blocks,) = sources, targets
        self.blocks = [blocks.at[0], blocks.at[1]]
        row_send, row_recv, side_send, side_recv, local_sem = scratch
        section, row = lax.axis_index(SEC), lax.axis_index(ROW)

        def place(slot):
            return blocks.at[section, row ^ slot]

        def source(slot):
            return place(slot) if slot else part

        local = pltpu.make_async_copy(part, place(0), local_sem.at[0])
        hops = [
            (slot, filled, remote(source(slot), place(slot), row_send.at[filled], row_recv.at[filled], (ROW, 1 << bit)))
            for slot, filled, bit in row_hops(self.bits)
        ]
        sides = [
            remote(source(slot), place(slot), side_send.at[slot], side_recv.at[slot], SECTION)
            for slot in range(1 << self.bits)
        ]
        arrived = {0}

        def arrive(slot):
            if slot not in arrived:
                arrived.add(slot)
                for _, filled, copy in hops:
                    if filled == slot:
                        copy.wait_recv()
                sides[slot].start()

        def start():
            local.start()
            for slot, _, copy in hops:
                if slot == 0:
                    copy.start()
            sides[0].start()

        def forward():
            for slot, _, copy in hops:
                if slot:
                    arrive(slot)
                    copy.start()

        def finish():
            for slot in range(len(sides)):
                arrive(slot)
            local.wait()
            wait_all(sides, [copy for _, _, copy in hops] + sides)

        self.steps = [start, forward, finish]


class ColumnGather(Move):
    def __init__(self, own, shape):
        super().__init__(own, [(4, *shape)], semaphores(8, 8, 1), [COL_LOW, COL_HIGH])

    def bind(self, sources, targets, scratch):
        (own,), (blocks,) = sources, targets
        send, recv, local_sem = scratch
        col = lax.axis_index(COL)
        h = own.shape[0] // 2
        links = Links((send, recv))
        place = blocks.at[col]
        local = pltpu.make_async_copy(own, place, local_sem.at[0])
        first = [links.copy(own, place, COL_LOW), links.copy(own, place, COL_HIGH)]
        top = blocks.at[col ^ COL_LOW[1], pl.ds(0, h)]
        bottom = blocks.at[col ^ COL_HIGH[1], pl.ds(h, h)]
        second = [links.copy(top, top, COL_HIGH), links.copy(bottom, bottom, COL_LOW)]

        def start():
            local.start()
            for copy in first:
                copy.start()

        def forward():
            for arrived, copy in zip(first, second, strict=True):
                arrived.wait_recv()
                copy.start()

        def finish():
            local.wait()
            wait_all(second, first + second)

        self.steps = [start, forward, finish]


class TokenGather(Move):
    def __init__(self, own, shape, a, b, sides):
        self.a, self.b, self.sides = a, b, sides
        ways = [a, b] + ([SECTION] if sides else [])
        super().__init__(own, [(4, 1 + sides, *shape)], semaphores(8, 8, 1), ways)

    def bind(self, sources, targets, scratch):
        (own,), (blocks,) = sources, targets
        send, recv, local_sem = scratch
        local = pltpu.make_async_copy(own, blocks.at[0, 0], local_sem.at[0])
        gather = BlockGather(Links((send, recv)), blocks, self.a, self.b, self.sides, own)

        def start():
            local.start()
            for copy in (gather.a, gather.b, gather.sides[0]):
                copy.start()

        def forward():
            gather.a.wait_recv()
            gather.ab.start()
            gather.sides[1].start()
            gather.b.wait_recv()
            gather.ba.start()
            gather.sides[2].start()

        def last():
            gather.ab.wait_recv()
            gather.ba.wait_recv()
            gather.sides[3].start()

        def finish():
            local.wait()
            wait_all(gather.sides, gather.copies)

        self.steps = [start, forward, last, finish]


class Across(Move):
    def __init__(self, grad, n, way):
        self.n, self.way = n, way
        super().__init__(grad, [(n, grad.shape[1])], semaphores(1, 1), [way])

    def bind(self, sources, targets, scratch):
        (grad,), (arrived,) = sources, targets
        send, recv = scratch
        copy = remote(grad.at[pl.ds(self.n, self.n)], arrived, send.at[0], recv.at[0], self.way)
        self.steps = [copy.start, lambda: wait_all([copy], [copy])]


class Rows(Move):
    def __init__(self, total):
        rows = total.shape[0]
        self.flips = list(range(1, rows))
        ways = [(ROW, flip) for flip in self.flips]
        super().__init__(total, [total.shape], semaphores(rows, rows), ways)

    def bind(self, sources, targets, scratch):
        (total,), (arrived,) = sources, targets
        send, recv = scratch
        copies = row_copies(total, arrived, send, recv, self.flips)

        def start():
            for copy in copies:
                copy.start()

        self.steps = [start, lambda: wait_all(copies, copies)]


def row_copies(total, arrived, send, recv, flips):
    row = lax.axis_index(ROW)
    return [
        remote(total.at[row ^ flip], arrived.at[flip], send.at[flip], recv.at[flip], (ROW, flip))
        for flip in flips
    ]


class GradScatter(Move):
    def __init__(self, grad, n, way):
        rows, width = lax.axis_size(ROW), grad.shape[1]
        self.n, self.way, self.flips = n, way, list(range(1, rows))
        shape = (rows, n, width // rows)
        scratch = [pltpu.VMEM((n, width), BF16), pltpu.VMEM((n, width), BF16), pltpu.VMEM(shape, BF16)]
        scratch += semaphores(1, 1, 1, 1, rows, rows)
        ways = [way] + [(ROW, flip) for flip in self.flips]
        super().__init__(grad, [shape[1:], shape], scratch, ways)

    def bind(self, sources, targets, scratch):
        (grad,), (own, arrived) = sources, targets
        mine, theirs, total, local_sem, own_sem, far_send, far_recv, row_send, row_recv = scratch
        n, row = self.n, lax.axis_index(ROW)
        depth = total.shape[2]
        local = pltpu.make_async_copy(grad.at[pl.ds(0, n)], mine, local_sem.at[0])
        far = remote(grad.at[pl.ds(n, n)], theirs, far_send.at[0], far_recv.at[0], self.way)
        keep = pltpu.make_async_copy(total.at[row], own, own_sem.at[0])
        copies = row_copies(total, arrived, row_send, row_recv, self.flips)

        def start():
            local.start()
            far.start()

        def forward():
            local.wait()
            far.wait_recv()
            for block in range(total.shape[0]):
                at = slice(block * depth, (block + 1) * depth)
                total[block] = (mine[:, at].astype(F32) + theirs[:, at].astype(F32)).astype(BF16)
            for copy in copies + [keep]:
                copy.start()

        def finish():
            keep.wait()
            wait_all(copies, copies + [far])

        self.steps = [start, forward, finish]


class AttnScatter(Move):
    def __init__(self, name, shape):
        rows, width, m = lax.axis_size(ROW), shape[1], shape[0] // 2
        self.bits, self.m = rows.bit_length() - 1, m
        blocks = (rows, m, width // rows)
        scratch = [
            pltpu.VMEM((m, width), BF16),
            pltpu.VMEM(blocks, F32),
            pltpu.VMEM(blocks, BF16),
            pltpu.VMEM(blocks, BF16),
        ]
        scratch += semaphores(1, 1, 1, rows, rows)
        ways = [SECTION] + [(ROW, 1 << bit) for bit in range(self.bits)]
        super().__init__(name, [blocks[1:]], scratch, ways)

    def bind(self, sources, targets, scratch):
        (grad,), (out,) = sources, targets
        theirs, total, going, coming, out_sem, side_send, side_recv, send, recv = scratch
        m, row, section = self.m, lax.axis_index(ROW), lax.axis_index(SEC)
        depth = total.shape[2]
        mine = grad.at[pl.ds(pl.multiple_of(section * m, m), m)]
        side = remote(
            grad.at[pl.ds(pl.multiple_of((1 - section) * m, m), m)],
            theirs,
            side_send.at[0],
            side_recv.at[0],
            SECTION,
        )
        keep = pltpu.make_async_copy(going.at[0], out, out_sem.at[0])
        hops = [
            (slot, filled, remote(going.at[filled], coming.at[filled], send.at[filled], recv.at[filled], (ROW, 1 << bit)))
            for slot, filled, bit in reversed(row_hops(self.bits))
        ]

        def sum_sides():
            side.wait_recv()
            for block in range(total.shape[0]):
                at = slice(block * depth, (block + 1) * depth)
                total[row ^ block] = mine[:, at].astype(F32) + theirs[:, at].astype(F32)
            send_bit(0)

        def send_bit(bit):
            for slot, filled, copy in hops:
                if filled - slot == 1 << bit:
                    going[filled] = total[filled].astype(BF16)
                    copy.start()

        def add_bit(bit):
            for slot, filled, copy in hops:
                if filled - slot == 1 << bit:
                    copy.wait_recv()
                    total[slot] = total[slot] + coming[filled].astype(F32)

        def hop(bit):
            def step():
                add_bit(bit - 1)
                send_bit(bit)

            return step

        def finish():
            add_bit(self.bits - 1)
            going[0] = total[0].astype(BF16)
            keep.start()
            keep.wait()
            wait_all([], [copy for _, _, copy in hops] + [side])

        self.steps = [side.start, sum_sides, *[hop(bit) for bit in range(1, self.bits)], finish]


class NoCopy:
    def start(self):
        pass

    wait_recv = wait_send = start


class BlockGather:
    def __init__(self, links, blocks, a, b, sides=True, own=None, there=False):
        h = blocks.shape[2] // 2
        own = blocks.at[0, 0] if own is None else own
        if there:
            self.a = self.b = self.ab = self.ba = NoCopy()
        else:
            self.a = links.copy(own, blocks.at[1, 0], a)
            self.b = links.copy(own, blocks.at[2, 0], b)
            self.ab = links.copy(blocks.at[1, 0, pl.ds(0, h)], blocks.at[3, 0, pl.ds(0, h)], b)
            self.ba = links.copy(blocks.at[2, 0, pl.ds(h, h)], blocks.at[3, 0, pl.ds(h, h)], a)
        self.sides = [NoCopy()] * 4
        if sides and not there:
            self.sides = [
                links.copy(blocks.at[k, 0] if k else own, blocks.at[k, 1], SECTION) for k in range(4)
            ]
        self.copies = [self.a, self.b, self.ab, self.ba, *self.sides]


class Scatter:
    def __init__(self, links, r, corner_in, edge_in, a, b):
        self.r, self.corner_in, self.edge_in = r, corner_in, edge_in
        self.corner_b = links.copy(r.corner_out.at[0], corner_in.at[0], b)
        self.corner_a = links.copy(r.corner_out.at[1], corner_in.at[1], a)
        self.edge_a = links.copy(r.edge_out.at[0], edge_in.at[0], a)
        self.edge_b = links.copy(r.edge_out.at[1], edge_in.at[1], b)
        self.copies = [self.corner_b, self.corner_a, self.edge_a, self.edge_b]

    def send_corner(self, value):
        corner = self.r.corner_out
        corner[...] = value.astype(BF16).reshape(corner.shape)
        self.corner_b.start()
        self.corner_a.start()

    def send_edge_a(self, value):
        edge, h = self.r.edge_out, value.shape[0] // 2
        self.corner_b.wait_recv()
        edge[0, :h] = (value[:h] + self.corner_in[0].astype(F32)).astype(BF16)
        edge[0, h:] = value[h:].astype(BF16)
        self.edge_a.start()

    def send_edge_b(self, value):
        edge, h = self.r.edge_out, value.shape[0] // 2
        self.corner_a.wait_recv()
        edge[1, :h] = value[:h].astype(BF16)
        edge[1, h:] = (value[h:] + self.corner_in[1].astype(F32)).astype(BF16)
        self.edge_b.start()

    def total(self, value):
        self.edge_a.wait_recv()
        self.edge_b.wait_recv()
        return value + self.edge_in[0].astype(F32) + self.edge_in[1].astype(F32)


def save(started, sems, pairs):
    for source, target in pairs:
        started.append(pltpu.make_async_copy(source, target, sems.at[len(started)]))
        started[-1].start()


class Load:
    def __init__(self, sources, target, stage, sems):
        self.sources, self.target, self.stage, self.copies, self.sems = sources, target, stage, [], sems
        if stage is None:
            for i, source in enumerate(sources):
                blocks, rows, columns = source.shape
                for block in range(blocks):
                    place = target.at[pl.ds(i * rows, rows), pl.ds(block * columns, columns)]
                    self.copies.append(
                        pltpu.make_async_copy(source.at[block], place, sems.at[len(self.copies)])
                    )

    def start(self):
        for copy in self.copies:
            copy.start()
        filled = sum(source.shape[1] for source in self.sources)
        if filled < self.target.shape[0]:
            self.target[filled:] = jnp.zeros((self.target.shape[0] - filled, self.target.shape[1]), BF16)

    def wait(self):
        for copy in self.copies:
            copy.wait()
        if self.stage is not None:
            for i, source in enumerate(self.sources):
                blocks, rows, columns = source.shape
                buffer = self.stage.at[:, pl.ds(0, rows)]
                copy = pltpu.make_async_copy(source, buffer, self.sems.at[0])
                copy.start()
                copy.wait()
                for block in range(blocks):
                    self.target[i * rows : (i + 1) * rows, block * columns : (block + 1) * columns] = (
                        self.stage[block, :rows]
                    )


def stage_of(sizes):
    if sizes.depth % 128 == 0:
        return {}
    return dict(stage=pltpu.VMEM((sizes.rows, max(sizes.unit, sizes.attn // 2), sizes.depth), BF16))


def stage_in(r):
    return r.named.get("stage")


def hidden_tiles(hidden):
    return [(at, min(384, hidden - at)) for at in range(0, hidden, 384)]


def padded(hidden):
    return -(-hidden // 128) * 128


def width_tiles(width):
    return [(at, 512) for at in range(0, width, 512)]


def put_partial(r, k, at, size, value):
    n = value.shape[0] // 2
    r.partial[k, :, pl.ds(at, size)] = value[:n]
    r.side_out[k, :, pl.ds(at, size)] = value[n:].astype(BF16)


def side_copies(links, r):
    return [links.copy(r.side_out.at[k], r.side_in.at[k], SECTION) for k in range(4)]


def with_side(r, k):
    return r.partial[k] + r.side_in[k].astype(F32)


def ffn_forward(r, layer, a, at, weights):
    r = r.of(layer)
    links = Links(r.f_sems)
    blocks, result_ref, second_ref = r.f_blocks, r.result, r.second
    gate_out, up_out, act_out = r.hidden[0], r.hidden[1], r.hidden[2]
    n, width = blocks.shape[2:]
    hidden = r.w_gate.shape[0]
    second = second_ref[...]
    inverse = lax.rsqrt(jnp.mean(second * second, axis=-1, keepdims=True) + EPS)
    blocks[0, 0] = (second * inverse * r.gain_ffn[...]).astype(BF16)
    gather = BlockGather(links, blocks, a, ROW_LOW)
    sides = side_copies(links, r)
    scatter = Scatter(links, r, r.f_corner_in, r.f_edge_in, a, ROW_LOW)
    gather.a.start()
    gather.b.start()
    gather.sides[0].start()
    at(layer).f_sent()
    gather.a.wait_recv()
    gather.ab.start()
    gather.sides[1].start()
    gather.b.wait_recv()
    gather.ba.start()
    gather.sides[2].start()
    gather.ab.wait_recv()
    gather.ba.wait_recv()
    gather.sides[3].start()
    at(layer).f_gathered()
    stage = stage_in(r)
    loads = [
        Load(move.blocks, weight, stage, sems)
        for move, weight, sems in zip(weights, (r.w_gate, r.w_up, r.w_down), r.f_load_sems, strict=True)
    ]
    loads[0].start()
    loads[1].start()
    loads[0].wait()
    loads[1].wait()
    saves = []
    for k in range(4):
        gather.sides[k].wait_recv()
        x = blocks[k].reshape(2 * n, width)
        rows = pl.ds(k * 2 * n, 2 * n)
        for lane, size in hidden_tiles(hidden):
            lanes = pl.ds(lane, size)
            gate = dot(x, r.w_gate[lanes], 1, 1)
            up = dot(x, r.w_up[lanes], 1, 1)
            act = gate / (1.0 + jnp.exp(-gate)) * up
            gate_out[rows, lanes] = gate.astype(BF16)
            up_out[rows, lanes] = up.astype(BF16)
            act_out[rows, lanes] = act.astype(BF16)
        pairs = [(blocks.at[k], r.f_blocks_hbm.at[k])]
        for source, target in ((gate_out, r.gate), (up_out, r.up), (act_out, r.act)):
            pairs.append((source.at[rows], target.at[rows]))
        save(saves, r.f_save_sem, pairs)
        getattr(at(layer), "f_up" + str(k))()
    at(layer).f_up()
    loads[2].start()
    loads[2].wait()

    def down(k):
        act = act_out[pl.ds(k * 2 * n, 2 * n)]
        for lane, size in width_tiles(width):
            put_partial(r, k, lane, size, dot(act, r.w_down[:, pl.ds(lane, size)], 1, 0))
        sides[k].start()

    down(3)
    down(1)
    sides[3].wait_recv()
    scatter.send_corner(with_side(r, 3))
    down(2)
    sides[1].wait_recv()
    scatter.send_edge_a(with_side(r, 1))
    sides[2].wait_recv()
    scatter.send_edge_b(with_side(r, 2))
    down(0)
    at(layer).f_edges()
    sides[0].wait_recv()
    result_ref[...] = second_ref[...] + scatter.total(with_side(r, 0))
    at(layer).f_end()
    wait_all([], [*gather.copies, *sides, *scatter.copies])
    for copy in saves:
        copy.wait()


def ffn_backward_loads(r, layer, gathers):
    r = r.of(layer)
    stage = stage_in(r)
    loads = [
        Load(halves, weight, stage, sems)
        for halves, weight, sems in zip(
            ([r.gate_own, r.gate_other], [r.up_own, r.up_other], [r.down_own, r.down_other]),
            (r.w_gate, r.w_up, r.w_down),
            r.f_load_sems,
            strict=True,
        )
    ]
    for load in loads:
        load.start()
    more = [(r.gate, r.hidden[0]), (r.up, r.hidden[1])]
    if not gathers:
        more.append((r.gathered, r.f_blocks))
    extra = []
    save(extra, r.f_extra_sem, more)
    return loads + extra


def ffn_backward(r, layer, a, at, gathers, loads):
    r = r.of(layer)
    links = Links(r.f_sems)
    blocks, second_ref, grad_ref = r.f_blocks, r.second, r.of(layer + 1).d_entry
    gate_in, up_in = r.hidden
    d_gate_out, d_up_out = r.hidden
    n, width = blocks.shape[2:]
    hidden = r.w_gate.shape[0]
    if gathers:
        blocks[0, 0] = grad_ref[...]
    gather = BlockGather(links, blocks, a, ROW_LOW, there=not gathers)
    sides = side_copies(links, r)
    scatter = Scatter(links, r, r.f_corner_in, r.f_edge_in, a, ROW_LOW)
    saves = []

    def step(k):
        g = blocks[k].reshape(2 * n, width)
        rows = pl.ds(k * 2 * n, 2 * n)
        for lane, size in hidden_tiles(hidden):
            lanes = pl.ds(lane, size)
            d_act = dot(g, r.w_down[lanes], 1, 1)
            gate = gate_in[rows, lanes].astype(F32)
            up = up_in[rows, lanes].astype(F32)
            sigma = 1.0 / (1.0 + jnp.exp(-gate))
            d_gate_out[rows, lanes] = (d_act * up * sigma * (1.0 + gate * (1.0 - sigma))).astype(BF16)
            d_up_out[rows, lanes] = (d_act * gate * sigma).astype(BF16)
        pairs = [(d_gate_out.at[rows], r.d_gate.at[rows]), (d_up_out.at[rows], r.d_up.at[rows])]
        if gathers:
            pairs.append((blocks.at[k], r.f_blocks_hbm.at[k]))
        save(saves, r.f_save_sem, pairs)
        d_gate = d_gate_out[rows]
        d_up = d_up_out[rows]
        for lane, size in width_tiles(width):
            lanes = pl.ds(lane, size)
            value = dot(d_gate, r.w_gate[:, lanes], 1, 0) + dot(d_up, r.w_up[:, lanes], 1, 0)
            put_partial(r, k, lane, size, value)
        sides[k].start()

    gather.a.start()
    gather.b.start()
    gather.sides[0].start()
    at(layer).f_sent()
    for load in loads:
        load.wait()
    gather.sides[0].wait_recv()
    step(0)
    gather.a.wait_recv()
    gather.ab.start()
    gather.sides[1].start()
    gather.b.wait_recv()
    gather.ba.start()
    gather.sides[2].start()
    gather.sides[1].wait_recv()
    step(1)
    gather.ab.wait_recv()
    gather.ba.wait_recv()
    gather.sides[3].start()
    gather.sides[3].wait_recv()
    step(3)
    sides[3].wait_recv()
    scatter.send_corner(with_side(r, 3))
    at(layer).f_corner()
    gather.sides[2].wait_recv()
    step(2)
    sides[1].wait_recv()
    scatter.send_edge_a(with_side(r, 1))
    sides[2].wait_recv()
    scatter.send_edge_b(with_side(r, 2))
    at(layer).f_edges()
    sides[0].wait_recv()
    d_normed = scatter.total(with_side(r, 0))
    second = second_ref[...]
    inverse = lax.rsqrt(jnp.mean(second * second, axis=-1, keepdims=True) + EPS)
    d_second, d_gain = norm_backward(second, inverse, r.gain_ffn[...], d_normed)
    r.d_gain_ffn[...] = d_gain
    r.d_second[...] = grad_ref[...].astype(F32) + d_second
    at(layer).f_end()
    wait_all([], [*gather.copies, *sides, *scatter.copies])
    for copy in saves:
        copy.wait()


def turn(vectors, cosine, sine):
    return vectors * cosine + pltpu.roll(vectors, HEAD // 2, 1) * sine


def seen(r, slot):
    key = r.key[...]
    visible = (key >= r.start[pl.ds(slot, 1)]) & (key <= r.own[...])
    return jnp.where(visible, 0.0, -1e30)


def attention_weights(r):
    weights = r.w_attn
    heads_width = (weights.shape[0] - 2 * HEAD) // 2
    return (
        weights.at[pl.ds(0, heads_width)],
        weights.at[pl.ds(heads_width, heads_width)],
        weights.at[pl.ds(2 * heads_width, 2 * HEAD)],
    )


def column_gather(links, blocks):
    h = blocks.shape[1] // 2
    return (
        links.copy(blocks.at[0], blocks.at[1], COL_LOW),
        links.copy(blocks.at[0], blocks.at[2], COL_HIGH),
        links.copy(blocks.at[1, pl.ds(0, h)], blocks.at[3, pl.ds(0, h)], COL_HIGH),
        links.copy(blocks.at[2, pl.ds(h, h)], blocks.at[3, pl.ds(h, h)], COL_LOW),
    )


def attention_forward(r, layer, at, gather):
    r = r.of(layer)
    links = Links(r.a_sems)
    entry, kv, bias, partial = r.entry, r.kv, r.bias, r.partial
    normed, query, mixed, lse_ref = r.normed, r.query, r.mixed, r.lse
    cos_ref, sin_ref = r.cos, r.sin
    n, width = entry.shape[1:]
    tokens = 2 * n
    rows = kv.shape[1]
    w_query, w_out, w_pair = attention_weights(r)
    heads = w_query.shape[0] // HEAD
    bits = rows.bit_length() - 1
    scale = 1.0 / math.sqrt(HEAD)
    stage = stage_in(r)
    load = Load(gather.blocks, r.w_attn, stage, r.a_load_sem)
    scatter = Scatter(links, r, r.a_corner_in, r.a_edge_in, COL_LOW, COL_HIGH)
    hops = [
        [(slot, filled, links.copy(kv.at[b, slot], kv.at[b, filled], (ROW, 1 << bit)))
         for slot, filled, bit in row_hops(bits)]
        for b in range(2)
    ]
    copies = scatter.copies + [copy for group in hops for _, _, copy in group]

    def normalise(k):
        x = entry[k].astype(F32)
        inverse = lax.rsqrt(jnp.mean(x * x, axis=-1, keepdims=True) + EPS)
        normed[pl.ds(k * n, n)] = (x * inverse * r.gain_attn[...]).astype(BF16)

    def project_pair(b):
        where = pl.ds(b * tokens, tokens)
        pair = dot(normed[where], w_pair[...], 1, 1) + r.b_pair[...]
        kv[b, 0, :, :HEAD] = turn(pair[:, :HEAD], cos_ref[where], sin_ref[where]).astype(BF16)
        kv[b, 0, :, HEAD:] = pair[:, HEAD:].astype(BF16)
        for slot, _, copy in hops[b]:
            if slot == 0:
                copy.start()

    def project_query(b):
        where = pl.ds(b * tokens, tokens)
        projected = dot(normed[where], w_query[...], 1, 1) + r.b_query[...]
        for head in range(heads):
            lanes = slice(head * HEAD, (head + 1) * HEAD)
            query[where, lanes] = turn(projected[:, lanes], cos_ref[where], sin_ref[where]).astype(BF16)

    arrived = [set(), set()]

    def arrive(b, slot):
        for _, filled, copy in hops[b]:
            if filled == slot and slot not in arrived[b]:
                copy.wait_recv()
                arrived[b].add(slot)

    if layer:
        entry[0] = r.result0[...].astype(BF16)
        to_low, to_high, corner_high, corner_low = column_gather(links, entry)
        copies += [to_low, to_high, corner_high, corner_low]
        to_low.start()
        to_high.start()
        at(layer).a_begin()
        load.start()
        normalise(0)
        to_low.wait_recv()
        corner_high.start()
        to_high.wait_recv()
        corner_low.start()
        normalise(1)
        normalise(2)
        load.wait()
        project_pair(0)
        corner_high.wait_recv()
        corner_low.wait_recv()
        normalise(3)
        project_pair(1)
    else:
        at(layer).a_begin()
        for k in range(4):
            normalise(k)
        at(layer).a_normed()
        load.start()
        load.wait()
        project_pair(1)
        project_pair(0)
    at(layer).a_pairs()
    project_query(1)
    project_query(0)
    at(layer).a_queries()
    for b in (1, 0):
        for slot, _, copy in hops[b]:
            if slot:
                arrive(b, slot)
                copy.start()
    at(layer).a_relayed()
    saves = []
    for b in (1, 0):
        for slot in range(1, rows):
            arrive(b, slot)
        save(saves, r.a_save_sem, [(kv.at[b], r.kv_hbm.at[b])])
        keys = kv[b, :, :, :HEAD].reshape(rows * tokens, HEAD)
        values = kv[b, :, :, HEAD:].reshape(rows * tokens, HEAD)
        where = pl.ds(b * tokens, tokens)
        bias[...] = seen(r, b)
        for head in range(heads):
            lanes = slice(head * HEAD, (head + 1) * HEAD)
            scores = dot(keys, query[where, lanes], 1, 1) * scale + bias[...]
            top = jnp.max(scores, axis=0, keepdims=True)
            raised = jnp.exp(scores - top)
            total = jnp.sum(raised, axis=0, keepdims=True)
            lse_ref[b, pl.ds(head, 1)] = top + jnp.log(total)
            probs = (raised * (1.0 / total)).astype(BF16)
            mixed[where, lanes] = dot(probs, values, 0, 0).astype(BF16)
            if b == 0:
                getattr(at(layer), "a_head" + str(head))()
        for k in (2 * b + 1, 2 * b):
            for lane, size in width_tiles(width):
                partial[k, :, pl.ds(lane, size)] = dot(
                    mixed[pl.ds(k * n, n)], w_out[:, pl.ds(lane, size)], 1, 0
                )
        if b == 1:
            scatter.send_corner(partial[3])
            at(layer).a_half()
    scatter.send_edge_b(partial[2])
    scatter.send_edge_a(partial[1])
    if layer:
        save(saves, r.a_save_sem, [(entry.at[0], r.entry_hbm)])
    at(layer).a_edges()
    r.second[...] = entry[0].astype(F32) + scatter.total(partial[0])
    at(layer).a_end()
    wait_all([], copies)
    for copy in saves:
        copy.wait()


def attention_backward(r, layer, at):
    r = r.of(layer)
    links = Links(r.a_sems)
    blocks, kv, bias, partial = r.a_blocks, r.kv, r.bias, r.partial
    d_mixed, d_kv, d_kv_out, d_kv_in = r.d_mixed, r.d_kv, r.d_kv_out, r.d_kv_in
    query, d_query, d_pair = r.query, r.d_query, r.d_pair
    share_out, share_in = r.share_out, r.share_in
    cos_ref, sin_ref = r.cos, r.sin
    n, width = blocks.shape[1:]
    tokens = 2 * n
    rows = kv.shape[1]
    w_query, w_out, w_pair = attention_weights(r)
    heads_width = w_query.shape[0]
    heads = heads_width // HEAD
    bits = rows.bit_length() - 1
    scale = 1.0 / math.sqrt(HEAD)
    stage = stage_in(r)
    load = Load([r.attn_blocks.at[0], r.attn_blocks.at[1]], r.w_attn, stage, r.a_load_sem)
    load.start()
    blocks[0] = r.d_second[...].astype(BF16)
    to_low, to_high, corner_high, corner_low = column_gather(links, blocks)
    hops = [
        [(slot, filled, links.copy(d_kv_out.at[b, filled], d_kv_in.at[b, filled], (ROW, 1 << bit)))
         for slot, filled, bit in reversed(row_hops(bits))]
        for b in range(2)
    ]
    share = [links.copy(share_out.at[b], share_in.at[b], COL_LOW) for b in range(2)]
    scatter = Scatter(links, r, r.a_corner_in, r.a_edge_in, COL_LOW, COL_HIGH)

    def unmix(k):
        d_mixed[pl.ds(k * n, n)] = dot(blocks[k], w_out[...], 1, 1).astype(BF16)

    def attend(b):
        keys = kv[b, :, :, :HEAD].reshape(rows * tokens, HEAD)
        values = kv[b, :, :, HEAD:].reshape(rows * tokens, HEAD)
        where = pl.ds(b * tokens, tokens)
        bias[...] = seen(r, b)
        for head in range(heads):
            lanes = slice(head * HEAD, (head + 1) * HEAD)
            q = query[where, lanes]
            d_o = d_mixed[where, lanes]
            scores = dot(keys, q, 1, 1) * scale + bias[...]
            probs = jnp.exp(scores - r.lse[b, pl.ds(head, 1)])
            d_probs = dot(values, d_o, 1, 1)
            delta = jnp.sum(d_probs * probs, axis=0, keepdims=True)
            d_scores = (probs * (d_probs - delta)).astype(BF16)
            d_keys = (dot(d_scores, q, 1, 0) * scale).reshape(rows, tokens, HEAD)
            d_values = dot(probs.astype(BF16), d_o, 1, 0).reshape(rows, tokens, HEAD)
            if head:
                d_keys = d_keys + d_kv[b, :, :, :HEAD]
                d_values = d_values + d_kv[b, :, :, HEAD:]
            d_kv[b, :, :, :HEAD] = d_keys
            d_kv[b, :, :, HEAD:] = d_values
            turned = dot(d_scores, keys, 0, 0) * scale
            d_query[where, lanes] = turn(turned, cos_ref[where], -sin_ref[where]).astype(BF16)

    def send_bit(b, step):
        for slot, filled, copy in hops[b]:
            if filled - slot == step:
                d_kv_out[b, filled] = d_kv[b, filled].astype(BF16)
                copy.start()

    def add_bit(b, step):
        for slot, filled, copy in hops[b]:
            if filled - slot == step:
                copy.wait_recv()
                d_kv[b, slot] = d_kv[b, slot] + d_kv_in[b, filled].astype(F32)

    def share_pair(b):
        share_out[b] = d_kv[b, 0, n:].astype(BF16)
        share[b].start()

    def finish_pair(b):
        share[b].wait_recv()
        total = d_kv[b, 0, :n] + share_in[b].astype(F32)
        where = pl.ds(b * tokens, n)
        rows_of = pl.ds(b * n, n)
        d_pair[rows_of, :HEAD] = turn(total[:, :HEAD], cos_ref[where], -sin_ref[where]).astype(BF16)
        d_pair[rows_of, HEAD:] = total[:, HEAD:].astype(BF16)

    def unproject(k):
        for lane, size in width_tiles(width):
            lanes = pl.ds(lane, size)
            value = dot(d_query[pl.ds(k * n, n)], w_query[:, lanes], 1, 0)
            if k % 2 == 0:
                value = value + dot(d_pair[pl.ds(k // 2 * n, n)], w_pair[:, lanes], 1, 0)
            partial[k, :, lanes] = value

    to_low.start()
    to_high.start()
    at(layer).a_sent()
    load.wait()
    unmix(0)
    to_low.wait_recv()
    corner_high.start()
    to_high.wait_recv()
    corner_low.start()
    at(layer).a_relayed()
    unmix(1)
    unmix(2)
    corner_high.wait_recv()
    corner_low.wait_recv()
    unmix(3)
    attend(1)
    send_bit(1, 1)
    unproject(3)
    scatter.send_corner(partial[3])
    attend(0)
    send_bit(0, 1)
    for bit in range(1, bits):
        for b in (1, 0):
            add_bit(b, 1 << (bit - 1))
            send_bit(b, 1 << bit)
    at(layer).a_hops()
    unproject(1)
    scatter.send_edge_a(partial[1])
    for b in (1, 0):
        add_bit(b, 1 << (bits - 1))
        share_pair(b)
    finish_pair(1)
    unproject(2)
    scatter.send_edge_b(partial[2])
    at(layer).a_edges()
    finish_pair(0)
    unproject(0)
    r.d_bias_query[...] = jnp.sum(d_query[...].astype(F32), axis=0, keepdims=True)
    r.d_bias_pair[...] = jnp.sum(d_pair[...].astype(F32), axis=0, keepdims=True)
    a_grad, normed = r.a_grad, r.normed
    turned_query, turned_mixed, turned_pair = d_query[...].T, r.mixed[...].T, d_pair[...].T
    for lane, size in width_tiles(width):
        lanes = pl.ds(lane, size)
        a_grad[:heads_width, lanes] = dot(turned_query, normed[:, lanes], 1, 0).astype(BF16)
        a_grad[heads_width : 2 * heads_width, lanes] = dot(
            turned_mixed, blocks[:, :, lanes].reshape(4 * n, size), 1, 0
        ).astype(BF16)
        normed_own = jnp.concatenate([normed[:n, lanes], normed[tokens : tokens + n, lanes]])
        a_grad[2 * heads_width :, lanes] = dot(turned_pair, normed_own, 1, 0).astype(BF16)
    at(layer).a_grads()
    d_normed = scatter.total(partial[0])
    stream = r.entry[...].astype(F32)
    inverse = lax.rsqrt(jnp.mean(stream * stream, axis=-1, keepdims=True) + EPS)
    d_first, d_gain = norm_backward(stream, inverse, r.gain_attn[...], d_normed)
    r.d_gain_attn[...] = d_gain
    r.d_entry[...] = (r.d_second[...] + d_first).astype(BF16)
    at(layer).a_end()
    copies = [to_low, to_high, corner_high, corner_low, *share, *scatter.copies]
    wait_all([], copies + [copy for group in hops for _, _, copy in group])


def sum_vectors(r, at, links):
    vector = r.vector
    vector[...] = jnp.zeros_like(vector)
    col = lax.axis_index(COL)
    lanes = r.d_gain_ffn0.shape[1] // HEAD
    heads = r.d_bias_query0.shape[1] // HEAD
    each = vector.shape[0] // 2
    for layer in range(2):
        of = r.of(layer)
        for gain, first in ((of.d_gain_attn, 0), (of.d_gain_ffn, lanes)):
            for i in range(lanes):
                vector[pl.ds(layer * each + first + i, 1)] = gain[:, i * HEAD : (i + 1) * HEAD]
        for i in range(heads):
            place = layer * each + 2 * lanes + col * heads + i
            vector[pl.ds(place, 1)] = of.d_bias_query[:, i * HEAD : (i + 1) * HEAD]
        for i in range(2):
            place = layer * each + 3 * lanes + i * KV + (col >> 1)
            vector[pl.ds(place, 1)] = of.d_bias_pair[:, i * HEAD : (i + 1) * HEAD]
    ways = [SECTION, COL_LOW, COL_HIGH] + [(ROW, 1 << bit) for bit in range(row_bits())]
    copies = []
    for i, way in enumerate(ways):
        r.vector_out[i] = vector[...]
        copies.append(links.copy(r.vector_out.at[i], r.vector_in.at[i], way))
        copies[-1].start()
        at(i).s_step()
        copies[-1].wait_recv()
        vector[...] = vector[...] + r.vector_in[i]
    r.sums[...] = vector[...]
    wait_all([], copies)


class Sizes:
    def __init__(self, n, width, rows, hidden, attn, depth):
        self.n, self.width, self.rows, self.depth = n, width, rows, depth
        self.unit, self.hidden, self.attn = hidden // 2, padded(hidden), attn
        self.heads_width = (attn - 2 * HEAD) // 2
        self.heads = self.heads_width // HEAD


def common_scratch(sizes):
    n, width = sizes.n, sizes.width
    return dict(
        partial=pltpu.VMEM((4, n, width), F32),
        corner_out=pltpu.VMEM((2, n // 2, width), BF16),
        edge_out=pltpu.VMEM((2, n, width), BF16),
        **stage_of(sizes),
    )


def ffn_scratch(sizes, count, saves):
    n, width, hidden = sizes.n, sizes.width, sizes.hidden
    each = 2 * sizes.rows
    return dict(
        w_gate=pltpu.VMEM((hidden, width), BF16),
        w_up=pltpu.VMEM((hidden, width), BF16),
        w_down=pltpu.VMEM((hidden, width), BF16),
        hidden=[pltpu.VMEM((8 * n, hidden), BF16) for _ in range(count)],
        side_out=pltpu.VMEM((4, n, width), BF16),
        f_load_sems=semaphores(each, each, each),
        f_extra_sem=pltpu.SemaphoreType.DMA((3,)),
        f_save_sem=pltpu.SemaphoreType.DMA((4 * saves,)),
    )


def ffn_buffers(sizes, layer):
    n, width = sizes.n, sizes.width
    return layered(
        layer,
        f_blocks=pltpu.VMEM((4, 2, n, width), BF16),
        side_in=pltpu.VMEM((4, n, width), BF16),
        f_corner_in=pltpu.VMEM((2, n // 2, width), BF16),
        f_edge_in=pltpu.VMEM((2, n, width), BF16),
        f_sems=semaphores(16, 16),
    )


def attention_scratch(sizes):
    tokens = 2 * sizes.n
    return dict(
        w_attn=pltpu.VMEM((sizes.attn, sizes.width), BF16),
        bias=pltpu.VMEM((sizes.rows * tokens, tokens), F32),
        a_load_sem=pltpu.SemaphoreType.DMA((2 * sizes.rows,)),
        a_save_sem=pltpu.SemaphoreType.DMA((3,)),
    )


def attention_buffers(sizes, layer, backward):
    n, width, rows = sizes.n, sizes.width, sizes.rows
    pairs = (2, rows, 2 * n, 2 * HEAD)
    count = 10 + 2 * (rows - 1)
    buffers = dict(
        a_corner_in=pltpu.VMEM((2, n // 2, width), BF16),
        a_edge_in=pltpu.VMEM((2, n, width), BF16),
        a_sems=semaphores(count, count),
    )
    if backward:
        buffers.update(a_blocks=pltpu.VMEM((4, n, width), BF16))
        buffers.update(d_kv_in=pltpu.VMEM(pairs, BF16))
        buffers.update(share_in=pltpu.VMEM((2, n, 2 * HEAD), BF16))
    else:
        buffers.update(kv=pltpu.VMEM(pairs, BF16))
    return layered(layer, **buffers)


def attention_back_scratch(sizes):
    n, rows = sizes.n, sizes.rows
    pairs = (2, rows, 2 * n, 2 * HEAD)
    return dict(
        **attention_scratch(sizes),
        d_mixed=pltpu.VMEM((4 * n, sizes.heads_width), BF16),
        d_kv=pltpu.VMEM(pairs, F32),
        d_kv_out=pltpu.VMEM(pairs, BF16),
        share_out=pltpu.VMEM((2, n, 2 * HEAD), BF16),
        d_query=pltpu.VMEM((4 * n, sizes.heads_width), BF16),
        d_pair=pltpu.VMEM((2 * n, 2 * HEAD), BF16),
        a_grad=pltpu.VMEM((sizes.attn, sizes.width), BF16),
    )


def small_outs(sizes, layer):
    return layered(
        layer,
        d_gain_attn=((1, sizes.width), F32, True),
        d_bias_query=((1, sizes.heads_width), F32, True),
        d_bias_pair=((1, 2 * HEAD), F32, True),
    )


def exchange_halves(parts, section):
    return pick(parts, section), swap(pick(parts, 1 - section), *SECTION)


def of_layer(layer, parts, section, token):
    own, other = parts
    return jnp.where(section + token == layer, own, other)


def to_owner(first, second, section):
    keep = jnp.where(section == 0, first, second)
    away = jnp.where(section == 0, second, first)
    other = swap(away, *SECTION)
    return jnp.where(section == 0, keep, other), jnp.where(section == 0, other, keep)


def local(
    tokens,
    cotangent,
    lengths,
    norm_attn,
    w_query,
    b_query,
    w_keyval,
    b_keyval,
    w_out,
    norm_ffn,
    w_gate,
    w_up,
    w_down,
):
    section = lax.axis_index(SEC)
    row = lax.axis_index(ROW)
    col = lax.axis_index(COL)
    rows = lax.axis_size(ROW)
    cols = lax.axis_size(COL)
    low, high = bit_of(col, 0), bit_of(col, 1)
    place = (section, row, low, high)
    row_count = tokens.shape[1]
    width = tokens.shape[2]
    half = row_count // 2
    depth = w_query.shape[1]
    heads_width = w_query.shape[2]

    def blocks_of(array):
        return jnp.concatenate(
            [
                lax.dynamic_slice(
                    array, (2 * section + (high ^ j), (low ^ k) * half, 0), (1, half, width)
                )
                for j in range(2)
                for k in range(2)
            ]
        )

    small = jnp.concatenate([norm_attn[0], norm_ffn[0], b_keyval[0], b_query[0]])
    small = (small, swap(small, *SECTION))
    small = [of_layer(layer, small, section, 0).astype(F32) for layer in range(2)]

    pair_cols = w_keyval[0].reshape(-1, 2, KV, HEAD)
    mine = pick(pair_cols, high, 2).reshape(-1, 2 * HEAD)
    away = pick(pair_cols, 1 - high, 2).reshape(-1, 2 * HEAD)
    pair_rows = ordered(mine[None, None], swap(away, *COL_HIGH)[None, None], high, 0)
    pair_rows = ordered(pair_rows, swap(pair_rows, *COL_LOW), low, 1)
    pair_rows = pair_rows.reshape(depth, 2 * HEAD)
    attn_own = jnp.concatenate([w_query[0].T, w_out[0], pair_rows.T])
    attn_halves = exchange_halves(attn_own.reshape(2, -1, depth), section)

    def ffn_parts(shard):
        hidden = shard.shape[0]
        parts = shard.reshape(2, 2, hidden // 4, shard.shape[1]).transpose(1, 0, 2, 3)
        return exchange_halves(parts, section)

    parts = [ffn_parts(shard) for shard in (w_gate[0].T, w_up[0].T, w_down[0])]
    ways = [(COL_LOW, COL_HIGH), (COL_HIGH, COL_LOW)]

    hidden = w_gate.shape[2] // 2

    tables = layout(lengths, place, row_count)
    sizes = Sizes(half, width, rows, hidden, 2 * attn_halves[0].shape[0], depth)
    entry = blocks_of(tokens)

    ffn_ways = [way for way, _ in ways]
    across = [way for _, way in ways]
    cosine, sine, start, own_index, key_index = tables
    shared = dict(
        cos=(cosine, True),
        sin=(sine, True),
        start=(start, True),
        own=(own_index, True),
        key=(key_index, True),
    )
    gains_attn, gains_ffn, vectors = [], [], []
    for layer in range(2):
        bias_pair = small[layer][2 * width : 2 * width + 2 * KV * HEAD].reshape(2, KV, HEAD)
        gains_attn.append(layered(layer, gain_attn=(small[layer][None, :width], True)))
        gains_ffn.append(layered(layer, gain_ffn=(small[layer][None, width : 2 * width], True)))
        vectors.append(
            layered(
                layer,
                b_query=(small[layer][None, 2 * width + 2 * KV * HEAD :], True),
                b_pair=(pick(bias_pair, high, 1).reshape(1, -1), True),
            )
        )
    chip_ways = [COL_LOW, COL_HIGH, SECTION] + [(ROW, 1 << bit) for bit in range(row_bits())]

    attn_moves = [AttnGather(of_layer(layer, attn_halves, section, 0)) for layer in range(2)]
    ffn_moves = [
        [FfnGather(of_layer(layer, parts[kind], section, 0), across[layer]) for kind in range(3)]
        for layer in range(2)
    ]
    grad_own = lax.dynamic_slice(
        cotangent, (2 * section + high, low * half, 0), (1, half, width)
    )[0]
    grad_move = TokenGather(grad_own, grad_own.shape, ffn_ways[1], ROW_LOW, True)
    (attn_a, attn_b), ((gate_a, up_a, down_a), (gate_b, up_b, down_b)) = attn_moves, ffn_moves
    some, rest = rows // 2, rows - rows // 2
    schedule = dict(
        a0_begin=[attn_a],
        a0_normed=[attn_a, gate_a, gate_a, attn_a],
        a0_queries=[gate_a] * rows,
        a0_relayed=[up_a, up_a, down_a, down_a],
        a0_head0=[up_a] * some,
        a0_head1=[up_a] * rest,
        f0_sent=[down_a] * some + [attn_b],
        f0_gathered=[gate_a] + [down_a] * rest + [up_a],
        f0_up=[down_a, attn_b],
        f0_edges=[gate_b, gate_b],
        f0_end=[attn_b],
        a1_queries=[gate_b] * rows,
        a1_relayed=[up_b, up_b, down_b, down_b],
        a1_head0=[up_b] * some,
        a1_head1=[up_b] * rest,
        f1_sent=[down_b] * some,
        f1_gathered=[gate_b] + [down_b] * rest + [up_b, grad_move],
        f1_up=[down_b, grad_move],
        f1_edges=[grad_move],
    )

    def forward_kernel(r, at):
        for layer in range(2):
            attention_forward(r, layer, at, attn_moves[layer])
            ffn_forward(r, layer, ffn_ways[layer], at, ffn_moves[layer])

    tokens_here = 4 * half
    outs = dict(entry_hbm1=((half, width), BF16, False), result1=((half, width), F32, True))
    buffers = dict(
        entry1=pltpu.VMEM((4, half, width), BF16), result0=pltpu.VMEM((half, width), F32)
    )
    units = ((8 * half, sizes.hidden), BF16, False)
    for layer in range(2):
        outs.update(
            layered(
                layer,
                second=((half, width), F32, True),
                normed=((tokens_here, width), BF16, True),
                query=((tokens_here, heads_width), BF16, True),
                mixed=((tokens_here, heads_width), BF16, True),
                lse=((2, sizes.heads, 2 * half), F32, True),
                kv_hbm=((2, rows, 2 * half, 2 * HEAD), BF16, False),
                f_blocks_hbm=((4, 2, half, width), BF16, False),
                gate=units,
                up=units,
                act=units,
            )
        )
        buffers.update(ffn_buffers(sizes, layer))
        buffers.update(attention_buffers(sizes, layer, False))
    done = kernel_call(
        forward_kernel,
        0,
        chip_ways,
        dict(
            entry0=(entry, True),
            **shared,
            **gains_attn[0],
            **gains_attn[1],
            **gains_ffn[0],
            **gains_ffn[1],
            **vectors[0],
            **vectors[1],
        ),
        outs,
        {**common_scratch(sizes), **ffn_scratch(sizes, 3, 4), **attention_scratch(sizes), **buffers},
        1 << 34,
        [*attn_moves, *ffn_moves[0], *ffn_moves[1], grad_move],
        schedule,
    )
    (grad_all,) = grad_move.results
    last_result = done.result1.astype(BF16)

    def grad_of(left, right):
        return dot(left, right.reshape(-1, width), 0, 0).astype(BF16)

    unit = sizes.unit

    def blocked(grad, arrived):
        total = (grad[:unit].astype(F32) + arrived.astype(F32)).astype(BF16)
        return jnp.stack([total[:, i * depth : (i + 1) * depth] for i in range(rows)])

    def ffn_back_operands(layer):
        of = done.of(layer)
        (gate, gate_far), (up, up_far), (down, down_far) = (move.results for move in ffn_moves[layer])
        return {
            **gains_ffn[layer],
            **layered(
                layer,
                second=(of.second, True),
                gate=(of.gate, False),
                up=(of.up, False),
                gate_own=(gate, False),
                gate_other=(gate_far, False),
                up_own=(up, False),
                up_other=(up_far, False),
                down_own=(down, False),
                down_other=(down_far, False),
            ),
        }

    def ffn_back_outs(layer):
        return layered(
            layer,
            d_second=((half, width), F32, True),
            d_gain_ffn=((1, width), F32, True),
            d_gate=units,
            d_up=units,
        )

    def attention_back_operands(layer, own):
        of = done.of(layer)
        return {
            **gains_attn[layer],
            **shared,
            **layered(
                layer,
                entry=(own, True),
                attn_blocks=(attn_moves[layer].results[0], False),
                kv=(of.kv_hbm, True),
                normed=(of.normed, True),
                query=(of.query, True),
                mixed=(of.mixed, True),
                lse=(of.lse, True),
            ),
        }

    down_grad = grad_of(done.act1, grad_all)
    down_move = Across(down_grad, unit, across[1])
    back = kernel_call(
        lambda r, at: ffn_backward(r, 1, ffn_ways[1], at, False, ffn_backward_loads(r, 1, False)),
        1,
        [ffn_ways[1], ROW_LOW, SECTION],
        dict(d_entry2=(grad_own, True), gathered1=(grad_all, False), **ffn_back_operands(1)),
        ffn_back_outs(1),
        {**common_scratch(sizes), **ffn_scratch(sizes, 2, 2), **ffn_buffers(sizes, 1)},
        1 << 33,
        [down_move],
        dict(f1_sent=[down_move]),
    )
    gate_grad = grad_of(back.d_gate1, done.f_blocks_hbm1)
    up_grad = grad_of(back.d_up1, done.f_blocks_hbm1)
    down_one = blocked(down_grad, down_move.results[0])

    down_rows = Rows(down_one)
    gate_move = GradScatter(gate_grad, unit, across[1])
    up_move = Across(up_grad, unit, across[1])
    last_move = ColumnGather(last_result, last_result.shape)
    entry_move = ColumnGather("d_entry1", (half, width))
    attn_move_one = AttnScatter("a_grad", (sizes.attn, width))

    def middle_kernel(r, at):
        loads = ffn_backward_loads(r, 0, True)
        attention_backward(r, 1, at)
        ffn_backward(r, 0, ffn_ways[0], at, True, loads)

    middle = kernel_call(
        middle_kernel,
        2,
        chip_ways,
        dict(
            d_second1=(back.d_second1, True),
            **attention_back_operands(1, done.entry_hbm1),
            **ffn_back_operands(0),
        ),
        dict(
            d_entry1=((half, width), BF16, True),
            f_blocks_hbm0=((4, 2, half, width), BF16, False),
            **small_outs(sizes, 1),
            **ffn_back_outs(0),
        ),
        {
            **common_scratch(sizes),
            **attention_back_scratch(sizes),
            **attention_buffers(sizes, 1, True),
            **ffn_scratch(sizes, 2, 3),
            **ffn_buffers(sizes, 0),
        },
        1 << 33,
        [down_rows, gate_move, up_move, last_move, entry_move, attn_move_one],
        dict(
            a1_relayed=[down_rows, gate_move],
            a1_grads=[attn_move_one],
            f0_edges=[gate_move, up_move, attn_move_one, last_move, entry_move],
        ),
    )
    up_one = blocked(up_grad, up_move.results[0])
    zero_grads = [
        grad_of(done.act0, middle.f_blocks_hbm0),
        grad_of(middle.d_gate0, done.f_blocks_hbm0),
        grad_of(middle.d_up0, done.f_blocks_hbm0),
    ]

    up_rows = Rows(up_one)
    zero_moves = [GradScatter(grad, unit, across[0]) for grad in zero_grads]
    attn_move_zero = AttnScatter("a_grad", (sizes.attn, width))
    first_move = ColumnGather("d_entry0", (half, width))
    result_move = ColumnGather(done.entry_hbm1, (half, width))
    sum_rows = 2 * (3 * width // HEAD + 2 * KV)
    sum_ways = 3 + row_bits()

    def last_kernel(r, at):
        attention_backward(r, 0, at)
        sum_vectors(r, at, Links(r.sum_sems))

    down_zero, gate_zero, up_zero = zero_moves
    final = kernel_call(
        last_kernel,
        3,
        chip_ways,
        dict(
            d_second0=(middle.d_second0, True),
            d_gain_ffn0=(middle.d_gain_ffn0, True),
            d_gain_ffn1=(back.d_gain_ffn1, True),
            **attention_back_operands(0, entry[0]),
            **{name: (middle.named[name], True) for name in small_outs(sizes, 1)},
        ),
        dict(d_entry0=((half, width), BF16, True), sums=((sum_rows, HEAD), F32, True)),
        {
            **common_scratch(sizes),
            **attention_back_scratch(sizes),
            **attention_buffers(sizes, 0, True),
            **{name: pltpu.VMEM(shape, F32) for name, (shape, _, _) in small_outs(sizes, 0).items()},
            **dict(
                vector=pltpu.VMEM((sum_rows, HEAD), F32),
                vector_out=pltpu.VMEM((sum_ways, sum_rows, HEAD), F32),
                vector_in=pltpu.VMEM((sum_ways, sum_rows, HEAD), F32),
                sum_sems=semaphores(sum_ways, sum_ways),
            ),
        },
        1 << 32,
        [up_rows, *zero_moves, attn_move_zero, first_move, result_move],
        dict(
            a0_relayed=[down_zero],
            a0_hops=[up_rows, result_move],
            a0_edges=[gate_zero, up_zero],
            a0_grads=[down_zero, attn_move_zero, result_move],
            a0_end=[attn_move_zero, gate_zero, first_move],
            s1_step=[attn_move_zero],
            s2_step=[first_move],
            s3_step=[attn_move_zero],
        ),
    )

    def by_row_bit(own, arrived):
        near, far = own.astype(F32), 0.0
        for flip in range(1, rows):
            if flip & 1:
                far = far + arrived[flip].astype(F32)
            else:
                near = near + arrived[flip].astype(F32)
        return ordered(near.astype(BF16)[None], far.astype(BF16)[None], row & 1, 0)

    ffn_grads = [
        [by_row_bit(*move.results) for move in (gate_zero, up_zero, down_zero)],
        [
            by_row_bit(*gate_move.results),
            by_row_bit(pick(up_one, row), up_rows.results[0]),
            by_row_bit(pick(down_one, row), down_rows.results[0]),
        ],
    ]
    sums = final.sums.reshape(2, -1)
    sums = jnp.where(section == 0, sums[0], sums[1])
    grad_norm_attn = sums[:width]
    grad_norm_ffn = sums[width : 2 * width]
    spread = sums[2 * width : 2 * width + cols * heads_width].reshape(cols, -1)
    grad_b_query = pick(spread, col)
    grad_b_keyval = sums[2 * width + cols * heads_width :]
    (first_result,), (last_blocks,) = result_move.results, last_move.results
    (grad_one_blocks,), (grad_zero_blocks,) = entry_move.results, first_move.results
    (attn_one_half,), (attn_zero_half,) = attn_move_one.results, attn_move_zero.results

    def assemble(first, second):
        shape = (2, row_count, width)
        zeroth, later = to_owner(first.reshape(shape), second.reshape(shape), section)
        return jnp.concatenate([zeroth, later])[None]

    outputs = assemble(first_result, last_blocks)
    grads_in = assemble(grad_zero_blocks, grad_one_blocks)

    def ffn_grad(kind):
        zeroth, later = to_owner(ffn_grads[0][kind], ffn_grads[1][kind], section)
        whole = jnp.stack([zeroth, later], axis=1)
        return whole.reshape(-1, whole.shape[-1])

    grad_gate = ffn_grad(0).T.astype(F32)
    grad_up = ffn_grad(1).T.astype(F32)
    grad_down = ffn_grad(2).astype(F32)

    total = jnp.concatenate(to_owner(attn_zero_half, attn_one_half, section)).astype(F32)
    grad_query = total[:heads_width].T
    grad_out = total[heads_width : 2 * heads_width]
    pair = total[2 * heads_width :].T.reshape(2, 2, depth // 4, 2 * HEAD)
    pair = pick(pair, low, 1) + swap(pick(pair, 1 - low, 1).astype(BF16), *COL_LOW).astype(F32)
    pair = pair.astype(BF16)
    pair = ordered(
        pick(pair, high)[:, None], swap(pick(pair, 1 - high), *COL_HIGH)[:, None], high, 1
    )
    grad_keyval = (
        pair.reshape(-1, 2, 2, HEAD).transpose(0, 2, 1, 3).reshape(-1, 2 * KV * HEAD).astype(F32)
    )

    return (
        outputs,
        grads_in,
        grad_norm_attn[None],
        grad_query[None],
        grad_b_query[None],
        grad_keyval[None],
        grad_b_keyval[None],
        grad_out[None],
        grad_norm_ffn[None],
        grad_gate[None],
        grad_up[None],
        grad_down[None],
    )


def solution(mesh):
    in_specs = (
        P(None, ROW, None),
        P(None, ROW, None),
        P(),
        P(SEC, None),
        P(SEC, ROW, COL),
        P(SEC, COL),
        P(SEC, (ROW, COL), None),
        P(SEC, None),
        P(SEC, COL, ROW),
        P(SEC, None),
        P(SEC, ROW, COL),
        P(SEC, ROW, COL),
        P(SEC, COL, ROW),
    )
    out_specs = (
        P(SEC, None, ROW, None),
        P(SEC, None, ROW, None),
        P(SEC, None),
        P(SEC, ROW, COL),
        P(SEC, COL),
        P(SEC, (ROW, COL), None),
        P(SEC, None),
        P(SEC, COL, ROW),
        P(SEC, None),
        P(SEC, ROW, COL),
        P(SEC, ROW, COL),
        P(SEC, COL, ROW),
    )
    return jax.shard_map(local, mesh=mesh, in_specs=in_specs, out_specs=out_specs, check_vma=False)
```

```python
import functools
import math

import jax
import jax.numpy as jnp
from jax import lax
from jax.experimental import pallas as pl
from jax.experimental.pallas import tpu as pltpu
from jax.sharding import PartitionSpec as P

HEADS = 12
KV = 2
HEAD = 128

EPS = 1e-06
THETA = 1000000.0

ROW, SEC, COL = "row", "section", "col"

F32 = jnp.float32
BF16 = jnp.bfloat16

COL_LOW = (COL, 1)
COL_HIGH = (COL, 2)
ROW_LOW = (ROW, 1)
SECTION = (SEC, 1)


def swap(value, axis, flip):
    pairs = [(i, i ^ flip) for i in range(lax.axis_size(axis))]
    return lax.ppermute(value, axis, pairs)


def bit_of(index, bit):
    return (index >> bit) & 1


def pick(array, index, axis=0):
    return lax.dynamic_index_in_dim(array, index, axis, keepdims=False)


def ordered(mine, other, bit, axis):
    first = jnp.where(bit == 0, mine, other)
    second = jnp.where(bit == 0, other, mine)
    return jnp.concatenate([first, second], axis=axis)


def row_bits():
    return lax.axis_size(ROW).bit_length() - 1


def norm_backward(stream, inverse, gain, gradient):
    inner = jnp.mean(gradient * gain * stream, axis=-1, keepdims=True)
    d_stream = gain * gradient * inverse - stream * (inverse * inverse * inverse) * inner
    return (d_stream, jnp.sum(gradient * stream * inverse, axis=0, keepdims=True))


def dot(left, right, left_dim, right_dim):
    return lax.dot_general(
        left, right, (((left_dim,), (right_dim,)), ((), ())), preferred_element_type=F32
    )


def layout(lengths, place, row_count):
    section, row, low, high = place
    rows = lax.axis_size(ROW)
    half = row_count // 2
    inside = jnp.arange(row_count, dtype=jnp.int32)
    inside = (((inside // half) ^ low) * half) + inside % half
    own_index = row * row_count + inside
    key_index = ((jnp.arange(rows, dtype=jnp.int32) ^ row) * row_count)[:, None] + inside[None, :]
    slots = 2 * section + (jnp.arange(2, dtype=jnp.int32) ^ high)
    picked = jnp.stack([pick(lengths, slots[0]), pick(lengths, slots[1])])
    ends = jnp.cumsum(picked, axis=1)
    starts = ends - picked
    inside_piece = (own_index[None, None, :] >= starts[:, :, None]) & (
        own_index[None, None, :] < ends[:, :, None]
    )
    first = jnp.sum(jnp.where(inside_piece, starts[:, :, None], 0), axis=1)
    inverse = THETA ** (-(jnp.arange(HEAD // 2, dtype=F32) * 2.0 / HEAD))
    angle = (own_index[None, :] - first).astype(F32).reshape(-1, 1) * inverse
    cosine, sine = jnp.cos(angle), jnp.sin(angle)
    return (
        jnp.concatenate([cosine, cosine], axis=1),
        jnp.concatenate([-sine, sine], axis=1),
        first,
        own_index[None, :],
        key_index.reshape(-1, 1),
    )


MESH = pl.DeviceIdType.MESH
VMEM_LIMIT = 62 * 1024 * 1024


def partner_of(way):
    axis, flip = way
    return {axis: lax.axis_index(axis) ^ flip}


def enter(ways):
    barrier = pltpu.get_barrier_semaphore()
    for way in ways:
        pl.semaphore_signal(barrier, inc=1, device_id=partner_of(way), device_id_type=MESH)
    pl.semaphore_wait(barrier, len(ways))


def remote(source, target, send, recv, way):
    return pltpu.make_async_remote_copy(
        src_ref=source,
        dst_ref=target,
        send_sem=send,
        recv_sem=recv,
        device_id=partner_of(way),
        device_id_type=MESH,
    )


class Links:
    def __init__(self, sems):
        self.send, self.recv = sems
        self.used = 0

    def copy(self, source, target, way):
        slot = self.used
        self.used += 1
        return remote(source, target, self.send.at[slot], self.recv.at[slot], way)


def semaphores(*counts):
    return [pltpu.SemaphoreType.DMA((count,)) for count in counts]


def wait_all(arriving, leaving):
    for copy in arriving:
        copy.wait_recv()
    for copy in leaving:
        copy.wait_send()


class Refs:
    def __init__(self, named, layer=None):
        self.named, self.layer = named, layer

    def __getattr__(self, name):
        return self.named[name] if name in self.named else self.named[name + str(self.layer)]

    def of(self, layer):
        return Refs(self.named, layer)


def layered(layer, **values):
    return {name + str(layer): value for name, value in values.items()}


class Pump:
    def __init__(self, schedule, number=None):
        self.schedule, self.number = schedule, number

    def __call__(self, number):
        return Pump(self.schedule, number)

    def __getattr__(self, point):
        def run():
            for move in self.schedule.get(point[0] + str(self.number) + point[1:], ()):
                move.advance()

        return run


def kernel_call(kernel, collective_id, ways, operands, outs, scratch, flops, moves, schedule):
    vmem = pl.BlockSpec(memory_space=pltpu.VMEM)
    hbm = pl.BlockSpec(memory_space=pl.ANY)
    moved_in = [array for move in moves for array in move.operands]
    moved_out = [out for move in moves for out in move.outs]
    every = list(ways)
    for move in moves:
        every += [way for way in move.ways if way not in every]
    scratch_list = []
    for spec in scratch.values():
        scratch_list += spec if isinstance(spec, list) else [spec]

    def body(*refs):
        refs = list(refs)

        def take(count):
            taken, refs[:] = refs[:count], refs[count:]
            return taken

        named = dict(zip(operands, take(len(operands))))
        sources = [take(len(move.operands)) for move in moves]
        named.update(zip(outs, take(len(outs))))
        targets = [take(len(move.outs)) for move in moves]
        for name, spec in scratch.items():
            named[name] = take(len(spec)) if isinstance(spec, list) else take(1)[0]
        for move, source, target in zip(moves, sources, targets, strict=True):
            if move.name:
                source = [named[move.name]]
            move.bind(source, target, take(len(move.scratch)))

        enter(every)
        kernel(Refs(named), Pump(schedule))
        while any(move.at < len(move.steps) for move in moves):
            for move in moves:
                move.advance()

    results = pl.pallas_call(
        body,
        out_shape=[jax.ShapeDtypeStruct(shape, dtype) for shape, dtype, _ in outs.values()]
        + [jax.ShapeDtypeStruct(shape, BF16) for shape in moved_out],
        in_specs=[vmem if inside else hbm for _, inside in operands.values()] + [hbm] * len(moved_in),
        out_specs=[vmem if inside else hbm for _, _, inside in outs.values()] + [hbm] * len(moved_out),
        scratch_shapes=scratch_list + [ref for move in moves for ref in move.scratch],
        compiler_params=pltpu.CompilerParams(
            collective_id=collective_id, has_side_effects=True, vmem_limit_bytes=VMEM_LIMIT
        ),
        cost_estimate=pl.CostEstimate(flops=flops, bytes_accessed=32 << 20, transcendentals=1 << 20),
    )(*[array for array, _ in operands.values()], *moved_in)
    moved = results[len(outs) :]
    for move in moves:
        move.results, moved = moved[: len(move.outs)], moved[len(move.outs) :]
    return Refs(dict(zip(outs, results)))


def row_hops(bits):
    hops, known = [], [0]
    for bit in reversed(range(bits)):
        step = 1 << bit
        hops += [(slot, slot | step, bit) for slot in known]
        known += [slot | step for slot in known]
    return hops


class Move:
    def __init__(self, source, outs, scratch, ways):
        self.name = source if isinstance(source, str) else None
        sources = list(source) if isinstance(source, tuple) else [source]
        self.operands = [] if self.name else sources
        self.outs, self.scratch, self.ways = outs, scratch, ways
        self.steps, self.at = [], 0

    def advance(self):
        if self.at < len(self.steps):
            self.steps[self.at]()
            self.at += 1


class FfnGather(Move):
    def __init__(self, layer, parts, across):
        rows, part = lax.axis_size(ROW), parts[0]
        self.layer = layer
        self.flips, self.across = list(range(rows - 1, 0, -1)), across
        outs = [(rows, *part.shape[1:])] * 2
        ways = [(ROW, flip) for flip in self.flips] + [across]
        super().__init__(tuple(parts), outs, semaphores(rows, rows, rows, rows, 1), ways)

    def bind(self, sources, targets, scratch):
        own, other = targets
        self.blocks = [own, other]
        row_send, row_recv, far_send, far_recv, local_sem = scratch
        row = lax.axis_index(ROW)
        is_own = lax.axis_index(SEC) == self.layer

        class Either:
            def __init__(self, make):
                self.made = [make(part) for part in sources]

            def start(self):
                pl.when(is_own)(self.made[0].start)
                pl.when(jnp.logical_not(is_own))(self.made[1].start)

            def wait(self):
                self.made[0].wait()

            def wait_recv(self):
                self.made[0].wait_recv()

            def wait_send(self):
                self.made[0].wait_send()

        def exchange(flip):
            return Either(
                lambda part: remote(
                    part.at[(row ^ flip) & 1], own.at[row], row_send.at[flip], row_recv.at[flip], (ROW, flip)
                )
            )

        local = Either(lambda part: pltpu.make_async_copy(part.at[row & 1], own.at[row], local_sem.at[0]))
        hops = {flip: exchange(flip) for flip in self.flips}
        far = {
            flip: remote(
                own.at[row ^ flip], other.at[row ^ flip], far_send.at[flip], far_recv.at[flip], self.across
            )
            for flip in self.flips
        }
        far[0] = Either(
            lambda part: remote(part.at[row & 1], other.at[row], far_send.at[0], far_recv.at[0], self.across)
        )

        def start():
            local.start()
            hops[self.flips[0]].start()

        def start_rest():
            for flip in self.flips[1:]:
                hops[flip].start()

        def forward(flip):
            def step():
                if flip:
                    hops[flip].wait_recv()
                far[flip].start()

            return step

        def finish():
            local.wait()
            wait_all(far.values(), [*hops.values(), *far.values()])

        self.steps = [start, start_rest, *[forward(flip) for flip in [0] + self.flips], finish]


class AttnGather(Move):
    def __init__(self, part):
        rows = lax.axis_size(ROW)
        self.bits = rows.bit_length() - 1
        ways = [(ROW, 1 << bit) for bit in range(self.bits)] + [SECTION]
        super().__init__(part, [(2, rows, *part.shape)], semaphores(rows, rows, rows, rows, 1), ways)

    def bind(self, sources, targets, scratch):
        (part,), (blocks,) = sources, targets
        self.blocks = [blocks.at[0], blocks.at[1]]
        row_send, row_recv, side_send, side_recv, local_sem = scratch
        section, row = lax.axis_index(SEC), lax.axis_index(ROW)

        def place(slot):
            return blocks.at[section, row ^ slot]

        def source(slot):
            return place(slot) if slot else part

        local = pltpu.make_async_copy(part, place(0), local_sem.at[0])
        hops = [
            (slot, filled, remote(source(slot), place(slot), row_send.at[filled], row_recv.at[filled], (ROW, 1 << bit)))
            for slot, filled, bit in row_hops(self.bits)
        ]
        sides = [
            remote(source(slot), place(slot), side_send.at[slot], side_recv.at[slot], SECTION)
            for slot in range(1 << self.bits)
        ]
        arrived = {0}

        def arrive(slot):
            if slot not in arrived:
                arrived.add(slot)
                for _, filled, copy in hops:
                    if filled == slot:
                        copy.wait_recv()
                sides[slot].start()

        def start():
            local.start()
            for slot, _, copy in hops:
                if slot == 0:
                    copy.start()
            sides[0].start()

        def forward():
            for slot, _, copy in hops:
                if slot:
                    arrive(slot)
                    copy.start()

        def finish():
            for slot in range(len(sides)):
                arrive(slot)
            local.wait()
            wait_all(sides, [copy for _, _, copy in hops] + sides)

        self.steps = [start, forward, finish]


class ColumnGather(Move):
    def __init__(self, own, shape):
        super().__init__(own, [(4, *shape)], semaphores(8, 8, 1), [COL_LOW, COL_HIGH])

    def bind(self, sources, targets, scratch):
        (own,), (blocks,) = sources, targets
        send, recv, local_sem = scratch
        col = lax.axis_index(COL)
        h = own.shape[0] // 2
        links = Links((send, recv))
        place = blocks.at[col]
        local = pltpu.make_async_copy(own, place, local_sem.at[0])
        first = [links.copy(own, place, COL_LOW), links.copy(own, place, COL_HIGH)]
        top = blocks.at[col ^ COL_LOW[1], pl.ds(0, h)]
        bottom = blocks.at[col ^ COL_HIGH[1], pl.ds(h, h)]
        second = [links.copy(top, top, COL_HIGH), links.copy(bottom, bottom, COL_LOW)]

        def start():
            local.start()
            for copy in first:
                copy.start()

        def forward():
            for arrived, copy in zip(first, second, strict=True):
                arrived.wait_recv()
                copy.start()

        def finish():
            local.wait()
            wait_all(second, first + second)

        self.steps = [start, forward, finish]


class TokenGather(Move):
    def __init__(self, own, shape, a, b, sides):
        self.a, self.b, self.sides = a, b, sides
        ways = [a, b] + ([SECTION] if sides else [])
        super().__init__(own, [(4, 1 + sides, *shape)], semaphores(8, 8, 1), ways)

    def bind(self, sources, targets, scratch):
        (own,), (blocks,) = sources, targets
        send, recv, local_sem = scratch
        local = pltpu.make_async_copy(own, blocks.at[0, 0], local_sem.at[0])
        gather = BlockGather(Links((send, recv)), blocks, self.a, self.b, self.sides, own)

        def start():
            local.start()
            for copy in (gather.a, gather.b, gather.sides[0]):
                copy.start()

        def forward():
            gather.a.wait_recv()
            gather.ab.start()
            gather.sides[1].start()
            gather.b.wait_recv()
            gather.ba.start()
            gather.sides[2].start()

        def last():
            gather.ab.wait_recv()
            gather.ba.wait_recv()
            gather.sides[3].start()

        def finish():
            local.wait()
            wait_all(gather.sides, gather.copies)

        self.steps = [start, forward, last, finish]


class Across(Move):
    def __init__(self, grad, n, way):
        self.n, self.way = n, way
        super().__init__(grad, [(n, grad.shape[1])], semaphores(1, 1), [way])

    def bind(self, sources, targets, scratch):
        (grad,), (arrived,) = sources, targets
        send, recv = scratch
        copy = remote(grad.at[pl.ds(self.n, self.n)], arrived, send.at[0], recv.at[0], self.way)
        self.steps = [copy.start, lambda: wait_all([copy], [copy])]


class Rows(Move):
    def __init__(self, total):
        rows = total.shape[0]
        self.flips = list(range(1, rows))
        ways = [(ROW, flip) for flip in self.flips]
        super().__init__(total, [total.shape], semaphores(rows, rows), ways)

    def bind(self, sources, targets, scratch):
        (total,), (arrived,) = sources, targets
        send, recv = scratch
        copies = row_copies(total, arrived, send, recv, self.flips)

        def start():
            for copy in copies:
                copy.start()

        self.steps = [start, lambda: wait_all(copies, copies)]


def row_copies(total, arrived, send, recv, flips):
    row = lax.axis_index(ROW)
    return [
        remote(total.at[row ^ flip], arrived.at[flip], send.at[flip], recv.at[flip], (ROW, flip))
        for flip in flips
    ]


class GradScatter(Move):
    def __init__(self, grad, n, way):
        rows, width = lax.axis_size(ROW), grad.shape[1]
        self.n, self.way, self.flips = n, way, list(range(1, rows))
        shape = (rows, n, width // rows)
        scratch = [pltpu.VMEM((n, width), BF16), pltpu.VMEM((n, width), BF16), pltpu.VMEM(shape, BF16)]
        scratch += semaphores(1, 1, 1, 1, rows, rows)
        ways = [way] + [(ROW, flip) for flip in self.flips]
        super().__init__(grad, [shape[1:], shape], scratch, ways)

    def bind(self, sources, targets, scratch):
        (grad,), (own, arrived) = sources, targets
        mine, theirs, total, local_sem, own_sem, far_send, far_recv, row_send, row_recv = scratch
        n, row = self.n, lax.axis_index(ROW)
        depth = total.shape[2]
        local = pltpu.make_async_copy(grad.at[pl.ds(0, n)], mine, local_sem.at[0])
        far = remote(grad.at[pl.ds(n, n)], theirs, far_send.at[0], far_recv.at[0], self.way)
        keep = pltpu.make_async_copy(total.at[row], own, own_sem.at[0])
        copies = row_copies(total, arrived, row_send, row_recv, self.flips)

        def start():
            local.start()
            far.start()

        def forward():
            local.wait()
            far.wait_recv()
            for block in range(total.shape[0]):
                at = slice(block * depth, (block + 1) * depth)
                total[block] = (mine[:, at].astype(F32) + theirs[:, at].astype(F32)).astype(BF16)
            for copy in copies + [keep]:
                copy.start()

        def finish():
            keep.wait()
            wait_all(copies, copies + [far])

        self.steps = [start, forward, finish]


class AttnScatter(Move):
    def __init__(self, name, shape):
        rows, width, m = lax.axis_size(ROW), shape[1], shape[0] // 2
        self.bits, self.m = rows.bit_length() - 1, m
        blocks = (rows, m, width // rows)
        scratch = [
            pltpu.VMEM((m, width), BF16),
            pltpu.VMEM(blocks, F32),
            pltpu.VMEM(blocks, BF16),
            pltpu.VMEM(blocks, BF16),
        ]
        scratch += semaphores(1, 1, 1, rows, rows)
        ways = [SECTION] + [(ROW, 1 << bit) for bit in range(self.bits)]
        super().__init__(name, [blocks[1:]], scratch, ways)

    def bind(self, sources, targets, scratch):
        (grad,), (out,) = sources, targets
        theirs, total, going, coming, out_sem, side_send, side_recv, send, recv = scratch
        m, row, section = self.m, lax.axis_index(ROW), lax.axis_index(SEC)
        depth = total.shape[2]
        mine = grad.at[pl.ds(pl.multiple_of(section * m, m), m)]
        side = remote(
            grad.at[pl.ds(pl.multiple_of((1 - section) * m, m), m)],
            theirs,
            side_send.at[0],
            side_recv.at[0],
            SECTION,
        )
        keep = pltpu.make_async_copy(going.at[0], out, out_sem.at[0])
        hops = [
            (slot, filled, remote(going.at[filled], coming.at[filled], send.at[filled], recv.at[filled], (ROW, 1 << bit)))
            for slot, filled, bit in reversed(row_hops(self.bits))
        ]

        def sum_sides():
            side.wait_recv()
            for block in range(total.shape[0]):
                at = slice(block * depth, (block + 1) * depth)
                total[row ^ block] = mine[:, at].astype(F32) + theirs[:, at].astype(F32)
            send_bit(0)

        def send_bit(bit):
            for slot, filled, copy in hops:
                if filled - slot == 1 << bit:
                    going[filled] = total[filled].astype(BF16)
                    copy.start()

        def add_bit(bit):
            for slot, filled, copy in hops:
                if filled - slot == 1 << bit:
                    copy.wait_recv()
                    total[slot] = total[slot] + coming[filled].astype(F32)

        def hop(bit):
            def step():
                add_bit(bit - 1)
                send_bit(bit)

            return step

        def finish():
            add_bit(self.bits - 1)
            going[0] = total[0].astype(BF16)
            keep.start()
            keep.wait()
            wait_all([], [copy for _, _, copy in hops] + [side])

        self.steps = [side.start, sum_sides, *[hop(bit) for bit in range(1, self.bits)], finish]


class NoCopy:
    def start(self):
        pass

    wait_recv = wait_send = start


class BlockGather:
    def __init__(self, links, blocks, a, b, sides=True, own=None, there=False):
        h = blocks.shape[2] // 2
        own = blocks.at[0, 0] if own is None else own
        if there:
            self.a = self.b = self.ab = self.ba = NoCopy()
        else:
            self.a = links.copy(own, blocks.at[1, 0], a)
            self.b = links.copy(own, blocks.at[2, 0], b)
            self.ab = links.copy(blocks.at[1, 0, pl.ds(0, h)], blocks.at[3, 0, pl.ds(0, h)], b)
            self.ba = links.copy(blocks.at[2, 0, pl.ds(h, h)], blocks.at[3, 0, pl.ds(h, h)], a)
        self.sides = [NoCopy()] * 4
        if sides and not there:
            self.sides = [
                links.copy(blocks.at[k, 0] if k else own, blocks.at[k, 1], SECTION) for k in range(4)
            ]
        self.copies = [self.a, self.b, self.ab, self.ba, *self.sides]


class Scatter:
    def __init__(self, links, r, corner_in, edge_in, a, b):
        self.r, self.corner_in, self.edge_in = r, corner_in, edge_in
        self.corner_b = links.copy(r.corner_out.at[0], corner_in.at[0], b)
        self.corner_a = links.copy(r.corner_out.at[1], corner_in.at[1], a)
        self.edge_a = links.copy(r.edge_out.at[0], edge_in.at[0], a)
        self.edge_b = links.copy(r.edge_out.at[1], edge_in.at[1], b)
        self.copies = [self.corner_b, self.corner_a, self.edge_a, self.edge_b]

    def send_corner(self, value):
        corner = self.r.corner_out
        corner[...] = value.astype(BF16).reshape(corner.shape)
        self.corner_b.start()
        self.corner_a.start()

    def send_edge_a(self, value):
        edge, h = self.r.edge_out, value.shape[0] // 2
        self.corner_b.wait_recv()
        edge[0, :h] = (value[:h] + self.corner_in[0].astype(F32)).astype(BF16)
        edge[0, h:] = value[h:].astype(BF16)
        self.edge_a.start()

    def send_edge_b(self, value):
        edge, h = self.r.edge_out, value.shape[0] // 2
        self.corner_a.wait_recv()
        edge[1, :h] = value[:h].astype(BF16)
        edge[1, h:] = (value[h:] + self.corner_in[1].astype(F32)).astype(BF16)
        self.edge_b.start()

    def total(self, value):
        self.edge_a.wait_recv()
        self.edge_b.wait_recv()
        return value + self.edge_in[0].astype(F32) + self.edge_in[1].astype(F32)


def save(started, sems, pairs):
    for source, target in pairs:
        started.append(pltpu.make_async_copy(source, target, sems.at[len(started)]))
        started[-1].start()


class Load:
    def __init__(self, sources, target, stage, sems):
        self.sources, self.target, self.stage, self.copies, self.sems = sources, target, stage, [], sems
        if stage is None:
            for i, source in enumerate(sources):
                blocks, rows, columns = source.shape
                for block in range(blocks):
                    place = target.at[pl.ds(i * rows, rows), pl.ds(block * columns, columns)]
                    self.copies.append(
                        pltpu.make_async_copy(source.at[block], place, sems.at[len(self.copies)])
                    )

    def start(self):
        for copy in self.copies:
            copy.start()
        filled = sum(source.shape[1] for source in self.sources)
        if filled < self.target.shape[0]:
            self.target[filled:] = jnp.zeros((self.target.shape[0] - filled, self.target.shape[1]), BF16)

    def wait(self):
        for copy in self.copies:
            copy.wait()
        if self.stage is not None:
            for i, source in enumerate(self.sources):
                blocks, rows, columns = source.shape
                buffer = self.stage.at[:, pl.ds(0, rows)]
                copy = pltpu.make_async_copy(source, buffer, self.sems.at[0])
                copy.start()
                copy.wait()
                for block in range(blocks):
                    self.target[i * rows : (i + 1) * rows, block * columns : (block + 1) * columns] = (
                        self.stage[block, :rows]
                    )


def stage_of(sizes):
    if sizes.depth % 128 == 0:
        return {}
    return dict(stage=pltpu.VMEM((sizes.rows, max(sizes.unit, sizes.attn // 2), sizes.depth), BF16))


def stage_in(r):
    return r.named.get("stage")


def hidden_tiles(hidden):
    return [(at, min(384, hidden - at)) for at in range(0, hidden, 384)]


def padded(hidden):
    return -(-hidden // 128) * 128


def width_tiles(width):
    return [(at, 512) for at in range(0, width, 512)]


def put_partial(r, k, at, size, value):
    n = value.shape[0] // 2
    r.partial[k, :, pl.ds(at, size)] = value[:n]
    r.side_out[k, :, pl.ds(at, size)] = value[n:].astype(BF16)


def side_copies(links, r):
    return [links.copy(r.side_out.at[k], r.side_in.at[k], SECTION) for k in range(4)]


def with_side(r, k):
    return r.partial[k] + r.side_in[k].astype(F32)


def ffn_forward(r, layer, a, at, weights):
    r = r.of(layer)
    links = Links(r.f_sems)
    blocks, result_ref, second_ref = r.f_blocks, r.result, r.second
    gate_out, up_out, act_out = r.hidden[0], r.hidden[1], r.hidden[2]
    n, width = blocks.shape[2:]
    hidden = r.w_gate.shape[0]
    second = second_ref[...]
    inverse = lax.rsqrt(jnp.mean(second * second, axis=-1, keepdims=True) + EPS)
    blocks[0, 0] = (second * inverse * r.gain_ffn[...]).astype(BF16)
    gather = BlockGather(links, blocks, a, ROW_LOW)
    sides = side_copies(links, r)
    scatter = Scatter(links, r, r.f_corner_in, r.f_edge_in, a, ROW_LOW)
    gather.a.start()
    gather.b.start()
    gather.sides[0].start()
    at(layer).f_sent()
    gather.a.wait_recv()
    gather.ab.start()
    gather.sides[1].start()
    gather.b.wait_recv()
    gather.ba.start()
    gather.sides[2].start()
    gather.ab.wait_recv()
    gather.ba.wait_recv()
    gather.sides[3].start()
    at(layer).f_gathered()
    stage = stage_in(r)
    loads = [
        Load(move.blocks, weight, stage, sems)
        for move, weight, sems in zip(weights, (r.w_gate, r.w_up, r.w_down), r.f_load_sems, strict=True)
    ]
    loads[0].start()
    loads[1].start()
    loads[0].wait()
    loads[1].wait()
    saves = []
    for k in range(4):
        gather.sides[k].wait_recv()
        x = blocks[k].reshape(2 * n, width)
        rows = pl.ds(k * 2 * n, 2 * n)
        for lane, size in hidden_tiles(hidden):
            lanes = pl.ds(lane, size)
            gate = dot(x, r.w_gate[lanes], 1, 1)
            up = dot(x, r.w_up[lanes], 1, 1)
            act = gate / (1.0 + jnp.exp(-gate)) * up
            gate_out[rows, lanes] = gate.astype(BF16)
            up_out[rows, lanes] = up.astype(BF16)
            act_out[rows, lanes] = act.astype(BF16)
        pairs = [(blocks.at[k], r.f_blocks_hbm.at[k])]
        for source, target in ((gate_out, r.gate), (up_out, r.up), (act_out, r.act)):
            pairs.append((source.at[rows], target.at[rows]))
        save(saves, r.f_save_sem, pairs)
        getattr(at(layer), "f_up" + str(k))()
    at(layer).f_up()
    loads[2].start()
    loads[2].wait()

    def down(k):
        act = act_out[pl.ds(k * 2 * n, 2 * n)]
        for lane, size in width_tiles(width):
            put_partial(r, k, lane, size, dot(act, r.w_down[:, pl.ds(lane, size)], 1, 0))
        sides[k].start()

    down(3)
    down(1)
    sides[3].wait_recv()
    scatter.send_corner(with_side(r, 3))
    down(2)
    sides[1].wait_recv()
    scatter.send_edge_a(with_side(r, 1))
    sides[2].wait_recv()
    scatter.send_edge_b(with_side(r, 2))
    down(0)
    at(layer).f_edges()
    sides[0].wait_recv()
    result_ref[...] = second_ref[...] + scatter.total(with_side(r, 0))
    at(layer).f_end()
    wait_all([], [*gather.copies, *sides, *scatter.copies])
    for copy in saves:
        copy.wait()


def ffn_backward_loads(r, layer, gathers):
    r = r.of(layer)
    stage = stage_in(r)
    loads = [
        Load(halves, weight, stage, sems)
        for halves, weight, sems in zip(
            ([r.gate_own, r.gate_other], [r.up_own, r.up_other], [r.down_own, r.down_other]),
            (r.w_gate, r.w_up, r.w_down),
            r.f_load_sems,
            strict=True,
        )
    ]
    for load in loads:
        load.start()
    more = [(r.gate, r.hidden[0]), (r.up, r.hidden[1])]
    if not gathers:
        more.append((r.gathered, r.f_blocks))
    extra = []
    save(extra, r.f_extra_sem, more)
    return loads + extra


def ffn_backward(r, layer, a, at, gathers, loads):
    r = r.of(layer)
    links = Links(r.f_sems)
    blocks, second_ref, grad_ref = r.f_blocks, r.second, r.of(layer + 1).d_entry
    gate_in, up_in = r.hidden
    d_gate_out, d_up_out = r.hidden
    n, width = blocks.shape[2:]
    hidden = r.w_gate.shape[0]
    if gathers:
        blocks[0, 0] = grad_ref[...]
    gather = BlockGather(links, blocks, a, ROW_LOW, there=not gathers)
    sides = side_copies(links, r)
    scatter = Scatter(links, r, r.f_corner_in, r.f_edge_in, a, ROW_LOW)
    saves = []

    def step(k):
        g = blocks[k].reshape(2 * n, width)
        rows = pl.ds(k * 2 * n, 2 * n)
        for lane, size in hidden_tiles(hidden):
            lanes = pl.ds(lane, size)
            d_act = dot(g, r.w_down[lanes], 1, 1)
            gate = gate_in[rows, lanes].astype(F32)
            up = up_in[rows, lanes].astype(F32)
            sigma = 1.0 / (1.0 + jnp.exp(-gate))
            d_gate_out[rows, lanes] = (d_act * up * sigma * (1.0 + gate * (1.0 - sigma))).astype(BF16)
            d_up_out[rows, lanes] = (d_act * gate * sigma).astype(BF16)
        pairs = [(d_gate_out.at[rows], r.d_gate.at[rows]), (d_up_out.at[rows], r.d_up.at[rows])]
        if gathers:
            pairs.append((blocks.at[k], r.f_blocks_hbm.at[k]))
        save(saves, r.f_save_sem, pairs)
        d_gate = d_gate_out[rows]
        d_up = d_up_out[rows]
        for lane, size in width_tiles(width):
            lanes = pl.ds(lane, size)
            value = dot(d_gate, r.w_gate[:, lanes], 1, 0) + dot(d_up, r.w_up[:, lanes], 1, 0)
            put_partial(r, k, lane, size, value)
        sides[k].start()

    gather.a.start()
    gather.b.start()
    gather.sides[0].start()
    at(layer).f_sent()
    for load in loads:
        load.wait()
    gather.sides[0].wait_recv()
    step(0)
    gather.a.wait_recv()
    gather.ab.start()
    gather.sides[1].start()
    gather.b.wait_recv()
    gather.ba.start()
    gather.sides[2].start()
    gather.sides[1].wait_recv()
    step(1)
    gather.ab.wait_recv()
    gather.ba.wait_recv()
    gather.sides[3].start()
    gather.sides[3].wait_recv()
    step(3)
    sides[3].wait_recv()
    scatter.send_corner(with_side(r, 3))
    at(layer).f_corner()
    gather.sides[2].wait_recv()
    step(2)
    sides[1].wait_recv()
    scatter.send_edge_a(with_side(r, 1))
    sides[2].wait_recv()
    scatter.send_edge_b(with_side(r, 2))
    at(layer).f_edges()
    sides[0].wait_recv()
    d_normed = scatter.total(with_side(r, 0))
    second = second_ref[...]
    inverse = lax.rsqrt(jnp.mean(second * second, axis=-1, keepdims=True) + EPS)
    d_second, d_gain = norm_backward(second, inverse, r.gain_ffn[...], d_normed)
    r.d_gain_ffn[...] = d_gain
    r.d_second[...] = grad_ref[...].astype(F32) + d_second
    at(layer).f_end()
    wait_all([], [*gather.copies, *sides, *scatter.copies])
    for copy in saves:
        copy.wait()


def turn(vectors, cosine, sine):
    return vectors * cosine + pltpu.roll(vectors, HEAD // 2, 1) * sine


def seen(r, slot):
    key = r.key[...]
    visible = (key >= r.start[pl.ds(slot, 1)]) & (key <= r.own[...])
    return jnp.where(visible, 0.0, -1e30)


def attention_weights(r):
    weights = r.w_attn
    heads_width = (weights.shape[0] - 2 * HEAD) // 2
    return (
        weights.at[pl.ds(0, heads_width)],
        weights.at[pl.ds(heads_width, heads_width)],
        weights.at[pl.ds(2 * heads_width, 2 * HEAD)],
    )


def column_gather(links, blocks):
    h = blocks.shape[1] // 2
    return (
        links.copy(blocks.at[0], blocks.at[1], COL_LOW),
        links.copy(blocks.at[0], blocks.at[2], COL_HIGH),
        links.copy(blocks.at[1, pl.ds(0, h)], blocks.at[3, pl.ds(0, h)], COL_HIGH),
        links.copy(blocks.at[2, pl.ds(h, h)], blocks.at[3, pl.ds(h, h)], COL_LOW),
    )


def attention_forward(r, layer, at, gather):
    r = r.of(layer)
    links = Links(r.a_sems)
    entry, kv, bias, partial = r.entry, r.kv, r.bias, r.partial
    normed, query, mixed, lse_ref = r.normed, r.query, r.mixed, r.lse
    cos_ref, sin_ref = r.cos, r.sin
    n, width = entry.shape[1:]
    tokens = 2 * n
    rows = kv.shape[1]
    w_query, w_out, w_pair = attention_weights(r)
    heads = w_query.shape[0] // HEAD
    bits = rows.bit_length() - 1
    scale = 1.0 / math.sqrt(HEAD)
    stage = stage_in(r)
    load = Load(gather.blocks, r.w_attn, stage, r.a_load_sem)
    scatter = Scatter(links, r, r.a_corner_in, r.a_edge_in, COL_LOW, COL_HIGH)
    hops = [
        [(slot, filled, links.copy(kv.at[b, slot], kv.at[b, filled], (ROW, 1 << bit)))
         for slot, filled, bit in row_hops(bits)]
        for b in range(2)
    ]
    copies = scatter.copies + [copy for group in hops for _, _, copy in group]

    def normalise(k):
        x = entry[k].astype(F32)
        inverse = lax.rsqrt(jnp.mean(x * x, axis=-1, keepdims=True) + EPS)
        normed[pl.ds(k * n, n)] = (x * inverse * r.gain_attn[...]).astype(BF16)

    def project_pair(b):
        where = pl.ds(b * tokens, tokens)
        pair = dot(normed[where], w_pair[...], 1, 1) + r.b_pair[...]
        kv[b, 0, :, :HEAD] = turn(pair[:, :HEAD], cos_ref[where], sin_ref[where]).astype(BF16)
        kv[b, 0, :, HEAD:] = pair[:, HEAD:].astype(BF16)
        for slot, _, copy in hops[b]:
            if slot == 0:
                copy.start()

    def project_query(b):
        where = pl.ds(b * tokens, tokens)
        projected = dot(normed[where], w_query[...], 1, 1) + r.b_query[...]
        for head in range(heads):
            lanes = slice(head * HEAD, (head + 1) * HEAD)
            query[where, lanes] = turn(projected[:, lanes], cos_ref[where], sin_ref[where]).astype(BF16)

    arrived = [set(), set()]

    def arrive(b, slot):
        for _, filled, copy in hops[b]:
            if filled == slot and slot not in arrived[b]:
                copy.wait_recv()
                arrived[b].add(slot)

    if layer:
        entry[0] = r.result0[...].astype(BF16)
        to_low, to_high, corner_high, corner_low = column_gather(links, entry)
        copies += [to_low, to_high, corner_high, corner_low]
        to_low.start()
        to_high.start()
        at(layer).a_begin()
        load.start()
        normalise(0)
        to_low.wait_recv()
        corner_high.start()
        to_high.wait_recv()
        corner_low.start()
        normalise(1)
        normalise(2)
        load.wait()
        project_pair(0)
        corner_high.wait_recv()
        corner_low.wait_recv()
        normalise(3)
        project_pair(1)
    else:
        at(layer).a_begin()
        for k in range(4):
            normalise(k)
        at(layer).a_normed()
        load.start()
        load.wait()
        project_pair(1)
        project_pair(0)
    at(layer).a_pairs()
    project_query(1)
    project_query(0)
    at(layer).a_queries()
    for b in (1, 0):
        for slot, _, copy in hops[b]:
            if slot:
                arrive(b, slot)
                copy.start()
    at(layer).a_relayed()
    saves = []
    for b in (1, 0):
        for slot in range(1, rows):
            arrive(b, slot)
        save(saves, r.a_save_sem, [(kv.at[b], r.kv_hbm.at[b])])
        keys = kv[b, :, :, :HEAD].reshape(rows * tokens, HEAD)
        values = kv[b, :, :, HEAD:].reshape(rows * tokens, HEAD)
        where = pl.ds(b * tokens, tokens)
        bias[...] = seen(r, b)
        for head in range(heads):
            lanes = slice(head * HEAD, (head + 1) * HEAD)
            scores = dot(keys, query[where, lanes], 1, 1) * scale + bias[...]
            top = jnp.max(scores, axis=0, keepdims=True)
            raised = jnp.exp(scores - top)
            total = jnp.sum(raised, axis=0, keepdims=True)
            lse_ref[b, pl.ds(head, 1)] = top + jnp.log(total)
            probs = (raised * (1.0 / total)).astype(BF16)
            mixed[where, lanes] = dot(probs, values, 0, 0).astype(BF16)
            if b == 0:
                getattr(at(layer), "a_head" + str(head))()
        for k in (2 * b + 1, 2 * b):
            for lane, size in width_tiles(width):
                partial[k, :, pl.ds(lane, size)] = dot(
                    mixed[pl.ds(k * n, n)], w_out[:, pl.ds(lane, size)], 1, 0
                )
        if b == 1:
            scatter.send_corner(partial[3])
            at(layer).a_half()
    scatter.send_edge_b(partial[2])
    scatter.send_edge_a(partial[1])
    if layer:
        save(saves, r.a_save_sem, [(entry.at[0], r.entry_hbm)])
    at(layer).a_edges()
    r.second[...] = entry[0].astype(F32) + scatter.total(partial[0])
    at(layer).a_end()
    wait_all([], copies)
    for copy in saves:
        copy.wait()


def attention_backward(r, layer, at):
    r = r.of(layer)
    links = Links(r.a_sems)
    blocks, kv, bias, partial = r.a_blocks, r.kv, r.bias, r.partial
    d_mixed, d_kv, d_kv_out, d_kv_in = r.d_mixed, r.d_kv, r.d_kv_out, r.d_kv_in
    query, d_query, d_pair = r.query, r.d_query, r.d_pair
    share_out, share_in = r.share_out, r.share_in
    cos_ref, sin_ref = r.cos, r.sin
    n, width = blocks.shape[1:]
    tokens = 2 * n
    rows = kv.shape[1]
    w_query, w_out, w_pair = attention_weights(r)
    heads_width = w_query.shape[0]
    heads = heads_width // HEAD
    bits = rows.bit_length() - 1
    scale = 1.0 / math.sqrt(HEAD)
    stage = stage_in(r)
    load = Load([r.attn_blocks.at[0], r.attn_blocks.at[1]], r.w_attn, stage, r.a_load_sem)
    load.start()
    blocks[0] = r.d_second[...].astype(BF16)
    to_low, to_high, corner_high, corner_low = column_gather(links, blocks)
    hops = [
        [(slot, filled, links.copy(d_kv_out.at[b, filled], d_kv_in.at[b, filled], (ROW, 1 << bit)))
         for slot, filled, bit in reversed(row_hops(bits))]
        for b in range(2)
    ]
    share = [links.copy(share_out.at[b], share_in.at[b], COL_LOW) for b in range(2)]
    scatter = Scatter(links, r, r.a_corner_in, r.a_edge_in, COL_LOW, COL_HIGH)

    def unmix(k):
        d_mixed[pl.ds(k * n, n)] = dot(blocks[k], w_out[...], 1, 1).astype(BF16)

    def attend(b):
        keys = kv[b, :, :, :HEAD].reshape(rows * tokens, HEAD)
        values = kv[b, :, :, HEAD:].reshape(rows * tokens, HEAD)
        where = pl.ds(b * tokens, tokens)
        bias[...] = seen(r, b)
        for head in range(heads):
            lanes = slice(head * HEAD, (head + 1) * HEAD)
            q = query[where, lanes]
            d_o = d_mixed[where, lanes]
            scores = dot(keys, q, 1, 1) * scale + bias[...]
            probs = jnp.exp(scores - r.lse[b, pl.ds(head, 1)])
            d_probs = dot(values, d_o, 1, 1)
            delta = jnp.sum(d_probs * probs, axis=0, keepdims=True)
            d_scores = (probs * (d_probs - delta)).astype(BF16)
            d_keys = (dot(d_scores, q, 1, 0) * scale).reshape(rows, tokens, HEAD)
            d_values = dot(probs.astype(BF16), d_o, 1, 0).reshape(rows, tokens, HEAD)
            if head:
                d_keys = d_keys + d_kv[b, :, :, :HEAD]
                d_values = d_values + d_kv[b, :, :, HEAD:]
            d_kv[b, :, :, :HEAD] = d_keys
            d_kv[b, :, :, HEAD:] = d_values
            turned = dot(d_scores, keys, 0, 0) * scale
            d_query[where, lanes] = turn(turned, cos_ref[where], -sin_ref[where]).astype(BF16)

    def send_bit(b, step):
        for slot, filled, copy in hops[b]:
            if filled - slot == step:
                d_kv_out[b, filled] = d_kv[b, filled].astype(BF16)
                copy.start()

    def add_bit(b, step):
        for slot, filled, copy in hops[b]:
            if filled - slot == step:
                copy.wait_recv()
                d_kv[b, slot] = d_kv[b, slot] + d_kv_in[b, filled].astype(F32)

    def share_pair(b):
        share_out[b] = d_kv[b, 0, n:].astype(BF16)
        share[b].start()

    def finish_pair(b):
        share[b].wait_recv()
        total = d_kv[b, 0, :n] + share_in[b].astype(F32)
        where = pl.ds(b * tokens, n)
        rows_of = pl.ds(b * n, n)
        d_pair[rows_of, :HEAD] = turn(total[:, :HEAD], cos_ref[where], -sin_ref[where]).astype(BF16)
        d_pair[rows_of, HEAD:] = total[:, HEAD:].astype(BF16)

    def unproject(k):
        for lane, size in width_tiles(width):
            lanes = pl.ds(lane, size)
            value = dot(d_query[pl.ds(k * n, n)], w_query[:, lanes], 1, 0)
            if k % 2 == 0:
                value = value + dot(d_pair[pl.ds(k // 2 * n, n)], w_pair[:, lanes], 1, 0)
            partial[k, :, lanes] = value

    to_low.start()
    to_high.start()
    at(layer).a_sent()
    load.wait()
    unmix(0)
    to_low.wait_recv()
    corner_high.start()
    to_high.wait_recv()
    corner_low.start()
    at(layer).a_relayed()
    unmix(1)
    unmix(2)
    corner_high.wait_recv()
    corner_low.wait_recv()
    unmix(3)
    attend(1)
    send_bit(1, 1)
    unproject(3)
    scatter.send_corner(partial[3])
    attend(0)
    send_bit(0, 1)
    for bit in range(1, bits):
        for b in (1, 0):
            add_bit(b, 1 << (bit - 1))
            send_bit(b, 1 << bit)
    at(layer).a_hops()
    unproject(1)
    scatter.send_edge_a(partial[1])
    for b in (1, 0):
        add_bit(b, 1 << (bits - 1))
        share_pair(b)
    finish_pair(1)
    unproject(2)
    scatter.send_edge_b(partial[2])
    at(layer).a_edges()
    finish_pair(0)
    unproject(0)
    r.d_bias_query[...] = jnp.sum(d_query[...].astype(F32), axis=0, keepdims=True)
    r.d_bias_pair[...] = jnp.sum(d_pair[...].astype(F32), axis=0, keepdims=True)
    a_grad, normed = r.a_grad, r.normed
    turned_query, turned_mixed, turned_pair = d_query[...].T, r.mixed[...].T, d_pair[...].T
    for lane, size in width_tiles(width):
        lanes = pl.ds(lane, size)
        a_grad[:heads_width, lanes] = dot(turned_query, normed[:, lanes], 1, 0).astype(BF16)
        a_grad[heads_width : 2 * heads_width, lanes] = dot(
            turned_mixed, blocks[:, :, lanes].reshape(4 * n, size), 1, 0
        ).astype(BF16)
        normed_own = jnp.concatenate([normed[:n, lanes], normed[tokens : tokens + n, lanes]])
        a_grad[2 * heads_width :, lanes] = dot(turned_pair, normed_own, 1, 0).astype(BF16)
    at(layer).a_grads()
    d_normed = scatter.total(partial[0])
    stream = r.entry[...].astype(F32)
    inverse = lax.rsqrt(jnp.mean(stream * stream, axis=-1, keepdims=True) + EPS)
    d_first, d_gain = norm_backward(stream, inverse, r.gain_attn[...], d_normed)
    r.d_gain_attn[...] = d_gain
    r.d_entry[...] = (r.d_second[...] + d_first).astype(BF16)
    at(layer).a_end()
    copies = [to_low, to_high, corner_high, corner_low, *share, *scatter.copies]
    wait_all([], copies + [copy for group in hops for _, _, copy in group])


def sum_vectors(r, at, links):
    vector = r.vector
    vector[...] = jnp.zeros_like(vector)
    col = lax.axis_index(COL)
    lanes = r.d_gain_ffn0.shape[1] // HEAD
    heads = r.d_bias_query0.shape[1] // HEAD
    each = vector.shape[0] // 2
    for layer in range(2):
        of = r.of(layer)
        for gain, first in ((of.d_gain_attn, 0), (of.d_gain_ffn, lanes)):
            for i in range(lanes):
                vector[pl.ds(layer * each + first + i, 1)] = gain[:, i * HEAD : (i + 1) * HEAD]
        for i in range(heads):
            place = layer * each + 2 * lanes + col * heads + i
            vector[pl.ds(place, 1)] = of.d_bias_query[:, i * HEAD : (i + 1) * HEAD]
        for i in range(2):
            place = layer * each + 3 * lanes + i * KV + (col >> 1)
            vector[pl.ds(place, 1)] = of.d_bias_pair[:, i * HEAD : (i + 1) * HEAD]
    ways = [SECTION, COL_LOW, COL_HIGH] + [(ROW, 1 << bit) for bit in range(row_bits())]
    copies = []
    for i, way in enumerate(ways):
        r.vector_out[i] = vector[...]
        copies.append(links.copy(r.vector_out.at[i], r.vector_in.at[i], way))
        copies[-1].start()
        at(i).s_step()
        copies[-1].wait_recv()
        vector[...] = vector[...] + r.vector_in[i]
    r.sums[...] = vector[...]
    wait_all([], copies)


class Sizes:
    def __init__(self, n, width, rows, hidden, attn, depth):
        self.n, self.width, self.rows, self.depth = n, width, rows, depth
        self.unit, self.hidden, self.attn = hidden // 2, padded(hidden), attn
        self.heads_width = (attn - 2 * HEAD) // 2
        self.heads = self.heads_width // HEAD


def common_scratch(sizes):
    n, width = sizes.n, sizes.width
    return dict(
        partial=pltpu.VMEM((4, n, width), F32),
        corner_out=pltpu.VMEM((2, n // 2, width), BF16),
        edge_out=pltpu.VMEM((2, n, width), BF16),
        **stage_of(sizes),
    )


def ffn_scratch(sizes, count, saves):
    n, width, hidden = sizes.n, sizes.width, sizes.hidden
    each = 2 * sizes.rows
    return dict(
        w_gate=pltpu.VMEM((hidden, width), BF16),
        w_up=pltpu.VMEM((hidden, width), BF16),
        w_down=pltpu.VMEM((hidden, width), BF16),
        hidden=[pltpu.VMEM((8 * n, hidden), BF16) for _ in range(count)],
        side_out=pltpu.VMEM((4, n, width), BF16),
        f_load_sems=semaphores(each, each, each),
        f_extra_sem=pltpu.SemaphoreType.DMA((3,)),
        f_save_sem=pltpu.SemaphoreType.DMA((4 * saves,)),
    )


def ffn_buffers(sizes, layer):
    n, width = sizes.n, sizes.width
    return layered(
        layer,
        f_blocks=pltpu.VMEM((4, 2, n, width), BF16),
        side_in=pltpu.VMEM((4, n, width), BF16),
        f_corner_in=pltpu.VMEM((2, n // 2, width), BF16),
        f_edge_in=pltpu.VMEM((2, n, width), BF16),
        f_sems=semaphores(16, 16),
    )


def attention_scratch(sizes):
    tokens = 2 * sizes.n
    return dict(
        w_attn=pltpu.VMEM((sizes.attn, sizes.width), BF16),
        bias=pltpu.VMEM((sizes.rows * tokens, tokens), F32),
        a_load_sem=pltpu.SemaphoreType.DMA((2 * sizes.rows,)),
        a_save_sem=pltpu.SemaphoreType.DMA((3,)),
    )


def attention_buffers(sizes, layer, backward):
    n, width, rows = sizes.n, sizes.width, sizes.rows
    pairs = (2, rows, 2 * n, 2 * HEAD)
    count = 10 + 2 * (rows - 1)
    buffers = dict(
        a_corner_in=pltpu.VMEM((2, n // 2, width), BF16),
        a_edge_in=pltpu.VMEM((2, n, width), BF16),
        a_sems=semaphores(count, count),
    )
    if backward:
        buffers.update(a_blocks=pltpu.VMEM((4, n, width), BF16))
        buffers.update(d_kv_in=pltpu.VMEM(pairs, BF16))
        buffers.update(share_in=pltpu.VMEM((2, n, 2 * HEAD), BF16))
    else:
        buffers.update(kv=pltpu.VMEM(pairs, BF16))
    return layered(layer, **buffers)


def attention_back_scratch(sizes):
    n, rows = sizes.n, sizes.rows
    pairs = (2, rows, 2 * n, 2 * HEAD)
    return dict(
        **attention_scratch(sizes),
        d_mixed=pltpu.VMEM((4 * n, sizes.heads_width), BF16),
        d_kv=pltpu.VMEM(pairs, F32),
        d_kv_out=pltpu.VMEM(pairs, BF16),
        share_out=pltpu.VMEM((2, n, 2 * HEAD), BF16),
        d_query=pltpu.VMEM((4 * n, sizes.heads_width), BF16),
        d_pair=pltpu.VMEM((2 * n, 2 * HEAD), BF16),
        a_grad=pltpu.VMEM((sizes.attn, sizes.width), BF16),
    )


def small_outs(sizes, layer):
    return layered(
        layer,
        d_gain_attn=((1, sizes.width), F32, True),
        d_bias_query=((1, sizes.heads_width), F32, True),
        d_bias_pair=((1, 2 * HEAD), F32, True),
    )


def exchange_halves(parts, section):
    return pick(parts, section), swap(pick(parts, 1 - section), *SECTION)


def of_layer(layer, parts, section, token):
    own, other = parts
    return jnp.where(section + token == layer, own, other)


def to_owner(first, second, section):
    keep = jnp.where(section == 0, first, second)
    away = jnp.where(section == 0, second, first)
    other = swap(away, *SECTION)
    return jnp.where(section == 0, keep, other), jnp.where(section == 0, other, keep)


def local(
    tokens,
    cotangent,
    lengths,
    norm_attn,
    w_query,
    b_query,
    w_keyval,
    b_keyval,
    w_out,
    norm_ffn,
    w_gate,
    w_up,
    w_down,
):
    section = lax.axis_index(SEC)
    row = lax.axis_index(ROW)
    col = lax.axis_index(COL)
    rows = lax.axis_size(ROW)
    cols = lax.axis_size(COL)
    low, high = bit_of(col, 0), bit_of(col, 1)
    place = (section, row, low, high)
    row_count = tokens.shape[1]
    width = tokens.shape[2]
    half = row_count // 2
    depth = w_query.shape[1]
    heads_width = w_query.shape[2]

    def blocks_of(array):
        return jnp.concatenate(
            [
                lax.dynamic_slice(
                    array, (2 * section + (high ^ j), (low ^ k) * half, 0), (1, half, width)
                )
                for j in range(2)
                for k in range(2)
            ]
        )

    small = jnp.concatenate([norm_attn[0], norm_ffn[0], b_keyval[0], b_query[0]])
    small = (small, swap(small, *SECTION))
    small = [of_layer(layer, small, section, 0).astype(F32) for layer in range(2)]

    pair_cols = w_keyval[0].reshape(-1, 2, KV, HEAD)
    mine = pick(pair_cols, high, 2).reshape(-1, 2 * HEAD)
    away = pick(pair_cols, 1 - high, 2).reshape(-1, 2 * HEAD)
    pair_rows = ordered(mine[None, None], swap(away, *COL_HIGH)[None, None], high, 0)
    pair_rows = ordered(pair_rows, swap(pair_rows, *COL_LOW), low, 1)
    pair_rows = pair_rows.reshape(depth, 2 * HEAD)
    attn_own = jnp.concatenate([w_query[0].T, w_out[0], pair_rows.T])
    attn_halves = exchange_halves(attn_own.reshape(2, -1, depth), section)

    def ffn_parts(shard):
        hidden = shard.shape[0]
        parts = shard.reshape(2, 2, hidden // 4, shard.shape[1]).transpose(1, 0, 2, 3)
        return exchange_halves(parts, section)

    parts = [ffn_parts(shard) for shard in (w_gate[0].T, w_up[0].T, w_down[0])]
    ways = [(COL_LOW, COL_HIGH), (COL_HIGH, COL_LOW)]

    hidden = w_gate.shape[2] // 2

    tables = layout(lengths, place, row_count)
    sizes = Sizes(half, width, rows, hidden, 2 * attn_halves[0].shape[0], depth)
    entry = blocks_of(tokens)

    ffn_ways = [way for way, _ in ways]
    across = [way for _, way in ways]
    cosine, sine, start, own_index, key_index = tables
    shared = dict(
        cos=(cosine, True),
        sin=(sine, True),
        start=(start, True),
        own=(own_index, True),
        key=(key_index, True),
    )
    gains_attn, gains_ffn, vectors = [], [], []
    for layer in range(2):
        bias_pair = small[layer][2 * width : 2 * width + 2 * KV * HEAD].reshape(2, KV, HEAD)
        gains_attn.append(layered(layer, gain_attn=(small[layer][None, :width], True)))
        gains_ffn.append(layered(layer, gain_ffn=(small[layer][None, width : 2 * width], True)))
        vectors.append(
            layered(
                layer,
                b_query=(small[layer][None, 2 * width + 2 * KV * HEAD :], True),
                b_pair=(pick(bias_pair, high, 1).reshape(1, -1), True),
            )
        )
    chip_ways = [COL_LOW, COL_HIGH, SECTION] + [(ROW, 1 << bit) for bit in range(row_bits())]

    attn_moves = [AttnGather(of_layer(layer, attn_halves, section, 0)) for layer in range(2)]
    ffn_moves = [
        [FfnGather(layer, parts[kind], across[layer]) for kind in range(3)]
        for layer in range(2)
    ]
    grad_own = lax.dynamic_slice(
        cotangent, (2 * section + high, low * half, 0), (1, half, width)
    )[0]
    grad_move = TokenGather(grad_own, grad_own.shape, ffn_ways[1], ROW_LOW, True)
    (attn_a, attn_b), ((gate_a, up_a, down_a), (gate_b, up_b, down_b)) = attn_moves, ffn_moves
    some, rest = rows // 2, rows - rows // 2
    schedule = dict(
        a0_begin=[attn_a],
        a0_normed=[attn_a, gate_a, gate_a, attn_a],
        a0_queries=[gate_a] * rows,
        a0_relayed=[up_a, up_a, down_a, down_a],
        a0_head0=[up_a] * some,
        a0_head1=[up_a] * rest,
        f0_sent=[down_a] * some + [attn_b],
        f0_gathered=[gate_a] + [down_a] * rest + [up_a],
        f0_up=[down_a, attn_b],
        f0_edges=[gate_b, gate_b],
        f0_end=[attn_b],
        a1_queries=[gate_b] * rows,
        a1_relayed=[up_b, up_b, down_b, down_b],
        a1_head0=[up_b] * some,
        a1_head1=[up_b] * rest,
        f1_sent=[down_b] * some,
        f1_gathered=[gate_b] + [down_b] * rest + [up_b, grad_move],
        f1_up=[down_b, grad_move],
        f1_edges=[grad_move],
    )

    def forward_kernel(r, at):
        for layer in range(2):
            attention_forward(r, layer, at, attn_moves[layer])
            ffn_forward(r, layer, ffn_ways[layer], at, ffn_moves[layer])

    tokens_here = 4 * half
    outs = dict(entry_hbm1=((half, width), BF16, False), result1=((half, width), F32, True))
    buffers = dict(
        entry1=pltpu.VMEM((4, half, width), BF16), result0=pltpu.VMEM((half, width), F32)
    )
    units = ((8 * half, sizes.hidden), BF16, False)
    for layer in range(2):
        outs.update(
            layered(
                layer,
                second=((half, width), F32, True),
                normed=((tokens_here, width), BF16, True),
                query=((tokens_here, heads_width), BF16, True),
                mixed=((tokens_here, heads_width), BF16, True),
                lse=((2, sizes.heads, 2 * half), F32, True),
                kv_hbm=((2, rows, 2 * half, 2 * HEAD), BF16, False),
                f_blocks_hbm=((4, 2, half, width), BF16, False),
                gate=units,
                up=units,
                act=units,
            )
        )
        buffers.update(ffn_buffers(sizes, layer))
        buffers.update(attention_buffers(sizes, layer, False))
    done = kernel_call(
        forward_kernel,
        0,
        chip_ways,
        dict(
            entry0=(entry, True),
            **shared,
            **gains_attn[0],
            **gains_attn[1],
            **gains_ffn[0],
            **gains_ffn[1],
            **vectors[0],
            **vectors[1],
        ),
        outs,
        {**common_scratch(sizes), **ffn_scratch(sizes, 3, 4), **attention_scratch(sizes), **buffers},
        1 << 34,
        [*attn_moves, *ffn_moves[0], *ffn_moves[1], grad_move],
        schedule,
    )
    (grad_all,) = grad_move.results
    last_result = done.result1.astype(BF16)

    def grad_of(left, right):
        return dot(left, right.reshape(-1, width), 0, 0).astype(BF16)

    unit = sizes.unit

    def blocked(grad, arrived):
        total = (grad[:unit].astype(F32) + arrived.astype(F32)).astype(BF16)
        return jnp.stack([total[:, i * depth : (i + 1) * depth] for i in range(rows)])

    def ffn_back_operands(layer):
        of = done.of(layer)
        (gate, gate_far), (up, up_far), (down, down_far) = (move.results for move in ffn_moves[layer])
        return {
            **gains_ffn[layer],
            **layered(
                layer,
                second=(of.second, True),
                gate=(of.gate, False),
                up=(of.up, False),
                gate_own=(gate, False),
                gate_other=(gate_far, False),
                up_own=(up, False),
                up_other=(up_far, False),
                down_own=(down, False),
                down_other=(down_far, False),
            ),
        }

    def ffn_back_outs(layer):
        return layered(
            layer,
            d_second=((half, width), F32, True),
            d_gain_ffn=((1, width), F32, True),
            d_gate=units,
            d_up=units,
        )

    def attention_back_operands(layer, own):
        of = done.of(layer)
        return {
            **gains_attn[layer],
            **shared,
            **layered(
                layer,
                entry=(own, True),
                attn_blocks=(attn_moves[layer].results[0], False),
                kv=(of.kv_hbm, True),
                normed=(of.normed, True),
                query=(of.query, True),
                mixed=(of.mixed, True),
                lse=(of.lse, True),
            ),
        }

    down_grad = grad_of(done.act1, grad_all)
    down_move = Across(down_grad, unit, across[1])
    back = kernel_call(
        lambda r, at: ffn_backward(r, 1, ffn_ways[1], at, False, ffn_backward_loads(r, 1, False)),
        1,
        [ffn_ways[1], ROW_LOW, SECTION],
        dict(d_entry2=(grad_own, True), gathered1=(grad_all, False), **ffn_back_operands(1)),
        ffn_back_outs(1),
        {**common_scratch(sizes), **ffn_scratch(sizes, 2, 2), **ffn_buffers(sizes, 1)},
        1 << 33,
        [down_move],
        dict(f1_sent=[down_move]),
    )
    gate_grad = grad_of(back.d_gate1, done.f_blocks_hbm1)
    up_grad = grad_of(back.d_up1, done.f_blocks_hbm1)
    down_one = blocked(down_grad, down_move.results[0])

    down_rows = Rows(down_one)
    gate_move = GradScatter(gate_grad, unit, across[1])
    up_move = Across(up_grad, unit, across[1])
    last_move = ColumnGather(last_result, last_result.shape)
    entry_move = ColumnGather("d_entry1", (half, width))
    attn_move_one = AttnScatter("a_grad", (sizes.attn, width))

    def middle_kernel(r, at):
        loads = ffn_backward_loads(r, 0, True)
        attention_backward(r, 1, at)
        ffn_backward(r, 0, ffn_ways[0], at, True, loads)

    middle = kernel_call(
        middle_kernel,
        2,
        chip_ways,
        dict(
            d_second1=(back.d_second1, True),
            **attention_back_operands(1, done.entry_hbm1),
            **ffn_back_operands(0),
        ),
        dict(
            d_entry1=((half, width), BF16, True),
            f_blocks_hbm0=((4, 2, half, width), BF16, False),
            **small_outs(sizes, 1),
            **ffn_back_outs(0),
        ),
        {
            **common_scratch(sizes),
            **attention_back_scratch(sizes),
            **attention_buffers(sizes, 1, True),
            **ffn_scratch(sizes, 2, 3),
            **ffn_buffers(sizes, 0),
        },
        1 << 33,
        [down_rows, gate_move, up_move, last_move, entry_move, attn_move_one],
        dict(
            a1_relayed=[down_rows, gate_move],
            a1_grads=[attn_move_one],
            f0_edges=[gate_move, up_move, attn_move_one, last_move, entry_move],
        ),
    )
    up_one = blocked(up_grad, up_move.results[0])
    zero_grads = [
        grad_of(done.act0, middle.f_blocks_hbm0),
        grad_of(middle.d_gate0, done.f_blocks_hbm0),
        grad_of(middle.d_up0, done.f_blocks_hbm0),
    ]

    up_rows = Rows(up_one)
    zero_moves = [GradScatter(grad, unit, across[0]) for grad in zero_grads]
    attn_move_zero = AttnScatter("a_grad", (sizes.attn, width))
    first_move = ColumnGather("d_entry0", (half, width))
    result_move = ColumnGather(done.entry_hbm1, (half, width))
    sum_rows = 2 * (3 * width // HEAD + 2 * KV)
    sum_ways = 3 + row_bits()

    def last_kernel(r, at):
        attention_backward(r, 0, at)
        sum_vectors(r, at, Links(r.sum_sems))

    down_zero, gate_zero, up_zero = zero_moves
    final = kernel_call(
        last_kernel,
        3,
        chip_ways,
        dict(
            d_second0=(middle.d_second0, True),
            d_gain_ffn0=(middle.d_gain_ffn0, True),
            d_gain_ffn1=(back.d_gain_ffn1, True),
            **attention_back_operands(0, entry[0]),
            **{name: (middle.named[name], True) for name in small_outs(sizes, 1)},
        ),
        dict(d_entry0=((half, width), BF16, True), sums=((sum_rows, HEAD), F32, True)),
        {
            **common_scratch(sizes),
            **attention_back_scratch(sizes),
            **attention_buffers(sizes, 0, True),
            **{name: pltpu.VMEM(shape, F32) for name, (shape, _, _) in small_outs(sizes, 0).items()},
            **dict(
                vector=pltpu.VMEM((sum_rows, HEAD), F32),
                vector_out=pltpu.VMEM((sum_ways, sum_rows, HEAD), F32),
                vector_in=pltpu.VMEM((sum_ways, sum_rows, HEAD), F32),
                sum_sems=semaphores(sum_ways, sum_ways),
            ),
        },
        1 << 32,
        [up_rows, *zero_moves, attn_move_zero, first_move, result_move],
        dict(
            a0_relayed=[down_zero],
            a0_hops=[up_rows, result_move],
            a0_edges=[gate_zero, up_zero],
            a0_grads=[down_zero, attn_move_zero, result_move],
            a0_end=[attn_move_zero, gate_zero, first_move],
            s1_step=[attn_move_zero],
            s2_step=[first_move],
            s3_step=[attn_move_zero],
        ),
    )

    def by_row_bit(own, arrived):
        near, far = own.astype(F32), 0.0
        for flip in range(1, rows):
            if flip & 1:
                far = far + arrived[flip].astype(F32)
            else:
                near = near + arrived[flip].astype(F32)
        return ordered(near.astype(BF16)[None], far.astype(BF16)[None], row & 1, 0)

    ffn_grads = [
        [by_row_bit(*move.results) for move in (gate_zero, up_zero, down_zero)],
        [
            by_row_bit(*gate_move.results),
            by_row_bit(pick(up_one, row), up_rows.results[0]),
            by_row_bit(pick(down_one, row), down_rows.results[0]),
        ],
    ]
    sums = final.sums.reshape(2, -1)
    sums = jnp.where(section == 0, sums[0], sums[1])
    grad_norm_attn = sums[:width]
    grad_norm_ffn = sums[width : 2 * width]
    spread = sums[2 * width : 2 * width + cols * heads_width].reshape(cols, -1)
    grad_b_query = pick(spread, col)
    grad_b_keyval = sums[2 * width + cols * heads_width :]
    (first_result,), (last_blocks,) = result_move.results, last_move.results
    (grad_one_blocks,), (grad_zero_blocks,) = entry_move.results, first_move.results
    (attn_one_half,), (attn_zero_half,) = attn_move_one.results, attn_move_zero.results

    def assemble(first, second):
        shape = (2, row_count, width)
        zeroth, later = to_owner(first.reshape(shape), second.reshape(shape), section)
        return jnp.concatenate([zeroth, later])[None]

    outputs = assemble(first_result, last_blocks)
    grads_in = assemble(grad_zero_blocks, grad_one_blocks)

    def ffn_grad(kind):
        zeroth, later = to_owner(ffn_grads[0][kind], ffn_grads[1][kind], section)
        whole = jnp.stack([zeroth, later], axis=1)
        return whole.reshape(-1, whole.shape[-1])

    grad_gate = ffn_grad(0).T.astype(F32)
    grad_up = ffn_grad(1).T.astype(F32)
    grad_down = ffn_grad(2).astype(F32)

    total = jnp.concatenate(to_owner(attn_zero_half, attn_one_half, section)).astype(F32)
    grad_query = total[:heads_width].T
    grad_out = total[heads_width : 2 * heads_width]
    pair = total[2 * heads_width :].T.reshape(2, 2, depth // 4, 2 * HEAD)
    pair = pick(pair, low, 1) + swap(pick(pair, 1 - low, 1).astype(BF16), *COL_LOW).astype(F32)
    pair = pair.astype(BF16)
    pair = ordered(
        pick(pair, high)[:, None], swap(pick(pair, 1 - high), *COL_HIGH)[:, None], high, 1
    )
    grad_keyval = (
        pair.reshape(-1, 2, 2, HEAD).transpose(0, 2, 1, 3).reshape(-1, 2 * KV * HEAD).astype(F32)
    )

    return (
        outputs,
        grads_in,
        grad_norm_attn[None],
        grad_query[None],
        grad_b_query[None],
        grad_keyval[None],
        grad_b_keyval[None],
        grad_out[None],
        grad_norm_ffn[None],
        grad_gate[None],
        grad_up[None],
        grad_down[None],
    )


def solution(mesh):
    in_specs = (
        P(None, ROW, None),
        P(None, ROW, None),
        P(),
        P(SEC, None),
        P(SEC, ROW, COL),
        P(SEC, COL),
        P(SEC, (ROW, COL), None),
        P(SEC, None),
        P(SEC, COL, ROW),
        P(SEC, None),
        P(SEC, ROW, COL),
        P(SEC, ROW, COL),
        P(SEC, COL, ROW),
    )
    out_specs = (
        P(SEC, None, ROW, None),
        P(SEC, None, ROW, None),
        P(SEC, None),
        P(SEC, ROW, COL),
        P(SEC, COL),
        P(SEC, (ROW, COL), None),
        P(SEC, None),
        P(SEC, COL, ROW),
        P(SEC, None),
        P(SEC, ROW, COL),
        P(SEC, ROW, COL),
        P(SEC, COL, ROW),
    )
    return jax.shard_map(local, mesh=mesh, in_specs=in_specs, out_specs=out_specs, check_vma=False)
```

```python
import functools
import math

import jax
import jax.numpy as jnp
from jax import lax
from jax.experimental import pallas as pl
from jax.experimental.pallas import tpu as pltpu
from jax.sharding import PartitionSpec as P

HEADS = 12
KV = 2
HEAD = 128

EPS = 1e-06
THETA = 1000000.0

ROW, SEC, COL = "row", "section", "col"

F32 = jnp.float32
BF16 = jnp.bfloat16

COL_LOW = (COL, 1)
COL_HIGH = (COL, 2)
ROW_LOW = (ROW, 1)
SECTION = (SEC, 1)


def swap(value, axis, flip):
    pairs = [(i, i ^ flip) for i in range(lax.axis_size(axis))]
    return lax.ppermute(value, axis, pairs)


def bit_of(index, bit):
    return (index >> bit) & 1


def pick(array, index, axis=0):
    return lax.dynamic_index_in_dim(array, index, axis, keepdims=False)


def ordered(mine, other, bit, axis):
    first = jnp.where(bit == 0, mine, other)
    second = jnp.where(bit == 0, other, mine)
    return jnp.concatenate([first, second], axis=axis)


def row_bits():
    return lax.axis_size(ROW).bit_length() - 1


def norm_backward(stream, inverse, gain, gradient):
    inner = jnp.mean(gradient * gain * stream, axis=-1, keepdims=True)
    d_stream = gain * gradient * inverse - stream * (inverse * inverse * inverse) * inner
    return (d_stream, jnp.sum(gradient * stream * inverse, axis=0, keepdims=True))


def dot(left, right, left_dim, right_dim):
    return lax.dot_general(
        left, right, (((left_dim,), (right_dim,)), ((), ())), preferred_element_type=F32
    )


def layout(lengths, place, row_count):
    section, row, low, high = place
    rows = lax.axis_size(ROW)
    half = row_count // 2
    inside = jnp.arange(row_count, dtype=jnp.int32)
    inside = (((inside // half) ^ low) * half) + inside % half
    own_index = row * row_count + inside
    key_index = ((jnp.arange(rows, dtype=jnp.int32) ^ row) * row_count)[:, None] + inside[None, :]
    slots = 2 * section + (jnp.arange(2, dtype=jnp.int32) ^ high)
    picked = jnp.stack([pick(lengths, slots[0]), pick(lengths, slots[1])])
    ends = jnp.cumsum(picked, axis=1)
    starts = ends - picked
    inside_piece = (own_index[None, None, :] >= starts[:, :, None]) & (
        own_index[None, None, :] < ends[:, :, None]
    )
    first = jnp.sum(jnp.where(inside_piece, starts[:, :, None], 0), axis=1)
    inverse = THETA ** (-(jnp.arange(HEAD // 2, dtype=F32) * 2.0 / HEAD))
    angle = (own_index[None, :] - first).astype(F32).reshape(-1, 1) * inverse
    cosine, sine = jnp.cos(angle), jnp.sin(angle)
    return (
        jnp.concatenate([cosine, cosine], axis=1),
        jnp.concatenate([-sine, sine], axis=1),
        first,
        own_index[None, :],
        key_index.reshape(-1, 1),
    )


MESH = pl.DeviceIdType.MESH
VMEM_LIMIT = 62 * 1024 * 1024


def partner_of(way):
    axis, flip = way
    return {axis: lax.axis_index(axis) ^ flip}


def enter(ways):
    barrier = pltpu.get_barrier_semaphore()
    for way in ways:
        pl.semaphore_signal(barrier, inc=1, device_id=partner_of(way), device_id_type=MESH)
    pl.semaphore_wait(barrier, len(ways))


def remote(source, target, send, recv, way):
    return pltpu.make_async_remote_copy(
        src_ref=source,
        dst_ref=target,
        send_sem=send,
        recv_sem=recv,
        device_id=partner_of(way),
        device_id_type=MESH,
    )


class Links:
    def __init__(self, sems):
        self.send, self.recv = sems
        self.used = 0

    def copy(self, source, target, way):
        slot = self.used
        self.used += 1
        return remote(source, target, self.send.at[slot], self.recv.at[slot], way)


def semaphores(*counts):
    return [pltpu.SemaphoreType.DMA((count,)) for count in counts]


def wait_all(arriving, leaving):
    for copy in arriving:
        copy.wait_recv()
    for copy in leaving:
        copy.wait_send()


class Refs:
    def __init__(self, named, layer=None):
        self.named, self.layer = named, layer

    def __getattr__(self, name):
        return self.named[name] if name in self.named else self.named[name + str(self.layer)]

    def of(self, layer):
        return Refs(self.named, layer)


def layered(layer, **values):
    return {name + str(layer): value for name, value in values.items()}


class Pump:
    def __init__(self, schedule, number=None):
        self.schedule, self.number = schedule, number

    def __call__(self, number):
        return Pump(self.schedule, number)

    def __getattr__(self, point):
        def run():
            for move in self.schedule.get(point[0] + str(self.number) + point[1:], ()):
                move.advance()

        return run


def kernel_call(kernel, collective_id, ways, operands, outs, scratch, flops, moves, schedule):
    vmem = pl.BlockSpec(memory_space=pltpu.VMEM)
    hbm = pl.BlockSpec(memory_space=pl.ANY)
    moved_in = [array for move in moves for array in move.operands]
    moved_out = [out for move in moves for out in move.outs]
    every = list(ways)
    for move in moves:
        every += [way for way in move.ways if way not in every]
    scratch_list = []
    for spec in scratch.values():
        scratch_list += spec if isinstance(spec, list) else [spec]

    def body(*refs):
        refs = list(refs)

        def take(count):
            taken, refs[:] = refs[:count], refs[count:]
            return taken

        named = dict(zip(operands, take(len(operands))))
        sources = [take(len(move.operands)) for move in moves]
        named.update(zip(outs, take(len(outs))))
        targets = [take(len(move.outs)) for move in moves]
        for name, spec in scratch.items():
            named[name] = take(len(spec)) if isinstance(spec, list) else take(1)[0]
        for move, source, target in zip(moves, sources, targets, strict=True):
            if move.name:
                source = [named[move.name]]
            move.bind(source, target, take(len(move.scratch)))

        enter(every)
        kernel(Refs(named), Pump(schedule))
        while any(move.at < len(move.steps) for move in moves):
            for move in moves:
                move.advance()

    results = pl.pallas_call(
        body,
        out_shape=[jax.ShapeDtypeStruct(shape, dtype) for shape, dtype, _ in outs.values()]
        + [jax.ShapeDtypeStruct(shape, BF16) for shape in moved_out],
        in_specs=[vmem if inside else hbm for _, inside in operands.values()] + [hbm] * len(moved_in),
        out_specs=[vmem if inside else hbm for _, _, inside in outs.values()] + [hbm] * len(moved_out),
        scratch_shapes=scratch_list + [ref for move in moves for ref in move.scratch],
        compiler_params=pltpu.CompilerParams(
            collective_id=collective_id, has_side_effects=True, vmem_limit_bytes=VMEM_LIMIT
        ),
        cost_estimate=pl.CostEstimate(flops=flops, bytes_accessed=32 << 20, transcendentals=1 << 20),
    )(*[array for array, _ in operands.values()], *moved_in)
    moved = results[len(outs) :]
    for move in moves:
        move.results, moved = moved[: len(move.outs)], moved[len(move.outs) :]
    return Refs(dict(zip(outs, results)))


def row_hops(bits):
    hops, known = [], [0]
    for bit in reversed(range(bits)):
        step = 1 << bit
        hops += [(slot, slot | step, bit) for slot in known]
        known += [slot | step for slot in known]
    return hops


class Move:
    def __init__(self, source, outs, scratch, ways):
        self.name = source if isinstance(source, str) else None
        sources = list(source) if isinstance(source, tuple) else [source]
        self.operands = [] if self.name else sources
        self.outs, self.scratch, self.ways = outs, scratch, ways
        self.steps, self.at = [], 0

    def advance(self):
        if self.at < len(self.steps):
            self.steps[self.at]()
            self.at += 1


class FfnGather(Move):
    def __init__(self, layer, parts, across):
        rows, part = lax.axis_size(ROW), parts[0]
        self.layer = layer
        self.flips, self.across = list(range(rows - 1, 0, -1)), across
        outs = [(rows, *part.shape[1:])] * 2
        ways = [(ROW, flip) for flip in self.flips] + [across]
        super().__init__(tuple(parts), outs, semaphores(rows, rows, rows, rows, 1), ways)

    def bind(self, sources, targets, scratch):
        own, other = targets
        self.blocks = [own, other]
        row_send, row_recv, far_send, far_recv, local_sem = scratch
        row = lax.axis_index(ROW)
        is_own = lax.axis_index(SEC) == self.layer

        class Either:
            def __init__(self, make):
                self.made = [make(part) for part in sources]

            def start(self):
                pl.when(is_own)(self.made[0].start)
                pl.when(jnp.logical_not(is_own))(self.made[1].start)

            def wait(self):
                self.made[0].wait()

            def wait_recv(self):
                self.made[0].wait_recv()

            def wait_send(self):
                self.made[0].wait_send()

        def exchange(flip):
            return Either(
                lambda part: remote(
                    part.at[(row ^ flip) & 1], own.at[row], row_send.at[flip], row_recv.at[flip], (ROW, flip)
                )
            )

        local = Either(lambda part: pltpu.make_async_copy(part.at[row & 1], own.at[row], local_sem.at[0]))
        hops = {flip: exchange(flip) for flip in self.flips}
        far = {
            flip: remote(
                own.at[row ^ flip], other.at[row ^ flip], far_send.at[flip], far_recv.at[flip], self.across
            )
            for flip in self.flips
        }
        far[0] = Either(
            lambda part: remote(part.at[row & 1], other.at[row], far_send.at[0], far_recv.at[0], self.across)
        )

        def start():
            local.start()
            hops[self.flips[0]].start()

        def start_rest():
            for flip in self.flips[1:]:
                hops[flip].start()

        def forward(flip):
            def step():
                if flip:
                    hops[flip].wait_recv()
                far[flip].start()

            return step

        def finish():
            local.wait()
            wait_all(far.values(), [*hops.values(), *far.values()])

        self.steps = [start, start_rest, *[forward(flip) for flip in [0] + self.flips], finish]


class AttnGather(Move):
    def __init__(self, part):
        rows = lax.axis_size(ROW)
        self.bits = rows.bit_length() - 1
        ways = [(ROW, 1 << bit) for bit in range(self.bits)] + [SECTION]
        super().__init__(part, [(2, rows, *part.shape)], semaphores(rows, rows, rows, rows, 1), ways)

    def bind(self, sources, targets, scratch):
        (part,), (blocks,) = sources, targets
        self.blocks = [blocks.at[0], blocks.at[1]]
        row_send, row_recv, side_send, side_recv, local_sem = scratch
        section, row = lax.axis_index(SEC), lax.axis_index(ROW)

        def place(slot):
            return blocks.at[section, row ^ slot]

        def source(slot):
            return place(slot) if slot else part

        local = pltpu.make_async_copy(part, place(0), local_sem.at[0])
        hops = [
            (slot, filled, remote(source(slot), place(slot), row_send.at[filled], row_recv.at[filled], (ROW, 1 << bit)))
            for slot, filled, bit in row_hops(self.bits)
        ]
        sides = [
            remote(source(slot), place(slot), side_send.at[slot], side_recv.at[slot], SECTION)
            for slot in range(1 << self.bits)
        ]
        arrived = {0}

        def arrive(slot):
            if slot not in arrived:
                arrived.add(slot)
                for _, filled, copy in hops:
                    if filled == slot:
                        copy.wait_recv()
                sides[slot].start()

        def start():
            local.start()
            for slot, _, copy in hops:
                if slot == 0:
                    copy.start()
            sides[0].start()

        def forward():
            for slot, _, copy in hops:
                if slot:
                    arrive(slot)
                    copy.start()

        def finish():
            for slot in range(len(sides)):
                arrive(slot)
            local.wait()
            wait_all(sides, [copy for _, _, copy in hops] + sides)

        self.steps = [start, forward, finish]


class ColumnGather(Move):
    def __init__(self, own, shape):
        super().__init__(own, [(4, *shape)], semaphores(8, 8, 1), [COL_LOW, COL_HIGH])

    def bind(self, sources, targets, scratch):
        (own,), (blocks,) = sources, targets
        send, recv, local_sem = scratch
        col = lax.axis_index(COL)
        h = own.shape[0] // 2
        links = Links((send, recv))
        place = blocks.at[col]
        local = pltpu.make_async_copy(own, place, local_sem.at[0])
        first = [links.copy(own, place, COL_LOW), links.copy(own, place, COL_HIGH)]
        top = blocks.at[col ^ COL_LOW[1], pl.ds(0, h)]
        bottom = blocks.at[col ^ COL_HIGH[1], pl.ds(h, h)]
        second = [links.copy(top, top, COL_HIGH), links.copy(bottom, bottom, COL_LOW)]

        def start():
            local.start()
            for copy in first:
                copy.start()

        def forward():
            for arrived, copy in zip(first, second, strict=True):
                arrived.wait_recv()
                copy.start()

        def finish():
            local.wait()
            wait_all(second, first + second)

        self.steps = [start, forward, finish]


class TokenGather(Move):
    def __init__(self, own, shape, a, b, sides):
        self.a, self.b, self.sides = a, b, sides
        ways = [a, b] + ([SECTION] if sides else [])
        super().__init__(own, [(4, 1 + sides, *shape)], semaphores(8, 8, 1), ways)

    def bind(self, sources, targets, scratch):
        (own,), (blocks,) = sources, targets
        send, recv, local_sem = scratch
        local = pltpu.make_async_copy(own, blocks.at[0, 0], local_sem.at[0])
        gather = BlockGather(Links((send, recv)), blocks, self.a, self.b, self.sides, own)

        def start():
            local.start()
            for copy in (gather.a, gather.b, gather.sides[0]):
                copy.start()

        def forward():
            gather.a.wait_recv()
            gather.ab.start()
            gather.sides[1].start()
            gather.b.wait_recv()
            gather.ba.start()
            gather.sides[2].start()

        def last():
            gather.ab.wait_recv()
            gather.ba.wait_recv()
            gather.sides[3].start()

        def finish():
            local.wait()
            wait_all(gather.sides, gather.copies)

        self.steps = [start, forward, last, finish]


class Across(Move):
    def __init__(self, grad, n, way):
        self.n, self.way = n, way
        super().__init__(grad, [(n, grad.shape[1])], semaphores(1, 1), [way])

    def bind(self, sources, targets, scratch):
        (grad,), (arrived,) = sources, targets
        send, recv = scratch
        copy = remote(grad.at[pl.ds(self.n, self.n)], arrived, send.at[0], recv.at[0], self.way)
        self.steps = [copy.start, lambda: wait_all([copy], [copy])]


class Rows(Move):
    def __init__(self, total):
        rows = total.shape[0]
        self.flips = list(range(1, rows))
        ways = [(ROW, flip) for flip in self.flips]
        super().__init__(total, [total.shape], semaphores(rows, rows), ways)

    def bind(self, sources, targets, scratch):
        (total,), (arrived,) = sources, targets
        send, recv = scratch
        copies = row_copies(total, arrived, send, recv, self.flips)

        def start():
            for copy in copies:
                copy.start()

        self.steps = [start, lambda: wait_all(copies, copies)]


def row_copies(total, arrived, send, recv, flips):
    row = lax.axis_index(ROW)
    return [
        remote(total.at[row ^ flip], arrived.at[flip], send.at[flip], recv.at[flip], (ROW, flip))
        for flip in flips
    ]


class GradScatter(Move):
    def __init__(self, grad, n, way):
        rows, width = lax.axis_size(ROW), grad.shape[1]
        self.n, self.way, self.flips = n, way, list(range(1, rows))
        shape = (rows, n, width // rows)
        scratch = [pltpu.VMEM((n, width), BF16), pltpu.VMEM((n, width), BF16), pltpu.VMEM(shape, BF16)]
        scratch += semaphores(1, 1, 1, 1, rows, rows)
        ways = [way] + [(ROW, flip) for flip in self.flips]
        super().__init__(grad, [shape[1:], shape], scratch, ways)

    def bind(self, sources, targets, scratch):
        (grad,), (own, arrived) = sources, targets
        mine, theirs, total, local_sem, own_sem, far_send, far_recv, row_send, row_recv = scratch
        n, row = self.n, lax.axis_index(ROW)
        depth = total.shape[2]
        local = pltpu.make_async_copy(grad.at[pl.ds(0, n)], mine, local_sem.at[0])
        far = remote(grad.at[pl.ds(n, n)], theirs, far_send.at[0], far_recv.at[0], self.way)
        keep = pltpu.make_async_copy(total.at[row], own, own_sem.at[0])
        copies = row_copies(total, arrived, row_send, row_recv, self.flips)

        def start():
            local.start()
            far.start()

        def forward():
            local.wait()
            far.wait_recv()
            for block in range(total.shape[0]):
                at = slice(block * depth, (block + 1) * depth)
                total[block] = (mine[:, at].astype(F32) + theirs[:, at].astype(F32)).astype(BF16)
            for copy in copies + [keep]:
                copy.start()

        def finish():
            keep.wait()
            wait_all(copies, copies + [far])

        self.steps = [start, forward, finish]


class AttnScatter(Move):
    def __init__(self, name, shape):
        rows, width, m = lax.axis_size(ROW), shape[1], shape[0] // 2
        self.bits, self.m = rows.bit_length() - 1, m
        blocks = (rows, m, width // rows)
        scratch = [
            pltpu.VMEM((m, width), BF16),
            pltpu.VMEM(blocks, F32),
            pltpu.VMEM(blocks, BF16),
            pltpu.VMEM(blocks, BF16),
        ]
        scratch += semaphores(1, 1, 1, rows, rows)
        ways = [SECTION] + [(ROW, 1 << bit) for bit in range(self.bits)]
        super().__init__(name, [blocks[1:]], scratch, ways)

    def bind(self, sources, targets, scratch):
        (grad,), (out,) = sources, targets
        theirs, total, going, coming, out_sem, side_send, side_recv, send, recv = scratch
        m, row, section = self.m, lax.axis_index(ROW), lax.axis_index(SEC)
        depth = total.shape[2]
        mine = grad.at[pl.ds(pl.multiple_of(section * m, m), m)]
        side = remote(
            grad.at[pl.ds(pl.multiple_of((1 - section) * m, m), m)],
            theirs,
            side_send.at[0],
            side_recv.at[0],
            SECTION,
        )
        keep = pltpu.make_async_copy(going.at[0], out, out_sem.at[0])
        hops = [
            (slot, filled, remote(going.at[filled], coming.at[filled], send.at[filled], recv.at[filled], (ROW, 1 << bit)))
            for slot, filled, bit in reversed(row_hops(self.bits))
        ]

        def sum_sides():
            side.wait_recv()
            for block in range(total.shape[0]):
                at = slice(block * depth, (block + 1) * depth)
                total[row ^ block] = mine[:, at].astype(F32) + theirs[:, at].astype(F32)
            send_bit(0)

        def send_bit(bit):
            for slot, filled, copy in hops:
                if filled - slot == 1 << bit:
                    going[filled] = total[filled].astype(BF16)
                    copy.start()

        def add_bit(bit):
            for slot, filled, copy in hops:
                if filled - slot == 1 << bit:
                    copy.wait_recv()
                    total[slot] = total[slot] + coming[filled].astype(F32)

        def hop(bit):
            def step():
                add_bit(bit - 1)
                send_bit(bit)

            return step

        def finish():
            add_bit(self.bits - 1)
            going[0] = total[0].astype(BF16)
            keep.start()
            keep.wait()
            wait_all([], [copy for _, _, copy in hops] + [side])

        self.steps = [side.start, sum_sides, *[hop(bit) for bit in range(1, self.bits)], finish]


class NoCopy:
    def start(self):
        pass

    wait_recv = wait_send = start


class BlockGather:
    def __init__(self, links, blocks, a, b, sides=True, own=None, there=False):
        h = blocks.shape[2] // 2
        own = blocks.at[0, 0] if own is None else own
        if there:
            self.a = self.b = self.ab = self.ba = NoCopy()
        else:
            self.a = links.copy(own, blocks.at[1, 0], a)
            self.b = links.copy(own, blocks.at[2, 0], b)
            self.ab = links.copy(blocks.at[1, 0, pl.ds(0, h)], blocks.at[3, 0, pl.ds(0, h)], b)
            self.ba = links.copy(blocks.at[2, 0, pl.ds(h, h)], blocks.at[3, 0, pl.ds(h, h)], a)
        self.sides = [NoCopy()] * 4
        if sides and not there:
            self.sides = [
                links.copy(blocks.at[k, 0] if k else own, blocks.at[k, 1], SECTION) for k in range(4)
            ]
        self.copies = [self.a, self.b, self.ab, self.ba, *self.sides]


class Scatter:
    def __init__(self, links, r, corner_in, edge_in, a, b):
        self.r, self.corner_in, self.edge_in = r, corner_in, edge_in
        self.corner_b = links.copy(r.corner_out.at[0], corner_in.at[0], b)
        self.corner_a = links.copy(r.corner_out.at[1], corner_in.at[1], a)
        self.edge_a = links.copy(r.edge_out.at[0], edge_in.at[0], a)
        self.edge_b = links.copy(r.edge_out.at[1], edge_in.at[1], b)
        self.copies = [self.corner_b, self.corner_a, self.edge_a, self.edge_b]

    def send_corner(self, value):
        corner = self.r.corner_out
        corner[...] = value.astype(BF16).reshape(corner.shape)
        self.corner_b.start()
        self.corner_a.start()

    def send_edge_a(self, value):
        edge, h = self.r.edge_out, value.shape[0] // 2
        self.corner_b.wait_recv()
        edge[0, :h] = (value[:h] + self.corner_in[0].astype(F32)).astype(BF16)
        edge[0, h:] = value[h:].astype(BF16)
        self.edge_a.start()

    def send_edge_b(self, value):
        edge, h = self.r.edge_out, value.shape[0] // 2
        self.corner_a.wait_recv()
        edge[1, :h] = value[:h].astype(BF16)
        edge[1, h:] = (value[h:] + self.corner_in[1].astype(F32)).astype(BF16)
        self.edge_b.start()

    def total(self, value):
        self.edge_a.wait_recv()
        self.edge_b.wait_recv()
        return value + self.edge_in[0].astype(F32) + self.edge_in[1].astype(F32)


def save(started, sems, pairs):
    for source, target in pairs:
        started.append(pltpu.make_async_copy(source, target, sems.at[len(started)]))
        started[-1].start()


class Load:
    def __init__(self, sources, target, stage, sems):
        self.sources, self.target, self.stage, self.copies, self.sems = sources, target, stage, [], sems
        if stage is None:
            for i, source in enumerate(sources):
                blocks, rows, columns = source.shape
                for block in range(blocks):
                    place = target.at[pl.ds(i * rows, rows), pl.ds(block * columns, columns)]
                    self.copies.append(
                        pltpu.make_async_copy(source.at[block], place, sems.at[len(self.copies)])
                    )

    def start(self):
        for copy in self.copies:
            copy.start()
        filled = sum(source.shape[1] for source in self.sources)
        if filled < self.target.shape[0]:
            self.target[filled:] = jnp.zeros((self.target.shape[0] - filled, self.target.shape[1]), BF16)

    def wait(self):
        for copy in self.copies:
            copy.wait()
        if self.stage is not None:
            for i, source in enumerate(self.sources):
                blocks, rows, columns = source.shape
                buffer = self.stage.at[:, pl.ds(0, rows)]
                copy = pltpu.make_async_copy(source, buffer, self.sems.at[0])
                copy.start()
                copy.wait()
                for block in range(blocks):
                    self.target[i * rows : (i + 1) * rows, block * columns : (block + 1) * columns] = (
                        self.stage[block, :rows]
                    )


def stage_of(sizes):
    if sizes.depth % 128 == 0:
        return {}
    return dict(stage=pltpu.VMEM((sizes.rows, max(sizes.unit, sizes.attn // 2), sizes.depth), BF16))


def stage_in(r):
    return r.named.get("stage")


def hidden_tiles(hidden):
    return [(at, min(384, hidden - at)) for at in range(0, hidden, 384)]


def padded(hidden):
    return -(-hidden // 128) * 128


def width_tiles(width):
    return [(at, 512) for at in range(0, width, 512)]


def put_partial(r, k, at, size, value):
    n = value.shape[0] // 2
    r.partial[k, :, pl.ds(at, size)] = value[:n]
    r.side_out[k, :, pl.ds(at, size)] = value[n:].astype(BF16)


def side_copies(links, r):
    return [links.copy(r.side_out.at[k], r.side_in.at[k], SECTION) for k in range(4)]


def with_side(r, k):
    return r.partial[k] + r.side_in[k].astype(F32)


def ffn_forward(r, layer, a, at, weights):
    r = r.of(layer)
    links = Links(r.f_sems)
    blocks, result_ref, second_ref = r.f_blocks, r.result, r.second
    gate_out, up_out, act_out = r.hidden[0], r.hidden[1], r.hidden[2]
    n, width = blocks.shape[2:]
    hidden = r.w_gate.shape[0]
    second = second_ref[...]
    inverse = lax.rsqrt(jnp.mean(second * second, axis=-1, keepdims=True) + EPS)
    blocks[0, 0] = (second * inverse * r.gain_ffn[...]).astype(BF16)
    gather = BlockGather(links, blocks, a, ROW_LOW)
    sides = side_copies(links, r)
    scatter = Scatter(links, r, r.f_corner_in, r.f_edge_in, a, ROW_LOW)
    gather.a.start()
    gather.b.start()
    gather.sides[0].start()
    at(layer).f_sent()
    gather.a.wait_recv()
    gather.ab.start()
    gather.sides[1].start()
    gather.b.wait_recv()
    gather.ba.start()
    gather.sides[2].start()
    gather.ab.wait_recv()
    gather.ba.wait_recv()
    gather.sides[3].start()
    at(layer).f_gathered()
    stage = stage_in(r)
    loads = [
        Load(move.blocks, weight, stage, sems)
        for move, weight, sems in zip(weights, (r.w_gate, r.w_up, r.w_down), r.f_load_sems, strict=True)
    ]
    loads[0].start()
    loads[1].start()
    loads[0].wait()
    loads[1].wait()
    saves = []
    for k in range(4):
        gather.sides[k].wait_recv()
        x = blocks[k].reshape(2 * n, width)
        rows = pl.ds(k * 2 * n, 2 * n)
        for lane, size in hidden_tiles(hidden):
            lanes = pl.ds(lane, size)
            gate = dot(x, r.w_gate[lanes], 1, 1)
            up = dot(x, r.w_up[lanes], 1, 1)
            act = gate / (1.0 + jnp.exp(-gate)) * up
            gate_out[rows, lanes] = gate.astype(BF16)
            up_out[rows, lanes] = up.astype(BF16)
            act_out[rows, lanes] = act.astype(BF16)
        pairs = [(blocks.at[k], r.f_blocks_hbm.at[k])]
        for source, target in ((gate_out, r.gate), (up_out, r.up), (act_out, r.act)):
            pairs.append((source.at[rows], target.at[rows]))
        save(saves, r.f_save_sem, pairs)
        getattr(at(layer), "f_up" + str(k))()
    at(layer).f_up()
    loads[2].start()
    loads[2].wait()

    def down(k):
        act = act_out[pl.ds(k * 2 * n, 2 * n)]
        for lane, size in width_tiles(width):
            put_partial(r, k, lane, size, dot(act, r.w_down[:, pl.ds(lane, size)], 1, 0))
        sides[k].start()

    down(3)
    down(1)
    sides[3].wait_recv()
    scatter.send_corner(with_side(r, 3))
    down(2)
    sides[1].wait_recv()
    scatter.send_edge_a(with_side(r, 1))
    sides[2].wait_recv()
    scatter.send_edge_b(with_side(r, 2))
    down(0)
    at(layer).f_edges()
    sides[0].wait_recv()
    result_ref[...] = second_ref[...] + scatter.total(with_side(r, 0))
    at(layer).f_end()
    wait_all([], [*gather.copies, *sides, *scatter.copies])
    for copy in saves:
        copy.wait()


def ffn_backward_loads(r, layer, gathers):
    r = r.of(layer)
    stage = stage_in(r)
    loads = [
        Load(halves, weight, stage, sems)
        for halves, weight, sems in zip(
            ([r.gate_own, r.gate_other], [r.up_own, r.up_other], [r.down_own, r.down_other]),
            (r.w_gate, r.w_up, r.w_down),
            r.f_load_sems,
            strict=True,
        )
    ]
    for load in loads:
        load.start()
    more = [(r.gate, r.hidden[0]), (r.up, r.hidden[1])]
    if not gathers:
        more.append((r.gathered, r.f_blocks))
    extra = []
    save(extra, r.f_extra_sem, more)
    return loads + extra


def ffn_backward(r, layer, a, at, gathers, loads):
    r = r.of(layer)
    links = Links(r.f_sems)
    blocks, second_ref, grad_ref = r.f_blocks, r.second, r.of(layer + 1).d_entry
    gate_in, up_in = r.hidden
    d_gate_out, d_up_out = r.hidden
    n, width = blocks.shape[2:]
    hidden = r.w_gate.shape[0]
    if gathers:
        blocks[0, 0] = grad_ref[...]
    gather = BlockGather(links, blocks, a, ROW_LOW, there=not gathers)
    sides = side_copies(links, r)
    scatter = Scatter(links, r, r.f_corner_in, r.f_edge_in, a, ROW_LOW)
    saves = []

    def step(k):
        g = blocks[k].reshape(2 * n, width)
        rows = pl.ds(k * 2 * n, 2 * n)
        for lane, size in hidden_tiles(hidden):
            lanes = pl.ds(lane, size)
            d_act = dot(g, r.w_down[lanes], 1, 1)
            gate = gate_in[rows, lanes].astype(F32)
            up = up_in[rows, lanes].astype(F32)
            sigma = 1.0 / (1.0 + jnp.exp(-gate))
            d_gate_out[rows, lanes] = (d_act * up * sigma * (1.0 + gate * (1.0 - sigma))).astype(BF16)
            d_up_out[rows, lanes] = (d_act * gate * sigma).astype(BF16)
        pairs = [(d_gate_out.at[rows], r.d_gate.at[rows]), (d_up_out.at[rows], r.d_up.at[rows])]
        if gathers:
            pairs.append((blocks.at[k], r.f_blocks_hbm.at[k]))
        save(saves, r.f_save_sem, pairs)
        d_gate = d_gate_out[rows]
        d_up = d_up_out[rows]
        for lane, size in width_tiles(width):
            lanes = pl.ds(lane, size)
            value = dot(d_gate, r.w_gate[:, lanes], 1, 0) + dot(d_up, r.w_up[:, lanes], 1, 0)
            put_partial(r, k, lane, size, value)
        sides[k].start()

    gather.a.start()
    gather.b.start()
    gather.sides[0].start()
    at(layer).f_sent()
    for load in loads:
        load.wait()
    gather.sides[0].wait_recv()
    step(0)
    gather.a.wait_recv()
    gather.ab.start()
    gather.sides[1].start()
    gather.b.wait_recv()
    gather.ba.start()
    gather.sides[2].start()
    gather.sides[1].wait_recv()
    step(1)
    gather.ab.wait_recv()
    gather.ba.wait_recv()
    gather.sides[3].start()
    gather.sides[3].wait_recv()
    step(3)
    sides[3].wait_recv()
    scatter.send_corner(with_side(r, 3))
    at(layer).f_corner()
    gather.sides[2].wait_recv()
    step(2)
    sides[1].wait_recv()
    scatter.send_edge_a(with_side(r, 1))
    sides[2].wait_recv()
    scatter.send_edge_b(with_side(r, 2))
    at(layer).f_edges()
    sides[0].wait_recv()
    d_normed = scatter.total(with_side(r, 0))
    second = second_ref[...]
    inverse = lax.rsqrt(jnp.mean(second * second, axis=-1, keepdims=True) + EPS)
    d_second, d_gain = norm_backward(second, inverse, r.gain_ffn[...], d_normed)
    r.d_gain_ffn[...] = d_gain
    r.d_second[...] = grad_ref[...].astype(F32) + d_second
    at(layer).f_end()
    wait_all([], [*gather.copies, *sides, *scatter.copies])
    for copy in saves:
        copy.wait()


def turn(vectors, cosine, sine):
    return vectors * cosine + pltpu.roll(vectors, HEAD // 2, 1) * sine


def seen(r, slot):
    key = r.key[...]
    visible = (key >= r.start[pl.ds(slot, 1)]) & (key <= r.own[...])
    return jnp.where(visible, 0.0, -1e30)


def attention_weights(r):
    weights = r.w_attn
    heads_width = (weights.shape[0] - 2 * HEAD) // 2
    return (
        weights.at[pl.ds(0, heads_width)],
        weights.at[pl.ds(heads_width, heads_width)],
        weights.at[pl.ds(2 * heads_width, 2 * HEAD)],
    )


def column_gather(links, blocks):
    h = blocks.shape[1] // 2
    return (
        links.copy(blocks.at[0], blocks.at[1], COL_LOW),
        links.copy(blocks.at[0], blocks.at[2], COL_HIGH),
        links.copy(blocks.at[1, pl.ds(0, h)], blocks.at[3, pl.ds(0, h)], COL_HIGH),
        links.copy(blocks.at[2, pl.ds(h, h)], blocks.at[3, pl.ds(h, h)], COL_LOW),
    )


def attention_forward(r, layer, at, gather):
    r = r.of(layer)
    links = Links(r.a_sems)
    entry, kv, bias, partial = r.entry, r.kv, r.bias, r.partial
    normed, query, mixed, lse_ref = r.normed, r.query, r.mixed, r.lse
    cos_ref, sin_ref = r.cos, r.sin
    n, width = entry.shape[1:]
    tokens = 2 * n
    rows = kv.shape[1]
    w_query, w_out, w_pair = attention_weights(r)
    heads = w_query.shape[0] // HEAD
    bits = rows.bit_length() - 1
    scale = 1.0 / math.sqrt(HEAD)
    stage = stage_in(r)
    load = Load(gather.blocks, r.w_attn, stage, r.a_load_sem)
    scatter = Scatter(links, r, r.a_corner_in, r.a_edge_in, COL_LOW, COL_HIGH)
    hops = [
        [(slot, filled, links.copy(kv.at[b, slot], kv.at[b, filled], (ROW, 1 << bit)))
         for slot, filled, bit in row_hops(bits)]
        for b in range(2)
    ]
    copies = scatter.copies + [copy for group in hops for _, _, copy in group]

    def normalise(k):
        x = entry[k].astype(F32)
        inverse = lax.rsqrt(jnp.mean(x * x, axis=-1, keepdims=True) + EPS)
        normed[pl.ds(k * n, n)] = (x * inverse * r.gain_attn[...]).astype(BF16)

    def project_pair(b):
        where = pl.ds(b * tokens, tokens)
        pair = dot(normed[where], w_pair[...], 1, 1) + r.b_pair[...]
        kv[b, 0, :, :HEAD] = turn(pair[:, :HEAD], cos_ref[where], sin_ref[where]).astype(BF16)
        kv[b, 0, :, HEAD:] = pair[:, HEAD:].astype(BF16)
        for slot, _, copy in hops[b]:
            if slot == 0:
                copy.start()

    def project_query(b):
        where = pl.ds(b * tokens, tokens)
        projected = dot(normed[where], w_query[...], 1, 1) + r.b_query[...]
        for head in range(heads):
            lanes = slice(head * HEAD, (head + 1) * HEAD)
            query[where, lanes] = turn(projected[:, lanes], cos_ref[where], sin_ref[where]).astype(BF16)

    arrived = [set(), set()]

    def arrive(b, slot):
        for _, filled, copy in hops[b]:
            if filled == slot and slot not in arrived[b]:
                copy.wait_recv()
                arrived[b].add(slot)

    if layer:
        entry[0] = r.result0[...].astype(BF16)
        to_low, to_high, corner_high, corner_low = column_gather(links, entry)
        copies += [to_low, to_high, corner_high, corner_low]
        to_low.start()
        to_high.start()
        at(layer).a_begin()
        load.start()
        normalise(0)
        to_low.wait_recv()
        corner_high.start()
        to_high.wait_recv()
        corner_low.start()
        normalise(1)
        normalise(2)
        load.wait()
        project_pair(0)
        corner_high.wait_recv()
        corner_low.wait_recv()
        normalise(3)
        project_pair(1)
    else:
        at(layer).a_begin()
        for k in range(4):
            normalise(k)
        at(layer).a_normed()
        load.start()
        load.wait()
        project_pair(1)
        project_pair(0)
    at(layer).a_pairs()
    project_query(1)
    project_query(0)
    at(layer).a_queries()
    for b in (1, 0):
        for slot, _, copy in hops[b]:
            if slot:
                arrive(b, slot)
                copy.start()
    at(layer).a_relayed()
    saves = []
    for b in (1, 0):
        for slot in range(1, rows):
            arrive(b, slot)
        save(saves, r.a_save_sem, [(kv.at[b], r.kv_hbm.at[b])])
        keys = kv[b, :, :, :HEAD].reshape(rows * tokens, HEAD)
        values = kv[b, :, :, HEAD:].reshape(rows * tokens, HEAD)
        where = pl.ds(b * tokens, tokens)
        bias[...] = seen(r, b)
        for head in range(heads):
            lanes = slice(head * HEAD, (head + 1) * HEAD)
            scores = dot(keys, query[where, lanes], 1, 1) * scale + bias[...]
            top = jnp.max(scores, axis=0, keepdims=True)
            raised = jnp.exp(scores - top)
            total = jnp.sum(raised, axis=0, keepdims=True)
            lse_ref[b, pl.ds(head, 1)] = top + jnp.log(total)
            probs = (raised * (1.0 / total)).astype(BF16)
            mixed[where, lanes] = dot(probs, values, 0, 0).astype(BF16)
            if b == 0:
                getattr(at(layer), "a_head" + str(head))()
        for k in (2 * b + 1, 2 * b):
            for lane, size in width_tiles(width):
                partial[k, :, pl.ds(lane, size)] = dot(
                    mixed[pl.ds(k * n, n)], w_out[:, pl.ds(lane, size)], 1, 0
                )
        if b == 1:
            scatter.send_corner(partial[3])
            at(layer).a_half()
    scatter.send_edge_b(partial[2])
    scatter.send_edge_a(partial[1])
    if layer:
        save(saves, r.a_save_sem, [(entry.at[0], r.entry_hbm)])
    at(layer).a_edges()
    r.second[...] = entry[0].astype(F32) + scatter.total(partial[0])
    at(layer).a_end()
    wait_all([], copies)
    for copy in saves:
        copy.wait()


def attention_backward(r, layer, at):
    r = r.of(layer)
    links = Links(r.a_sems)
    blocks, kv, bias, partial = r.a_blocks, r.kv, r.bias, r.partial
    d_mixed, d_kv, d_kv_out, d_kv_in = r.d_mixed, r.d_kv, r.d_kv_out, r.d_kv_in
    query, d_query, d_pair = r.query, r.d_query, r.d_pair
    share_out, share_in = r.share_out, r.share_in
    cos_ref, sin_ref = r.cos, r.sin
    n, width = blocks.shape[1:]
    tokens = 2 * n
    rows = kv.shape[1]
    w_query, w_out, w_pair = attention_weights(r)
    heads_width = w_query.shape[0]
    heads = heads_width // HEAD
    bits = rows.bit_length() - 1
    scale = 1.0 / math.sqrt(HEAD)
    stage = stage_in(r)
    load = Load([r.attn_blocks.at[0], r.attn_blocks.at[1]], r.w_attn, stage, r.a_load_sem)
    load.start()
    blocks[0] = r.d_second[...].astype(BF16)
    to_low, to_high, corner_high, corner_low = column_gather(links, blocks)
    hops = [
        [(slot, filled, links.copy(d_kv_out.at[b, filled], d_kv_in.at[b, filled], (ROW, 1 << bit)))
         for slot, filled, bit in reversed(row_hops(bits))]
        for b in range(2)
    ]
    share = [links.copy(share_out.at[b], share_in.at[b], COL_LOW) for b in range(2)]
    scatter = Scatter(links, r, r.a_corner_in, r.a_edge_in, COL_LOW, COL_HIGH)

    def unmix(k):
        d_mixed[pl.ds(k * n, n)] = dot(blocks[k], w_out[...], 1, 1).astype(BF16)

    def attend(b):
        keys = kv[b, :, :, :HEAD].reshape(rows * tokens, HEAD)
        values = kv[b, :, :, HEAD:].reshape(rows * tokens, HEAD)
        where = pl.ds(b * tokens, tokens)
        bias[...] = seen(r, b)
        for head in range(heads):
            lanes = slice(head * HEAD, (head + 1) * HEAD)
            q = query[where, lanes]
            d_o = d_mixed[where, lanes]
            scores = dot(keys, q, 1, 1) * scale + bias[...]
            probs = jnp.exp(scores - r.lse[b, pl.ds(head, 1)])
            d_probs = dot(values, d_o, 1, 1)
            delta = jnp.sum(d_probs * probs, axis=0, keepdims=True)
            d_scores = (probs * (d_probs - delta)).astype(BF16)
            d_keys = (dot(d_scores, q, 1, 0) * scale).reshape(rows, tokens, HEAD)
            d_values = dot(probs.astype(BF16), d_o, 1, 0).reshape(rows, tokens, HEAD)
            if head:
                d_keys = d_keys + d_kv[b, :, :, :HEAD]
                d_values = d_values + d_kv[b, :, :, HEAD:]
            d_kv[b, :, :, :HEAD] = d_keys
            d_kv[b, :, :, HEAD:] = d_values
            turned = dot(d_scores, keys, 0, 0) * scale
            d_query[where, lanes] = turn(turned, cos_ref[where], -sin_ref[where]).astype(BF16)

    def send_bit(b, step):
        for slot, filled, copy in hops[b]:
            if filled - slot == step:
                d_kv_out[b, filled] = d_kv[b, filled].astype(BF16)
                copy.start()

    def add_bit(b, step):
        for slot, filled, copy in hops[b]:
            if filled - slot == step:
                copy.wait_recv()
                d_kv[b, slot] = d_kv[b, slot] + d_kv_in[b, filled].astype(F32)

    def share_pair(b):
        share_out[b] = d_kv[b, 0, n:].astype(BF16)
        share[b].start()

    def finish_pair(b):
        share[b].wait_recv()
        total = d_kv[b, 0, :n] + share_in[b].astype(F32)
        where = pl.ds(b * tokens, n)
        rows_of = pl.ds(b * n, n)
        d_pair[rows_of, :HEAD] = turn(total[:, :HEAD], cos_ref[where], -sin_ref[where]).astype(BF16)
        d_pair[rows_of, HEAD:] = total[:, HEAD:].astype(BF16)

    def unproject(k):
        for lane, size in width_tiles(width):
            lanes = pl.ds(lane, size)
            value = dot(d_query[pl.ds(k * n, n)], w_query[:, lanes], 1, 0)
            if k % 2 == 0:
                value = value + dot(d_pair[pl.ds(k // 2 * n, n)], w_pair[:, lanes], 1, 0)
            partial[k, :, lanes] = value

    to_low.start()
    to_high.start()
    at(layer).a_sent()
    load.wait()
    unmix(0)
    to_low.wait_recv()
    corner_high.start()
    to_high.wait_recv()
    corner_low.start()
    at(layer).a_relayed()
    unmix(1)
    unmix(2)
    corner_high.wait_recv()
    corner_low.wait_recv()
    unmix(3)
    attend(1)
    send_bit(1, 1)
    unproject(3)
    scatter.send_corner(partial[3])
    attend(0)
    send_bit(0, 1)
    for bit in range(1, bits):
        for b in (1, 0):
            add_bit(b, 1 << (bit - 1))
            send_bit(b, 1 << bit)
    at(layer).a_hops()
    unproject(1)
    scatter.send_edge_a(partial[1])
    for b in (1, 0):
        add_bit(b, 1 << (bits - 1))
        share_pair(b)
    finish_pair(1)
    unproject(2)
    scatter.send_edge_b(partial[2])
    at(layer).a_edges()
    finish_pair(0)
    unproject(0)
    r.d_bias_query[...] = jnp.sum(d_query[...].astype(F32), axis=0, keepdims=True)
    r.d_bias_pair[...] = jnp.sum(d_pair[...].astype(F32), axis=0, keepdims=True)
    a_grad, normed = r.a_grad, r.normed
    turned_query, turned_mixed, turned_pair = d_query[...].T, r.mixed[...].T, d_pair[...].T
    for lane, size in width_tiles(width):
        lanes = pl.ds(lane, size)
        a_grad[:heads_width, lanes] = dot(turned_query, normed[:, lanes], 1, 0).astype(BF16)
        a_grad[heads_width : 2 * heads_width, lanes] = dot(
            turned_mixed, blocks[:, :, lanes].reshape(4 * n, size), 1, 0
        ).astype(BF16)
        normed_own = jnp.concatenate([normed[:n, lanes], normed[tokens : tokens + n, lanes]])
        a_grad[2 * heads_width :, lanes] = dot(turned_pair, normed_own, 1, 0).astype(BF16)
    at(layer).a_grads()
    d_normed = scatter.total(partial[0])
    stream = r.entry[...].astype(F32)
    inverse = lax.rsqrt(jnp.mean(stream * stream, axis=-1, keepdims=True) + EPS)
    d_first, d_gain = norm_backward(stream, inverse, r.gain_attn[...], d_normed)
    r.d_gain_attn[...] = d_gain
    r.d_entry[...] = (r.d_second[...] + d_first).astype(BF16)
    at(layer).a_end()
    copies = [to_low, to_high, corner_high, corner_low, *share, *scatter.copies]
    wait_all([], copies + [copy for group in hops for _, _, copy in group])


def sum_vectors(r, at, links):
    vector = r.vector
    vector[...] = jnp.zeros_like(vector)
    col = lax.axis_index(COL)
    lanes = r.d_gain_ffn0.shape[1] // HEAD
    heads = r.d_bias_query0.shape[1] // HEAD
    each = vector.shape[0] // 2
    for layer in range(2):
        of = r.of(layer)
        for gain, first in ((of.d_gain_attn, 0), (of.d_gain_ffn, lanes)):
            for i in range(lanes):
                vector[pl.ds(layer * each + first + i, 1)] = gain[:, i * HEAD : (i + 1) * HEAD]
        for i in range(heads):
            place = layer * each + 2 * lanes + col * heads + i
            vector[pl.ds(place, 1)] = of.d_bias_query[:, i * HEAD : (i + 1) * HEAD]
        for i in range(2):
            place = layer * each + 3 * lanes + i * KV + (col >> 1)
            vector[pl.ds(place, 1)] = of.d_bias_pair[:, i * HEAD : (i + 1) * HEAD]
    ways = [SECTION, COL_LOW, COL_HIGH] + [(ROW, 1 << bit) for bit in range(row_bits())]
    copies = []
    for i, way in enumerate(ways):
        r.vector_out[i] = vector[...]
        copies.append(links.copy(r.vector_out.at[i], r.vector_in.at[i], way))
        copies[-1].start()
        at(i).s_step()
        copies[-1].wait_recv()
        vector[...] = vector[...] + r.vector_in[i]
    r.sums[...] = vector[...]
    wait_all([], copies)


class Sizes:
    def __init__(self, n, width, rows, hidden, attn, depth):
        self.n, self.width, self.rows, self.depth = n, width, rows, depth
        self.unit, self.hidden, self.attn = hidden // 2, padded(hidden), attn
        self.heads_width = (attn - 2 * HEAD) // 2
        self.heads = self.heads_width // HEAD


def common_scratch(sizes):
    n, width = sizes.n, sizes.width
    return dict(
        partial=pltpu.VMEM((4, n, width), F32),
        corner_out=pltpu.VMEM((2, n // 2, width), BF16),
        edge_out=pltpu.VMEM((2, n, width), BF16),
        **stage_of(sizes),
    )


def ffn_scratch(sizes, count, saves):
    n, width, hidden = sizes.n, sizes.width, sizes.hidden
    each = 2 * sizes.rows
    return dict(
        w_gate=pltpu.VMEM((hidden, width), BF16),
        w_up=pltpu.VMEM((hidden, width), BF16),
        w_down=pltpu.VMEM((hidden, width), BF16),
        hidden=[pltpu.VMEM((8 * n, hidden), BF16) for _ in range(count)],
        side_out=pltpu.VMEM((4, n, width), BF16),
        f_load_sems=semaphores(each, each, each),
        f_extra_sem=pltpu.SemaphoreType.DMA((3,)),
        f_save_sem=pltpu.SemaphoreType.DMA((4 * saves,)),
    )


def ffn_buffers(sizes, layer):
    n, width = sizes.n, sizes.width
    return layered(
        layer,
        f_blocks=pltpu.VMEM((4, 2, n, width), BF16),
        side_in=pltpu.VMEM((4, n, width), BF16),
        f_corner_in=pltpu.VMEM((2, n // 2, width), BF16),
        f_edge_in=pltpu.VMEM((2, n, width), BF16),
        f_sems=semaphores(16, 16),
    )


def attention_scratch(sizes):
    tokens = 2 * sizes.n
    return dict(
        w_attn=pltpu.VMEM((sizes.attn, sizes.width), BF16),
        bias=pltpu.VMEM((sizes.rows * tokens, tokens), F32),
        a_load_sem=pltpu.SemaphoreType.DMA((2 * sizes.rows,)),
        a_save_sem=pltpu.SemaphoreType.DMA((3,)),
    )


def attention_buffers(sizes, layer, backward):
    n, width, rows = sizes.n, sizes.width, sizes.rows
    pairs = (2, rows, 2 * n, 2 * HEAD)
    count = 10 + 2 * (rows - 1)
    buffers = dict(
        a_corner_in=pltpu.VMEM((2, n // 2, width), BF16),
        a_edge_in=pltpu.VMEM((2, n, width), BF16),
        a_sems=semaphores(count, count),
    )
    if backward:
        buffers.update(a_blocks=pltpu.VMEM((4, n, width), BF16))
        buffers.update(d_kv_in=pltpu.VMEM(pairs, BF16))
        buffers.update(share_in=pltpu.VMEM((2, n, 2 * HEAD), BF16))
    else:
        buffers.update(kv=pltpu.VMEM(pairs, BF16))
    return layered(layer, **buffers)


def attention_back_scratch(sizes):
    n, rows = sizes.n, sizes.rows
    pairs = (2, rows, 2 * n, 2 * HEAD)
    return dict(
        **attention_scratch(sizes),
        d_mixed=pltpu.VMEM((4 * n, sizes.heads_width), BF16),
        d_kv=pltpu.VMEM(pairs, F32),
        d_kv_out=pltpu.VMEM(pairs, BF16),
        share_out=pltpu.VMEM((2, n, 2 * HEAD), BF16),
        d_query=pltpu.VMEM((4 * n, sizes.heads_width), BF16),
        d_pair=pltpu.VMEM((2 * n, 2 * HEAD), BF16),
        a_grad=pltpu.VMEM((sizes.attn, sizes.width), BF16),
    )


def small_outs(sizes, layer):
    return layered(
        layer,
        d_gain_attn=((1, sizes.width), F32, True),
        d_bias_query=((1, sizes.heads_width), F32, True),
        d_bias_pair=((1, 2 * HEAD), F32, True),
    )


def exchange_halves(parts, section):
    return pick(parts, section), swap(pick(parts, 1 - section), *SECTION)


def of_layer(layer, parts, section, token):
    own, other = parts
    return jnp.where(section + token == layer, own, other)


def to_owner(first, second, section):
    keep = jnp.where(section == 0, first, second)
    away = jnp.where(section == 0, second, first)
    other = swap(away, *SECTION)
    return jnp.where(section == 0, keep, other), jnp.where(section == 0, other, keep)


def local(
    tokens,
    cotangent,
    lengths,
    norm_attn,
    w_query,
    b_query,
    w_keyval,
    b_keyval,
    w_out,
    norm_ffn,
    w_gate,
    w_up,
    w_down,
):
    section = lax.axis_index(SEC)
    row = lax.axis_index(ROW)
    col = lax.axis_index(COL)
    rows = lax.axis_size(ROW)
    cols = lax.axis_size(COL)
    low, high = bit_of(col, 0), bit_of(col, 1)
    place = (section, row, low, high)
    row_count = tokens.shape[1]
    width = tokens.shape[2]
    half = row_count // 2
    depth = w_query.shape[1]
    heads_width = w_query.shape[2]

    def blocks_of(array):
        return jnp.concatenate(
            [
                lax.dynamic_slice(
                    array, (2 * section + (high ^ j), (low ^ k) * half, 0), (1, half, width)
                )
                for j in range(2)
                for k in range(2)
            ]
        )

    small = jnp.concatenate([norm_attn[0], norm_ffn[0], b_keyval[0], b_query[0]])
    small = (small, swap(small, *SECTION))
    small = [of_layer(layer, small, section, 0).astype(F32) for layer in range(2)]

    pair_cols = w_keyval[0].reshape(-1, 2, KV, HEAD)
    mine = pick(pair_cols, high, 2).reshape(-1, 2 * HEAD)
    away = pick(pair_cols, 1 - high, 2).reshape(-1, 2 * HEAD)
    pair_rows = ordered(mine[None, None], swap(away, *COL_HIGH)[None, None], high, 0)
    pair_rows = ordered(pair_rows, swap(pair_rows, *COL_LOW), low, 1)
    pair_rows = pair_rows.reshape(depth, 2 * HEAD)
    attn_own = jnp.concatenate([w_query[0].T, w_out[0], pair_rows.T])
    attn_halves = exchange_halves(attn_own.reshape(2, -1, depth), section)

    def ffn_parts(shard):
        hidden = shard.shape[0]
        parts = shard.reshape(2, 2, hidden // 4, shard.shape[1]).transpose(1, 0, 2, 3)
        return exchange_halves(parts, section)

    parts = [ffn_parts(shard) for shard in (w_gate[0].T, w_up[0].T, w_down[0])]
    ways = [(COL_LOW, COL_HIGH), (COL_HIGH, COL_LOW)]

    hidden = w_gate.shape[2] // 2

    tables = layout(lengths, place, row_count)
    sizes = Sizes(half, width, rows, hidden, 2 * attn_halves[0].shape[0], depth)
    entry = blocks_of(tokens)

    ffn_ways = [way for way, _ in ways]
    across = [way for _, way in ways]
    cosine, sine, start, own_index, key_index = tables
    shared = dict(
        cos=(cosine, True),
        sin=(sine, True),
        start=(start, True),
        own=(own_index, True),
        key=(key_index, True),
    )
    gains_attn, gains_ffn, vectors = [], [], []
    for layer in range(2):
        bias_pair = small[layer][2 * width : 2 * width + 2 * KV * HEAD].reshape(2, KV, HEAD)
        gains_attn.append(layered(layer, gain_attn=(small[layer][None, :width], True)))
        gains_ffn.append(layered(layer, gain_ffn=(small[layer][None, width : 2 * width], True)))
        vectors.append(
            layered(
                layer,
                b_query=(small[layer][None, 2 * width + 2 * KV * HEAD :], True),
                b_pair=(pick(bias_pair, high, 1).reshape(1, -1), True),
            )
        )
    chip_ways = [COL_LOW, COL_HIGH, SECTION] + [(ROW, 1 << bit) for bit in range(row_bits())]

    attn_moves = [AttnGather(of_layer(layer, attn_halves, section, 0)) for layer in range(2)]
    ffn_moves = [
        [FfnGather(layer, parts[kind], across[layer]) for kind in range(3)]
        for layer in range(2)
    ]
    grad_own = lax.dynamic_slice(
        cotangent, (2 * section + high, low * half, 0), (1, half, width)
    )[0]
    grad_move = TokenGather(grad_own, grad_own.shape, ffn_ways[1], ROW_LOW, True)
    (attn_a, attn_b), ((gate_a, up_a, down_a), (gate_b, up_b, down_b)) = attn_moves, ffn_moves
    some, rest = rows // 2, rows - rows // 2
    schedule = dict(
        a0_begin=[attn_a],
        a0_normed=[attn_a, gate_a, gate_a, attn_a],
        a0_queries=[gate_a] * rows,
        a0_relayed=[up_a, up_a, down_a, down_a],
        a0_head0=[up_a] * some,
        a0_head1=[up_a] * rest,
        f0_sent=[down_a] * some + [attn_b],
        f0_gathered=[gate_a] + [down_a] * rest + [up_a],
        f0_up=[down_a, attn_b],
        f0_edges=[gate_b, gate_b],
        f0_end=[attn_b],
        a1_queries=[gate_b] * rows,
        a1_relayed=[up_b, up_b, down_b, down_b],
        a1_head0=[up_b] * some,
        a1_head1=[up_b] * rest,
        f1_sent=[down_b] * some,
        f1_gathered=[gate_b] + [down_b] * rest + [up_b, grad_move],
        f1_up=[down_b, grad_move],
        f1_edges=[grad_move],
    )

    def forward_kernel(r, at):
        for layer in range(2):
            attention_forward(r, layer, at, attn_moves[layer])
            ffn_forward(r, layer, ffn_ways[layer], at, ffn_moves[layer])

    tokens_here = 4 * half
    outs = dict(entry_hbm1=((half, width), BF16, False), result1=((half, width), F32, True))
    buffers = dict(
        entry1=pltpu.VMEM((4, half, width), BF16), result0=pltpu.VMEM((half, width), F32)
    )
    units = ((8 * half, sizes.hidden), BF16, False)
    for layer in range(2):
        outs.update(
            layered(
                layer,
                second=((half, width), F32, True),
                normed=((tokens_here, width), BF16, True),
                query=((tokens_here, heads_width), BF16, True),
                mixed=((tokens_here, heads_width), BF16, True),
                lse=((2, sizes.heads, 2 * half), F32, True),
                kv_hbm=((2, rows, 2 * half, 2 * HEAD), BF16, False),
                f_blocks_hbm=((4, 2, half, width), BF16, False),
                gate=units,
                up=units,
                act=units,
            )
        )
        buffers.update(ffn_buffers(sizes, layer))
        buffers.update(attention_buffers(sizes, layer, False))
    done = kernel_call(
        forward_kernel,
        0,
        chip_ways,
        dict(
            entry0=(entry, True),
            **shared,
            **gains_attn[0],
            **gains_attn[1],
            **gains_ffn[0],
            **gains_ffn[1],
            **vectors[0],
            **vectors[1],
        ),
        outs,
        {**common_scratch(sizes), **ffn_scratch(sizes, 3, 4), **attention_scratch(sizes), **buffers},
        1 << 34,
        [*attn_moves, *ffn_moves[0], *ffn_moves[1], grad_move],
        schedule,
    )
    (grad_all,) = grad_move.results
    last_result = done.result1.astype(BF16)

    def grad_of(left, right):
        return dot(left, right.reshape(-1, width), 0, 0).astype(BF16)

    unit = sizes.unit

    def blocked(grad, arrived):
        total = (grad[:unit].astype(F32) + arrived.astype(F32)).astype(BF16)
        return jnp.stack([total[:, i * depth : (i + 1) * depth] for i in range(rows)])

    def ffn_back_operands(layer):
        of = done.of(layer)
        (gate, gate_far), (up, up_far), (down, down_far) = (move.results for move in ffn_moves[layer])
        return {
            **gains_ffn[layer],
            **layered(
                layer,
                second=(of.second, True),
                gate=(of.gate, False),
                up=(of.up, False),
                gate_own=(gate, False),
                gate_other=(gate_far, False),
                up_own=(up, False),
                up_other=(up_far, False),
                down_own=(down, False),
                down_other=(down_far, False),
            ),
        }

    def ffn_back_outs(layer):
        return layered(
            layer,
            d_second=((half, width), F32, True),
            d_gain_ffn=((1, width), F32, True),
            d_gate=units,
            d_up=units,
        )

    def attention_back_operands(layer, own):
        of = done.of(layer)
        return {
            **gains_attn[layer],
            **shared,
            **layered(
                layer,
                entry=(own, True),
                attn_blocks=(attn_moves[layer].results[0], False),
                kv=(of.kv_hbm, True),
                normed=(of.normed, True),
                query=(of.query, True),
                mixed=(of.mixed, True),
                lse=(of.lse, True),
            ),
        }

    down_grad = grad_of(done.act1, grad_all)
    down_move = Across(down_grad, unit, across[1])
    back = kernel_call(
        lambda r, at: ffn_backward(r, 1, ffn_ways[1], at, False, ffn_backward_loads(r, 1, False)),
        1,
        [ffn_ways[1], ROW_LOW, SECTION],
        dict(d_entry2=(grad_own, True), gathered1=(grad_all, False), **ffn_back_operands(1)),
        ffn_back_outs(1),
        {**common_scratch(sizes), **ffn_scratch(sizes, 2, 2), **ffn_buffers(sizes, 1)},
        1 << 33,
        [down_move],
        dict(f1_sent=[down_move]),
    )
    gate_grad = grad_of(back.d_gate1, done.f_blocks_hbm1)
    up_grad = grad_of(back.d_up1, done.f_blocks_hbm1)
    down_one = blocked(down_grad, down_move.results[0])

    down_rows = Rows(down_one)
    gate_move = GradScatter(gate_grad, unit, across[1])
    up_move = Across(up_grad, unit, across[1])
    last_move = ColumnGather(last_result, last_result.shape)
    entry_move = ColumnGather("d_entry1", (half, width))
    attn_move_one = AttnScatter("a_grad", (sizes.attn, width))

    def middle_kernel(r, at):
        loads = ffn_backward_loads(r, 0, True)
        attention_backward(r, 1, at)
        ffn_backward(r, 0, ffn_ways[0], at, True, loads)

    middle = kernel_call(
        middle_kernel,
        2,
        chip_ways,
        dict(
            d_second1=(back.d_second1, True),
            **attention_back_operands(1, done.entry_hbm1),
            **ffn_back_operands(0),
        ),
        dict(
            d_entry1=((half, width), BF16, True),
            f_blocks_hbm0=((4, 2, half, width), BF16, False),
            **small_outs(sizes, 1),
            **ffn_back_outs(0),
        ),
        {
            **common_scratch(sizes),
            **attention_back_scratch(sizes),
            **attention_buffers(sizes, 1, True),
            **ffn_scratch(sizes, 2, 3),
            **ffn_buffers(sizes, 0),
        },
        1 << 33,
        [down_rows, gate_move, up_move, last_move, entry_move, attn_move_one],
        dict(
            a1_relayed=[down_rows, gate_move],
            a1_grads=[attn_move_one],
            f0_edges=[gate_move, up_move, attn_move_one, last_move, entry_move],
        ),
    )
    up_one = blocked(up_grad, up_move.results[0])
    zero_grads = [
        grad_of(done.act0, middle.f_blocks_hbm0),
        grad_of(middle.d_gate0, done.f_blocks_hbm0),
        grad_of(middle.d_up0, done.f_blocks_hbm0),
    ]

    up_rows = Rows(up_one)
    zero_moves = [GradScatter(grad, unit, across[0]) for grad in zero_grads]
    attn_move_zero = AttnScatter("a_grad", (sizes.attn, width))
    first_move = ColumnGather("d_entry0", (half, width))
    result_move = ColumnGather(done.entry_hbm1, (half, width))
    sum_rows = 2 * (3 * width // HEAD + 2 * KV)
    sum_ways = 3 + row_bits()

    def last_kernel(r, at):
        attention_backward(r, 0, at)
        sum_vectors(r, at, Links(r.sum_sems))

    down_zero, gate_zero, up_zero = zero_moves
    final = kernel_call(
        last_kernel,
        3,
        chip_ways,
        dict(
            d_second0=(middle.d_second0, True),
            d_gain_ffn0=(middle.d_gain_ffn0, True),
            d_gain_ffn1=(back.d_gain_ffn1, True),
            **attention_back_operands(0, entry[0]),
            **{name: (middle.named[name], True) for name in small_outs(sizes, 1)},
        ),
        dict(d_entry0=((half, width), BF16, True), sums=((sum_rows, HEAD), F32, True)),
        {
            **common_scratch(sizes),
            **attention_back_scratch(sizes),
            **attention_buffers(sizes, 0, True),
            **{name: pltpu.VMEM(shape, F32) for name, (shape, _, _) in small_outs(sizes, 0).items()},
            **dict(
                vector=pltpu.VMEM((sum_rows, HEAD), F32),
                vector_out=pltpu.VMEM((sum_ways, sum_rows, HEAD), F32),
                vector_in=pltpu.VMEM((sum_ways, sum_rows, HEAD), F32),
                sum_sems=semaphores(sum_ways, sum_ways),
            ),
        },
        1 << 32,
        [up_rows, *zero_moves, attn_move_zero, first_move, result_move],
        dict(
            a0_relayed=[down_zero, up_rows],
            a0_hops=[result_move],
            a0_edges=[down_zero, gate_zero, up_zero],
            a0_grads=[attn_move_zero, result_move],
            a0_end=[attn_move_zero, gate_zero, first_move],
            s0_step=[attn_move_zero, up_zero],
            s2_step=[first_move],
            s3_step=[attn_move_zero],
        ),
    )

    def by_row_bit(own, arrived):
        near, far = own.astype(F32), 0.0
        for flip in range(1, rows):
            if flip & 1:
                far = far + arrived[flip].astype(F32)
            else:
                near = near + arrived[flip].astype(F32)
        return ordered(near.astype(BF16)[None], far.astype(BF16)[None], row & 1, 0)

    ffn_grads = [
        [by_row_bit(*move.results) for move in (gate_zero, up_zero, down_zero)],
        [
            by_row_bit(*gate_move.results),
            by_row_bit(pick(up_one, row), up_rows.results[0]),
            by_row_bit(pick(down_one, row), down_rows.results[0]),
        ],
    ]
    sums = final.sums.reshape(2, -1)
    sums = jnp.where(section == 0, sums[0], sums[1])
    grad_norm_attn = sums[:width]
    grad_norm_ffn = sums[width : 2 * width]
    spread = sums[2 * width : 2 * width + cols * heads_width].reshape(cols, -1)
    grad_b_query = pick(spread, col)
    grad_b_keyval = sums[2 * width + cols * heads_width :]
    (first_result,), (last_blocks,) = result_move.results, last_move.results
    (grad_one_blocks,), (grad_zero_blocks,) = entry_move.results, first_move.results
    (attn_one_half,), (attn_zero_half,) = attn_move_one.results, attn_move_zero.results

    def assemble(first, second):
        shape = (2, row_count, width)
        zeroth, later = to_owner(first.reshape(shape), second.reshape(shape), section)
        return jnp.concatenate([zeroth, later])[None]

    outputs = assemble(first_result, last_blocks)
    grads_in = assemble(grad_zero_blocks, grad_one_blocks)

    def ffn_grad(kind):
        zeroth, later = to_owner(ffn_grads[0][kind], ffn_grads[1][kind], section)
        whole = jnp.stack([zeroth, later], axis=1)
        return whole.reshape(-1, whole.shape[-1])

    grad_gate = ffn_grad(0).T.astype(F32)
    grad_up = ffn_grad(1).T.astype(F32)
    grad_down = ffn_grad(2).astype(F32)

    total = jnp.concatenate(to_owner(attn_zero_half, attn_one_half, section)).astype(F32)
    grad_query = total[:heads_width].T
    grad_out = total[heads_width : 2 * heads_width]
    pair = total[2 * heads_width :].T.reshape(2, 2, depth // 4, 2 * HEAD)
    pair = pick(pair, low, 1) + swap(pick(pair, 1 - low, 1).astype(BF16), *COL_LOW).astype(F32)
    pair = pair.astype(BF16)
    pair = ordered(
        pick(pair, high)[:, None], swap(pick(pair, 1 - high), *COL_HIGH)[:, None], high, 1
    )
    grad_keyval = (
        pair.reshape(-1, 2, 2, HEAD).transpose(0, 2, 1, 3).reshape(-1, 2 * KV * HEAD).astype(F32)
    )

    return (
        outputs,
        grads_in,
        grad_norm_attn[None],
        grad_query[None],
        grad_b_query[None],
        grad_keyval[None],
        grad_b_keyval[None],
        grad_out[None],
        grad_norm_ffn[None],
        grad_gate[None],
        grad_up[None],
        grad_down[None],
    )


def solution(mesh):
    in_specs = (
        P(None, ROW, None),
        P(None, ROW, None),
        P(),
        P(SEC, None),
        P(SEC, ROW, COL),
        P(SEC, COL),
        P(SEC, (ROW, COL), None),
        P(SEC, None),
        P(SEC, COL, ROW),
        P(SEC, None),
        P(SEC, ROW, COL),
        P(SEC, ROW, COL),
        P(SEC, COL, ROW),
    )
    out_specs = (
        P(SEC, None, ROW, None),
        P(SEC, None, ROW, None),
        P(SEC, None),
        P(SEC, ROW, COL),
        P(SEC, COL),
        P(SEC, (ROW, COL), None),
        P(SEC, None),
        P(SEC, COL, ROW),
        P(SEC, None),
        P(SEC, ROW, COL),
        P(SEC, ROW, COL),
        P(SEC, COL, ROW),
    )
    return jax.shard_map(local, mesh=mesh, in_specs=in_specs, out_specs=out_specs, check_vma=False)
```
